128 devices in a mesh: ctx: 4 (over y_lo, core), fsdp: 32 (over y_hi, x, z).
Axes of the slice: x: 4, y: 4 (y_hi: 2, y_lo: 2; y = y_hi * 2 + y_lo), z: 4, core: 2. Of those that a mesh axis runs over, the one named last changes fastest.
Arguments:
- tokens: bfloat16 [32, 512, 1024], P('fsdp', 'ctx'), may hold values from -6 to 6
- cotangent: bfloat16 [32, 512, 2048], P('fsdp', 'ctx'), may hold values from -6 to 6
- w_xz: bfloat16 [1024, 4096], P('fsdp'), may hold values from -0.1875 to 0.1875
- w_bcdt: bfloat16 [1024, 288], P('fsdp'), may hold values from -0.1875 to 0.1875
- rate: float32 [32], replicated, may hold values from 0.0001953125 to 1
- dt_bias: float32 [32], replicated, may hold values from -3 to 0.5
- skip: float32 [32], replicated, may hold values from 0.5 to 1.5
- gain: float32 [2048], replicated, may hold values from 0.5 to 1.5
Outputs:
- layer_out: bfloat16 [32, 512, 2048], P('fsdp', 'ctx')
- grad_input: bfloat16 [32, 512, 1024], P('fsdp', 'ctx')
- grad_xz: float32 [1024, 4096], P(('ctx', 'fsdp'))
- grad_bcdt: float32 [1024, 288], P(('ctx', 'fsdp'))
The draws below stay inside these ranges and needn't reach their ends.
All inputs are finite; a program needn't handle non-finite values.
Results may differ from the reference program's by a relative error of at most 0.005.
Values may be sent and summed in bfloat16 or wider, within the bound.
No kernel may reach another device: no remote copies, remote signals or barrier semaphores. Data moves between devices by JAX's collectives and lax.ppermute only.
A program may use at most 128 MiB of HBM per device.

```python
import math
import jax
import jax.numpy as jnp
from jax import lax

D = 1024
H = 32
N = 128
DI = 2048
TOKENS = 512
SEQS = 32


def with_spikes(array, own_key, source, target, shards_of, factor):
    owner, partner = [(jnp.arange(array.shape[position]) // (array.shape[position] // shards_of)).reshape([-1 if axis == position else 1 for axis in range(array.ndim)]) for position in (source, target)]
    chosen = jax.random.permutation(own_key, shards_of)[partner]
    strong = (owner == chosen) | (owner == (partner + shards_of // 2) % shards_of)
    return jnp.where(strong, factor * array, array)


def steps_of(own_key, shape, cuts, least, high):
    def one(axis_at, shards_of):
        heights = jax.random.uniform(jax.random.fold_in(jax.random.fold_in(own_key, 6), axis_at), (shards_of,), jnp.float32, least / len(cuts), high / len(cuts))
        return jnp.repeat(jnp.exp(heights), shape[axis_at] // shards_of).reshape((-1,) + (1,) * (len(shape) - axis_at - 1))

    factor_of = one(*cuts[0])
    for cut in cuts[1:]:
        factor_of = factor_of * one(*cut)
    return factor_of


def bell_draw(stream_key, shape, scale, limit, cuts=(), held_as=jnp.bfloat16):
    drawn = jax.random.normal(stream_key, shape, jnp.float32) * scale
    if len(cuts) > 0:
        drawn = steps_of(stream_key, shape, cuts, -0.22, 0.18) * drawn
    return jnp.clip(drawn, min=-limit, max=limit).astype(held_as)


def heavy_noise(own_key, extent, spread, bound, cuts, heavy, kind=jnp.bfloat16):
    result = spread * jax.random.normal(own_key, extent, jnp.float32)
    if cuts:
        result = result * steps_of(own_key, extent, cuts, -0.22, 0.18)
    return jnp.clip(with_spikes(result, jax.random.fold_in(own_key, 3), *heavy), -bound, bound).astype(kind)


def setup_inputs(seed: int = 0) -> dict:
    key_of = jax.random.split(jax.random.key(seed), 9)
    tokens = heavy_noise(key_of[0], (SEQS, TOKENS, D), 1.0, 6.0, ((0, 32), (1, 4)), (0, 2, 32, 2.75))
    cotangent = bell_draw(key_of[1], (SEQS, TOKENS, DI), 1.0, 6.0, ((0, 32), (1, 4)))
    w_xz = bell_draw(key_of[2], (D, 2 * DI), D ** -0.5, 0.1875, ((0, 32),))
    w_bcdt = bell_draw(key_of[3], (D, 2 * N + H), D ** -0.5, 0.1875, ((0, 32),))
    rate = jnp.clip(jnp.exp(jax.random.uniform(key_of[4], (H,), jnp.float32, math.log(0.0001953125), math.log(1.0))), 0.0001953125, 1.0)
    dt_bias = jnp.clip(jax.random.uniform(key_of[5], (H,), jnp.float32, -3.0, 0.5), -3.0, 0.5)
    skip = jnp.clip(jax.random.uniform(key_of[6], (H,), jnp.float32, 0.5, 1.5), 0.5, 1.5)
    gain = jnp.clip(1.0 + 0.1 * jax.random.normal(key_of[7], (DI,), jnp.float32), 0.5, 1.5)
    return dict(tokens=tokens, cotangent=cotangent, w_xz=w_xz, w_bcdt=w_bcdt, rate=rate, dt_bias=dt_bias, skip=skip, gain=gain)


highest = lax.Precision.HIGHEST
norm_eps = 1e-05

def split_proj(xz, bcdt, dt_bias, rate):
    inner = xz.shape[1] // 2
    heads = dt_bias.shape[0]
    states = (bcdt.shape[1] - heads) // 2
    values = jax.nn.silu(xz[:, :inner])
    gate_in = xz[:, inner:]
    b_in = bcdt[:, :states]
    c_out = bcdt[:, states:2 * states]
    step_size = jax.nn.softplus(bcdt[:, 2 * states:] + dt_bias)
    log_decay = -step_size * rate
    return (values, gate_in, b_in, c_out, step_size, log_decay)

def ssd_blocks(values, b_in, c_out, step_size, log_decay, start):
    length = values.shape[0]
    heads, width, states = start.shape
    block = math.gcd(length, 128)
    count = length // block
    vals_b = values.reshape(count, block, heads, width)
    b_blocks = b_in.reshape(count, block, states)
    c_blocks = c_out.reshape(count, block, states)
    step_b = step_size.reshape(count, block, heads)
    log_b = log_decay.reshape(count, block, heads)
    causal = jnp.arange(block)[:, None] >= jnp.arange(block)[None, :]

    def one_block(state, pieces):
        vals, b_part, c_part, steps, logs = pieces
        cumul = jnp.cumsum(logs, axis=0)
        scores = jnp.dot(c_part, b_part.T, precision=highest)
        gaps = jnp.where(causal[:, :, None], cumul[:, None, :] - cumul[None, :, :], -1e+30)
        weights = scores[:, :, None] * jnp.exp(gaps) * steps[None, :, :]
        inner = jnp.einsum('tsh,shp->thp', weights, vals, precision=highest)
        carried = jnp.exp(cumul)[:, :, None] * jnp.einsum('tn,hpn->thp', c_part, state, precision=highest)
        tail = jnp.exp(cumul[-1][None, :] - cumul) * steps
        update = jnp.einsum('sh,shp,sn->hpn', tail, vals, b_part, precision=highest)
        new_state = jnp.exp(cumul[-1])[:, None, None] * state + update
        return (new_state, (inner + carried).reshape(block, heads * width))
    final, outs = lax.scan(one_block, start, (vals_b, b_blocks, c_blocks, step_b, log_b))
    return (outs.reshape(length, heads * width), final)

def gated_norm(ssd, gate_in, gain):
    mixed = ssd * jax.nn.silu(gate_in)
    scale = lax.rsqrt(lax.optimization_barrier(jnp.mean(mixed * mixed, axis=-1, keepdims=True)) + norm_eps)
    return mixed * scale * gain

def core(xz, bcdt, dt_bias, rate, skip, gain):
    values, gate_in, b_in, c_out, step_size, log_decay = split_proj(xz, bcdt, dt_bias, rate)
    heads = rate.shape[0]
    width = values.shape[1] // heads
    start = jnp.zeros((heads, width, b_in.shape[1]), jnp.float32)
    ssd, final = ssd_blocks(values, b_in, c_out, step_size, log_decay, start)
    ssd = ssd + values * jnp.repeat(skip, width)
    return gated_norm(ssd, gate_in, gain)

def reference(tokens, cotangent, w_xz, w_bcdt, rate, dt_bias, skip, gain):
    seqs, length, model = tokens.shape
    flat = tokens.reshape(seqs * length, model)
    xz = jnp.dot(flat, w_xz, preferred_element_type=jnp.float32).reshape(seqs, length, -1)
    bcdt = jnp.dot(flat, w_bcdt, preferred_element_type=jnp.float32).reshape(seqs, length, -1)

    def one_sequence(triple):
        xz_one, bcdt_one, cot_one = triple
        normed, pull = jax.vjp(lambda first, second: core(first, second, dt_bias, rate, skip, gain), xz_one, bcdt_one)
        d_first, d_second = pull(cot_one.astype(jnp.float32))
        return (normed.astype(jnp.bfloat16), d_first.astype(jnp.bfloat16), d_second.astype(jnp.bfloat16))
    layer_out, d_xz, d_bcdt = lax.map(one_sequence, (xz, bcdt, cotangent))
    d_xz = d_xz.reshape(seqs * length, -1)
    d_bcdt = d_bcdt.reshape(seqs * length, -1)
    grad_input = (jnp.dot(d_xz, w_xz.T, preferred_element_type=jnp.float32) + jnp.dot(d_bcdt, w_bcdt.T, preferred_element_type=jnp.float32)).astype(jnp.bfloat16)
    grad_xz = jnp.dot(flat.T, d_xz, preferred_element_type=jnp.float32)
    grad_bcdt = jnp.dot(flat.T, d_bcdt, preferred_element_type=jnp.float32)
    return (layer_out, grad_input.reshape(seqs, length, model), grad_xz, grad_bcdt)
```

```python
import jax
import jax.numpy as jnp
from jax import lax
from jax.experimental import pallas as pl
from jax.experimental.pallas import tpu as pltpu
from jax.sharding import Mesh, PartitionSpec as P

f32 = jnp.float32
bf16 = jnp.bfloat16
norm_eps = 1e-05
lanes = 128
NN = (((1,), (0,)), ((), ()))
NT = (((1,), (1,)), ((), ()))
TN = (((0,), (0,)), ((), ()))

whole = ("yl", "core", "yh", "x", "z")
rows_axes = ("yh", "x", "z")
group_axes = ("yl", "core", "yh")
vmem = 56 * 2**20


def dot1(a, b, dims):
    return lax.dot_general(a.astype(bf16), b.astype(bf16), dims, preferred_element_type=f32)


def halves(a):
    high = a.astype(bf16)
    return (high, (a - high.astype(f32)).astype(bf16))


def dot3(a, b, dims):
    a_high, a_low = a if isinstance(a, tuple) else halves(a)
    b_high, b_low = b if isinstance(b, tuple) else halves(b)
    dot = lambda left, right: lax.dot_general(left, right, dims, preferred_element_type=f32)
    return dot(a_high, b_high) + (dot(a_high, b_low) + dot(a_low, b_high))


def thirds(a):
    high = a.astype(bf16)
    rest = a - high.astype(f32)
    mid = rest.astype(bf16)
    return (high, mid, (rest - mid.astype(f32)).astype(bf16))


def dot_exact(a, ones, dims):
    high, mid, low = thirds(a)
    dot = lambda left: lax.dot_general(left, ones, dims, preferred_element_type=f32)
    return dot(high) + (dot(mid) + dot(low))


def iota(shape, axis):
    return lax.broadcasted_iota(jnp.int32, shape, axis)


def head_expander(inner, width):
    shape = (lanes, inner)
    start = iota(shape, 0) * width
    col = iota(shape, 1)
    return ((col >= start) & (col < start + width)).astype(f32).astype(bf16)


def lower_ones(block):
    shape = (block, block)
    return (iota(shape, 0) >= iota(shape, 1)).astype(f32).astype(bf16)


def cumulated(steps, rate, lower):
    log_decay = -steps * rate
    high, mid, low = thirds(log_decay)
    dot = lambda right: lax.dot_general(lower, right, NN, preferred_element_type=f32)
    return dot(high) + (dot(mid) + dot(low))


def softplus(a):
    return jnp.maximum(a, 0.0) + jnp.log1p(jnp.exp(-jnp.abs(a)))


def pair_halves(a, block, width):
    left = iota(a.shape, 1) < width
    zero = jnp.zeros_like(a)
    return jnp.concatenate([jnp.where(left, a, zero), jnp.where(left, zero, a)], axis=0)


def forward_kernel(tok, weights, par, cot, xv_o, g_o, bc_o, y_o, st_o, stat_o, state, *, seqs, block, width, inner):
    heads = inner // width
    step = pl.program_id(0)

    @pl.when(step == 0)
    def _():
        state[...] = jnp.zeros_like(state)

    rows = seqs * block
    proj = lax.dot_general(tok[0].reshape(rows, -1), weights[...], NN, preferred_element_type=f32)
    expander = head_expander(inner, width)
    lower = lower_ones(block)
    causal = iota((block, block), 0) >= iota((block, block), 1)
    skip, gain = par[0:1, :], par[1:2, :]
    bias, rate = par[2:3, :lanes], par[3:4, :lanes]
    for s in range(seqs):
        part = proj[s * block : (s + 1) * block]
        xv, gate = part[:, :inner], part[:, inner : 2 * inner]
        b_in, c_out = part[:, 2 * inner : 2 * inner + lanes], part[:, 2 * inner + lanes : 2 * inner + 2 * lanes]
        raw = part[:, 2 * inner + 2 * lanes :] + bias
        xv_o[0, s] = xv
        g_o[0, s] = gate
        bc_o[0, s] = jnp.concatenate([b_in, c_out, raw], axis=1)
        values = xv * jax.nn.sigmoid(xv)
        steps = softplus(raw)
        cumul = cumulated(steps, rate, lower)
        cumul_t = cumul.T
        wide = dot_exact(jnp.concatenate([steps, cumul], axis=0), expander, NN)
        step_wide, cumul_wide = wide[:block], wide[block:]
        last_wide = cumul_wide[block - 1 : block]
        scaled = values * step_wide
        b_two, c_two = halves(b_in), halves(c_out)
        scores = dot3(c_two, b_two, NT)
        old = state[s]
        st_o[0, s] = old
        carried = jnp.exp(cumul_wide) * dot3(c_two, old, NN)
        inners = []
        for pair in range(heads // 2):
            both = []
            for h in (2 * pair, 2 * pair + 1):
                gap = jnp.where(causal, cumul[:, h : h + 1] - cumul_t[h : h + 1, :], -1e30)
                both.append((scores * jnp.exp(gap)).astype(bf16))
            cols = scaled[:, 2 * pair * width : (2 * pair + 2) * width]
            inners.append(
                lax.dot_general(
                    jnp.concatenate(both, axis=1),
                    pair_halves(cols, block, width).astype(bf16),
                    NN,
                    preferred_element_type=f32,
                )
            )
        y = carried + jnp.concatenate(inners, axis=1)
        y_o[0, s] = y
        state[s] = jnp.exp(last_wide) * old + dot3(b_two, scaled * jnp.exp(last_wide - cumul_wide), TN)
        mixed = (y + skip * values) * (gate * jax.nn.sigmoid(gate))
        weighted = cot[0, s].astype(f32) * gain * mixed
        both = jnp.concatenate([mixed * mixed, weighted], axis=1)
        row, col = iota((8, 2 * inner), 0), iota((8, 2 * inner), 1)
        chooser = ((row < 2) & ((col >= inner) == (row == 1))).astype(f32).astype(bf16)
        high, mid, low = thirds(both)
        dot = lambda right: lax.dot_general(chooser, right, NT, preferred_element_type=f32)
        stat_o[0, :, s * block : (s + 1) * block] = dot(high) + (dot(mid) + dot(low))


def backward_kernel(
    xv_i, g_i, bc_i, y_i, st_i, cot, stat, par, out_o, d_o, grad_state, next_state, *, seqs, block, width, inner, total
):
    heads = inner // width
    step = pl.program_id(0)

    @pl.when(step == 0)
    def _():
        grad_state[...] = jnp.zeros_like(grad_state)
        next_state[...] = jnp.zeros_like(next_state)

    expander = head_expander(inner, width)
    lower = lower_ones(block)
    later = iota((block, block), 1) >= iota((block, block), 0)
    upper = (iota((block, block), 1) >= iota((block, block), 0)).astype(f32).astype(bf16)
    skip, gain = par[0:1, :], par[1:2, :]
    bias_rate = par[3:4, :lanes]
    sums = stat[0]
    scale_row = lax.rsqrt(sums[0:1] * (1.0 / total) + norm_eps)
    pull_row = scale_row * scale_row * scale_row * sums[1:2] * (1.0 / total)
    packed = jnp.concatenate([scale_row, pull_row, jnp.zeros((6, scale_row.shape[1]), f32)], axis=0)
    row, col = iota((8, 2 * inner), 0), iota((8, 2 * inner), 1)
    chooser = ((row < 2) & ((col >= inner) == (row == 1))).astype(f32).astype(bf16)
    spread = dot_exact(packed, chooser, TN)
    for s in range(seqs):
        span = slice(s * block, (s + 1) * block)
        scale, pull = spread[span, :inner], spread[span, inner:]
        xv, gate, y = xv_i[0, s], g_i[0, s], y_i[0, s]
        b_in, c_out = bc_i[0, s, :, :lanes], bc_i[0, s, :, lanes : 2 * lanes]
        raw = bc_i[0, s, :, 2 * lanes :]
        sig = jax.nn.sigmoid(xv)
        values = xv * sig
        gate_sig = jax.nn.sigmoid(gate)
        gate_silu = gate * gate_sig
        full = y + skip * values
        mixed = full * gate_silu
        out_o[0, s] = (mixed * scale * gain).astype(bf16)
        d_mixed = cot[0, s].astype(f32) * gain * scale - mixed * pull
        d_y = d_mixed * gate_silu
        d_gate = d_mixed * full * (gate_sig * (1.0 + gate * (1.0 - gate_sig)))

        steps = softplus(raw)
        cumul = cumulated(steps, bias_rate, lower)
        cumul_t = cumul.T
        wide = dot_exact(jnp.concatenate([steps, cumul], axis=0), expander, NN)
        step_wide, cumul_wide = wide[:block], wide[block:]
        last_wide = cumul_wide[block - 1 : block]
        tail = jnp.exp(last_wide - cumul_wide)
        scaled = values * step_wide
        b_two, c_two = halves(b_in), halves(c_out)
        scores_t = dot3(b_two, c_two, NT)
        old = st_i[0, s]
        grad = grad_state[s]
        grad_two = halves(grad)
        back = tail * dot3(b_two, grad_two, NN)
        inners = []
        d_scores_t = jnp.zeros((block, block), f32)
        for pair in range(heads // 2):
            cols = slice(2 * pair * width, (2 * pair + 2) * width)
            dy_pair = d_y[:, cols].astype(bf16)
            products = lax.dot_general(
                pair_halves(scaled[:, cols], block, width).astype(bf16), dy_pair, NT, preferred_element_type=f32
            )
            both = []
            for k in range(2):
                h = 2 * pair + k
                gap = jnp.where(later, cumul_t[h : h + 1, :] - cumul[:, h : h + 1], -1e30)
                decay = jnp.exp(gap)
                both.append((scores_t * decay).astype(bf16))
                d_scores_t += products[k * block : (k + 1) * block] * decay
            inners.append(
                lax.dot_general(
                    jnp.concatenate(both, axis=1),
                    pair_halves(d_y[:, cols], block, width).astype(bf16),
                    NN,
                    preferred_element_type=f32,
                )
            )
        back = back + jnp.concatenate(inners, axis=1)
        lifted = halves(d_y * jnp.exp(cumul_wide))
        ds_two = halves(d_scores_t)
        d_c = dot3(ds_two, b_two, TN) + dot3(lifted, old, NT)
        d_b = dot3(ds_two, c_two, NN) + dot3(scaled * tail, grad_two, NT)
        through = jnp.sum(next_state[s] * grad, axis=0, keepdims=True)
        grad_state[s] = jnp.exp(last_wide) * grad + dot3(c_two, lifted, TN)
        next_state[s] = old
        last_row = iota((block, inner), 0) == block - 1
        reduced = dot_exact(
            jnp.concatenate([values * back, d_y * y + jnp.where(last_row, through, 0.0)], axis=0), expander, NT
        )
        d_steps = reduced[:block]
        d_cumul = reduced[block:] - steps * d_steps
        high, mid, low = thirds(d_cumul)
        dot = lambda right: lax.dot_general(upper, right, NN, preferred_element_type=f32)
        d_log = dot(high) + (dot(mid) + dot(low))
        d_raw = (d_steps - d_log * bias_rate) * jax.nn.sigmoid(raw)
        d_values = back * step_wide + skip * d_y
        d_xv = d_values * (sig * (1.0 + xv * (1.0 - sig)))
        d_o[0, s] = jnp.concatenate([d_xv, d_gate, d_b, d_c, d_raw], axis=1).astype(bf16)


def chunk_spec(shape, count=None):
    blank = (0,) * (len(shape) - 1)
    if count is None:
        return pl.BlockSpec((1,) + shape[1:], lambda i: (i,) + blank)
    return pl.BlockSpec((1,) + shape[1:], lambda i: (count - 1 - i,) + blank)


def fixed_spec(shape):
    return pl.BlockSpec(shape, lambda i: (0,) * len(shape))


def forward_call(tok, weights, par, cot, width):
    chunks, seqs, block, model = tok.shape
    inner = cot.shape[3]
    shapes = [
        (chunks, seqs, block, inner),
        (chunks, seqs, block, inner),
        (chunks, seqs, block, 3 * lanes),
        (chunks, seqs, block, inner),
        (chunks, seqs, lanes, inner),
        (chunks, 8, seqs * block),
    ]

    def kernel(*refs):
        forward_kernel(*refs, seqs=seqs, block=block, width=width, inner=inner)

    return pl.pallas_call(
        kernel,
        grid=(chunks,),
        in_specs=[chunk_spec(tok.shape), fixed_spec(weights.shape), fixed_spec(par.shape), chunk_spec(cot.shape)],
        out_specs=[chunk_spec(s) for s in shapes],
        out_shape=[jax.ShapeDtypeStruct(s, f32) for s in shapes],
        scratch_shapes=[pltpu.VMEM((seqs, lanes, inner), f32)],
        compiler_params=pltpu.CompilerParams(vmem_limit_bytes=vmem),
        name="forward_scan",
    )(tok, weights, par, cot)


def backward_call(xv, gate, bc, y, states, cot, stats, par, width, total):
    chunks, seqs, block, inner = xv.shape
    ins = (xv, gate, bc, y, states, cot, stats)
    out_shapes = [(chunks, seqs, block, inner), (chunks, seqs, block, 2 * inner + 3 * lanes)]

    def kernel(*refs):
        backward_kernel(*refs, seqs=seqs, block=block, width=width, inner=inner, total=total)

    return pl.pallas_call(
        kernel,
        grid=(chunks,),
        in_specs=[chunk_spec(a.shape, chunks) for a in ins] + [fixed_spec(par.shape)],
        out_specs=[chunk_spec(s, chunks) for s in out_shapes],
        out_shape=[jax.ShapeDtypeStruct(s, bf16) for s in out_shapes],
        scratch_shapes=[pltpu.VMEM((seqs, lanes, inner), f32), pltpu.VMEM((seqs, lanes, inner), f32)],
        compiler_params=pltpu.CompilerParams(vmem_limit_bytes=vmem),
        name="backward_scan",
    )(*ins, par)


def body(tokens, cotangent, w_xz, w_bcdt, rate, dt_bias, skip, gain):
    group = lax.axis_size(group_axes)
    devices = lax.axis_size(whole)
    mine = lax.axis_index(group_axes)
    chunks = lax.axis_size("yl") * lax.axis_size("core")
    seqs = group // chunks
    owners = lax.axis_size(rows_axes)
    block, model = tokens.shape[1:]
    total = cotangent.shape[2]
    inner = total // group
    heads = rate.shape[0] // group
    width = inner // heads
    states = (w_bcdt.shape[1] - rate.shape[0]) // 2

    def picked(target):
        w_dt = lax.dynamic_slice_in_dim(w_bcdt[:, 2 * states :], target * heads, heads, 1)
        return jnp.concatenate(
            [
                lax.dynamic_slice_in_dim(w_xz, target * inner, inner, 1),
                lax.dynamic_slice_in_dim(w_xz, total + target * inner, inner, 1),
                w_bcdt[:, : 2 * states],
                jnp.pad(w_dt, ((0, 0), (0, lanes - heads))),
            ],
            axis=1,
        )

    w_picked = jnp.stack([picked(lax.axis_index(("yl", "core")) * seqs + k) for k in range(seqs)])
    copies = jnp.broadcast_to(w_picked[:, None], (seqs, owners // seqs) + w_picked.shape[1:])
    copies = copies.reshape((owners,) + w_picked.shape[1:])
    weights = lax.all_to_all(copies, rows_axes, 0, 0, tiled=True).reshape(model, -1)

    tok = lax.all_gather(tokens[0], group_axes, axis=0).reshape(chunks, seqs, block, model)
    cot = lax.all_to_all(
        cotangent[0].reshape(block, group, inner).transpose(1, 0, 2), group_axes, 0, 0, tiled=True
    ).reshape(chunks, seqs, block, inner)

    own = lambda a: lax.dynamic_slice_in_dim(a, mine * heads, heads, 0)
    padded = lambda a: jnp.pad(own(a), (0, inner - heads))
    par = jnp.stack(
        [jnp.repeat(own(skip), width), lax.dynamic_slice_in_dim(gain, mine * inner, inner, 0)]
        + [padded(dt_bias), padded(rate)]
        + [jnp.zeros((inner,), f32)] * 4
    )
    xv, gate, bc, y, chunk_states, stats = forward_call(tok, weights, par, cot, width)
    stats = lax.all_gather(stats[:, :2], group_axes, axis=0).sum(axis=0)
    stats = jnp.pad(stats, ((0, 0), (0, 6), (0, 0)))
    out, d_all = backward_call(xv, gate, bc, y, chunk_states, cot, stats, par, width, float(total))

    flat_d = d_all.reshape(group * block, -1)
    term = lax.dot_general(tok.reshape(group * block, model), flat_d, TN, preferred_element_type=f32).astype(bf16)
    shares = lax.all_to_all(term.reshape(devices, model // devices, -1), whole, 0, 0, tiled=True)
    partial_input = lax.dot_general(flat_d, weights, NT, preferred_element_type=f32).astype(bf16)
    pieces = lax.all_to_all(partial_input.reshape(group, block, model), group_axes, 0, 0, tiled=True)
    grad_input = pieces.astype(f32).sum(axis=0).astype(bf16)[None]
    layer_out = lax.all_to_all(out.reshape(group, block, inner), group_axes, 0, 0, tiled=True)
    layer_out = layer_out.transpose(1, 0, 2).reshape(1, block, total)

    summed = shares.reshape(group, devices // group, model // devices, -1).astype(f32).sum(axis=1)
    spread = lambda a: a.transpose(1, 0, 2).reshape(model // devices, -1)
    grad_xz = jnp.concatenate([spread(summed[..., :inner]), spread(summed[..., inner : 2 * inner])], axis=1)
    grad_bcdt = jnp.concatenate(
        [
            summed[..., 2 * inner : 2 * inner + 2 * states].sum(axis=0),
            spread(summed[..., 2 * inner + 2 * states : 2 * inner + 2 * states + heads]),
        ],
        axis=1,
    )
    return (layer_out, grad_input, grad_xz, grad_bcdt)


def solution(mesh):
    split = Mesh(mesh.devices.reshape(2, 2, 2, 4, 4), whole)
    ctx, fsdp = ("yl", "core"), rows_axes
    placed = (P(fsdp, ctx, None), P(fsdp, ctx, None), P(fsdp, None), P(fsdp, None), P(), P(), P(), P())
    return jax.shard_map(
        body,
        mesh=split,
        in_specs=placed,
        out_specs=(P(fsdp, ctx, None), P(fsdp, ctx, None), P(ctx + fsdp, None), P(ctx + fsdp, None)),
        check_vma=False,
    )
```

```python
import jax
import jax.numpy as jnp
from jax import lax
from jax.experimental import pallas as pl
from jax.experimental.pallas import tpu as pltpu
from jax.sharding import Mesh, PartitionSpec as P

f32 = jnp.float32
bf16 = jnp.bfloat16
norm_eps = 1e-05
lanes = 128
NN = (((1,), (0,)), ((), ()))
NT = (((1,), (1,)), ((), ()))
TN = (((0,), (0,)), ((), ()))

whole = ("yl", "core", "yh", "x", "z")
rows_axes = ("yh", "x", "z")
group_axes = ("yl", "core", "yh")
vmem = 56 * 2**20


def dot1(a, b, dims):
    return lax.dot_general(a.astype(bf16), b.astype(bf16), dims, preferred_element_type=f32)


def halves(a):
    high = a.astype(bf16)
    return (high, (a - high.astype(f32)).astype(bf16))


def dot3(a, b, dims):
    a_high, a_low = a if isinstance(a, tuple) else halves(a)
    b_high, b_low = b if isinstance(b, tuple) else halves(b)
    dot = lambda left, right: lax.dot_general(left, right, dims, preferred_element_type=f32)
    return dot(a_high, b_high) + (dot(a_high, b_low) + dot(a_low, b_high))


def thirds(a):
    high = a.astype(bf16)
    rest = a - high.astype(f32)
    mid = rest.astype(bf16)
    return (high, mid, (rest - mid.astype(f32)).astype(bf16))


def dot_exact(a, ones, dims):
    high, mid, low = thirds(a)
    dot = lambda left: lax.dot_general(left, ones, dims, preferred_element_type=f32)
    return dot(high) + (dot(mid) + dot(low))


def iota(shape, axis):
    return lax.broadcasted_iota(jnp.int32, shape, axis)


def head_expander(inner, width):
    shape = (lanes, inner)
    start = iota(shape, 0) * width
    col = iota(shape, 1)
    return ((col >= start) & (col < start + width)).astype(f32).astype(bf16)


def lower_ones(block):
    shape = (block, block)
    return (iota(shape, 0) >= iota(shape, 1)).astype(f32).astype(bf16)


def cumulated(steps, rate, lower):
    log_decay = -steps * rate
    high, mid, low = thirds(log_decay)
    dot = lambda right: lax.dot_general(lower, right, NN, preferred_element_type=f32)
    return dot(high) + (dot(mid) + dot(low))


def softplus(a):
    return jnp.maximum(a, 0.0) + jnp.log1p(jnp.exp(-jnp.abs(a)))


def pair_halves(a, block, width):
    left = iota(a.shape, 1) < width
    zero = jnp.zeros_like(a)
    return jnp.concatenate([jnp.where(left, a, zero), jnp.where(left, zero, a)], axis=0)


def forward_kernel(tok, weights, par, cot, xv_o, g_o, bc_o, y_o, st_o, stat_o, state, *, seqs, block, width, inner):
    heads = inner // width
    step = pl.program_id(0)

    @pl.when(step == 0)
    def _():
        state[...] = jnp.zeros_like(state)

    rows = seqs * block
    proj = lax.dot_general(tok[0].reshape(rows, -1), weights[...], NN, preferred_element_type=f32)
    expander = head_expander(inner, width)
    lower = lower_ones(block)
    causal = iota((block, block), 0) >= iota((block, block), 1)
    skip, gain = par[0:1, :], par[1:2, :]
    bias, rate = par[2:3, :lanes], par[3:4, :lanes]
    for s in range(seqs):
        part = proj[s * block : (s + 1) * block]
        xv, gate = part[:, :inner], part[:, inner : 2 * inner]
        b_in, c_out = part[:, 2 * inner : 2 * inner + lanes], part[:, 2 * inner + lanes : 2 * inner + 2 * lanes]
        raw = part[:, 2 * inner + 2 * lanes :] + bias
        xv_o[0, s] = xv
        g_o[0, s] = gate
        bc_o[0, s] = jnp.concatenate([b_in, c_out, raw], axis=1)
        values = xv * jax.nn.sigmoid(xv)
        steps = softplus(raw)
        cumul = cumulated(steps, rate, lower)
        cumul_t = cumul.T
        wide = dot_exact(jnp.concatenate([steps, cumul], axis=0), expander, NN)
        step_wide, cumul_wide = wide[:block], wide[block:]
        last_wide = cumul_wide[block - 1 : block]
        scaled = values * step_wide
        b_two, c_two = halves(b_in), halves(c_out)
        scores = dot3(c_two, b_two, NT)
        old = state[s]
        st_o[0, s] = old
        carried = jnp.exp(cumul_wide) * dot3(c_two, old, NN)
        inners = []
        for pair in range(heads // 2):
            both = []
            for h in (2 * pair, 2 * pair + 1):
                gap = jnp.where(causal, cumul[:, h : h + 1] - cumul_t[h : h + 1, :], -1e30)
                both.append((scores * jnp.exp(gap)).astype(bf16))
            cols = scaled[:, 2 * pair * width : (2 * pair + 2) * width]
            inners.append(
                lax.dot_general(
                    jnp.concatenate(both, axis=1),
                    pair_halves(cols, block, width).astype(bf16),
                    NN,
                    preferred_element_type=f32,
                )
            )
        y = carried + jnp.concatenate(inners, axis=1)
        y_o[0, s] = y
        state[s] = jnp.exp(last_wide) * old + dot3(b_two, scaled * jnp.exp(last_wide - cumul_wide), TN)
        mixed = (y + skip * values) * (gate * jax.nn.sigmoid(gate))
        weighted = cot[0, s].astype(f32) * gain * mixed
        both = jnp.concatenate([mixed * mixed, weighted], axis=1)
        row, col = iota((8, 2 * inner), 0), iota((8, 2 * inner), 1)
        chooser = ((row < 2) & ((col >= inner) == (row == 1))).astype(f32).astype(bf16)
        high, mid, low = thirds(both)
        dot = lambda right: lax.dot_general(chooser, right, NT, preferred_element_type=f32)
        stat_o[0, :, s * block : (s + 1) * block] = dot(high) + (dot(mid) + dot(low))


def backward_kernel(
    xv_i, g_i, bc_i, y_i, st_i, cot, stat_0, stat_1, stat_2, stat_3, par, tok, weights,
    out_o, near_o, far_o, term_o, grad_state, next_state, d_all, *, seqs, block, width, inner, total, chunks
):
    heads = inner // width
    step = pl.program_id(0)
    chunk = chunks - 1 - step
    rows = seqs * block

    @pl.when(step == 0)
    def _():
        grad_state[...] = jnp.zeros_like(grad_state)
        next_state[...] = jnp.zeros_like(next_state)

    expander = head_expander(inner, width)
    lower = lower_ones(block)
    later = iota((block, block), 1) >= iota((block, block), 0)
    upper = (iota((block, block), 1) >= iota((block, block), 0)).astype(f32).astype(bf16)
    skip, gain = par[0:1, :], par[1:2, :]
    bias_rate = par[3:4, :lanes]
    sums = (stat_0[0] + stat_1[0]) + (stat_2[0] + stat_3[0])
    scale_row = lax.rsqrt(sums[0:1] * (1.0 / total) + norm_eps)
    pull_row = scale_row * scale_row * scale_row * sums[1:2] * (1.0 / total)
    packed = jnp.concatenate([scale_row, pull_row, jnp.zeros((6, scale_row.shape[1]), f32)], axis=0)
    row, col = iota((8, 2 * inner), 0), iota((8, 2 * inner), 1)
    chooser = ((row < 2) & ((col >= inner) == (row == 1))).astype(f32).astype(bf16)
    spread = dot_exact(packed, chooser, TN)
    for s in range(seqs):
        span = slice(s * block, (s + 1) * block)
        scale, pull = spread[span, :inner], spread[span, inner:]
        xv, gate, y = xv_i[0, s], g_i[0, s], y_i[0, s]
        b_in, c_out = bc_i[0, s, :, :lanes], bc_i[0, s, :, lanes : 2 * lanes]
        raw = bc_i[0, s, :, 2 * lanes :]
        sig = jax.nn.sigmoid(xv)
        values = xv * sig
        gate_sig = jax.nn.sigmoid(gate)
        gate_silu = gate * gate_sig
        full = y + skip * values
        mixed = full * gate_silu
        out_o[0, s] = (mixed * scale * gain).astype(bf16)
        d_mixed = cot[0, s].astype(f32) * gain * scale - mixed * pull
        d_y = d_mixed * gate_silu
        d_gate = d_mixed * full * (gate_sig * (1.0 + gate * (1.0 - gate_sig)))

        steps = softplus(raw)
        cumul = cumulated(steps, bias_rate, lower)
        cumul_t = cumul.T
        wide = dot_exact(jnp.concatenate([steps, cumul], axis=0), expander, NN)
        step_wide, cumul_wide = wide[:block], wide[block:]
        last_wide = cumul_wide[block - 1 : block]
        tail = jnp.exp(last_wide - cumul_wide)
        scaled = values * step_wide
        b_two, c_two = halves(b_in), halves(c_out)
        scores_t = dot3(b_two, c_two, NT)
        old = st_i[0, s]
        grad = grad_state[s]
        grad_two = halves(grad)
        back = tail * dot3(b_two, grad_two, NN)
        inners = []
        d_scores_t = jnp.zeros((block, block), f32)
        for pair in range(heads // 2):
            cols = slice(2 * pair * width, (2 * pair + 2) * width)
            dy_pair = d_y[:, cols].astype(bf16)
            products = lax.dot_general(
                pair_halves(scaled[:, cols], block, width).astype(bf16), dy_pair, NT, preferred_element_type=f32
            )
            both = []
            for k in range(2):
                h = 2 * pair + k
                gap = jnp.where(later, cumul_t[h : h + 1, :] - cumul[:, h : h + 1], -1e30)
                decay = jnp.exp(gap)
                both.append((scores_t * decay).astype(bf16))
                d_scores_t += products[k * block : (k + 1) * block] * decay
            inners.append(
                lax.dot_general(
                    jnp.concatenate(both, axis=1),
                    pair_halves(d_y[:, cols], block, width).astype(bf16),
                    NN,
                    preferred_element_type=f32,
                )
            )
        back = back + jnp.concatenate(inners, axis=1)
        lifted = halves(d_y * jnp.exp(cumul_wide))
        ds_two = halves(d_scores_t)
        d_c = dot3(ds_two, b_two, TN) + dot3(lifted, old, NT)
        d_b = dot3(ds_two, c_two, NN) + dot3(scaled * tail, grad_two, NT)
        through = jnp.sum(next_state[s] * grad, axis=0, keepdims=True)
        grad_state[s] = jnp.exp(last_wide) * grad + dot3(c_two, lifted, TN)
        next_state[s] = old
        last_row = iota((block, inner), 0) == block - 1
        reduced = dot_exact(
            jnp.concatenate([values * back, d_y * y + jnp.where(last_row, through, 0.0)], axis=0), expander, NT
        )
        d_steps = reduced[:block]
        d_cumul = reduced[block:] - steps * d_steps
        high, mid, low = thirds(d_cumul)
        dot = lambda right: lax.dot_general(upper, right, NN, preferred_element_type=f32)
        d_log = dot(high) + (dot(mid) + dot(low))
        d_raw = (d_steps - d_log * bias_rate) * jax.nn.sigmoid(raw)
        d_values = back * step_wide + skip * d_y
        d_xv = d_values * (sig * (1.0 + xv * (1.0 - sig)))
        start = pl.multiple_of(chunk * rows + s * block, block)
        d_all[pl.ds(start, block), :] = jnp.concatenate([d_xv, d_gate, d_b, d_c, d_raw], axis=1).astype(bf16)

    here = d_all[pl.ds(pl.multiple_of(chunk * rows, rows), rows), :]
    partial = lax.dot_general(here, weights[...], NT, preferred_element_type=f32)
    partial = partial.reshape(near_o.shape)
    near_o[...] = partial
    far_o[...] = partial.astype(bf16)

    @pl.when(step == chunks - 1)
    def _():
        slab = 256
        for first in range(0, term_o.shape[0], slab):
            left = tok[:, :, :, first : first + slab].reshape(chunks * rows, slab)
            term_o[first : first + slab, :] = lax.dot_general(
                left, d_all[...], TN, preferred_element_type=f32
            ).astype(bf16)


def chunk_spec(shape, count=None):
    blank = (0,) * (len(shape) - 1)
    if count is None:
        return pl.BlockSpec((1,) + shape[1:], lambda i: (i,) + blank)
    return pl.BlockSpec((1,) + shape[1:], lambda i: (count - 1 - i,) + blank)


def fixed_spec(shape):
    return pl.BlockSpec(shape, lambda i: (0,) * len(shape))


def forward_call(tok, weights, par, cot, width):
    chunks, seqs, block, model = tok.shape
    inner = cot.shape[3]
    shapes = [
        (chunks, seqs, block, inner),
        (chunks, seqs, block, inner),
        (chunks, seqs, block, 3 * lanes),
        (chunks, seqs, block, inner),
        (chunks, seqs, lanes, inner),
        (chunks, 8, seqs * block),
    ]

    def kernel(*refs):
        forward_kernel(*refs, seqs=seqs, block=block, width=width, inner=inner)

    return pl.pallas_call(
        kernel,
        grid=(chunks,),
        in_specs=[chunk_spec(tok.shape), fixed_spec(weights.shape), fixed_spec(par.shape), chunk_spec(cot.shape)],
        out_specs=[chunk_spec(s) for s in shapes],
        out_shape=[jax.ShapeDtypeStruct(s, f32) for s in shapes],
        scratch_shapes=[pltpu.VMEM((seqs, lanes, inner), f32)],
        compiler_params=pltpu.CompilerParams(vmem_limit_bytes=vmem),
        name="forward_scan",
    )(tok, weights, par, cot)


def backward_call(xv, gate, bc, y, states, cot, stats, par, tok, weights, width, total):
    chunks, seqs, block, inner = xv.shape
    model, columns = weights.shape
    ins = (xv, gate, bc, y, states, cot) + tuple(stats)
    fixed = (par, tok, weights)
    split_spec = pl.BlockSpec((1, 1, seqs, block, model), lambda i: ((chunks - 1 - i) % 2, (chunks - 1 - i) // 2, 0, 0, 0))
    split_shape = (2, chunks // 2, seqs, block, model)

    def kernel(*refs):
        backward_kernel(*refs, seqs=seqs, block=block, width=width, inner=inner, total=total, chunks=chunks)

    return pl.pallas_call(
        kernel,
        grid=(chunks,),
        in_specs=[chunk_spec(a.shape, chunks) for a in ins] + [fixed_spec(a.shape) for a in fixed],
        out_specs=[chunk_spec(xv.shape, chunks), split_spec, split_spec, fixed_spec((model, columns))],
        out_shape=[
            jax.ShapeDtypeStruct(xv.shape, bf16),
            jax.ShapeDtypeStruct(split_shape, f32),
            jax.ShapeDtypeStruct(split_shape, bf16),
            jax.ShapeDtypeStruct((model, columns), bf16),
        ],
        scratch_shapes=[
            pltpu.VMEM((seqs, lanes, inner), f32),
            pltpu.VMEM((seqs, lanes, inner), f32),
            pltpu.VMEM((chunks * seqs * block, columns), bf16),
        ],
        compiler_params=pltpu.CompilerParams(vmem_limit_bytes=vmem),
        name="backward_scan",
    )(*ins, *fixed)


def partner(a):
    return lax.ppermute(a, "core", [(0, 1), (1, 0)])


def around(give, mine):
    came = [give(mine)]
    spot = lambda y: (y % 2) * 2 + y // 2
    for shift in (1, 3, 2):
        pairs = [(spot(y), spot((y + shift) % 4)) for y in range(4)]
        came.append(lax.ppermute(give((mine + shift) % 4), ("yl", "yh"), pairs))
    return [came[0], came[1], came[3], came[2]]


def in_order(came, mine):
    turned = [came[0], came[3], came[2], came[1]]
    return lax.dynamic_slice_in_dim(jnp.stack(turned + turned), 4 - mine, 4, 0)


def by_core(own, other, core):
    first = core == 0
    return jnp.stack([jnp.where(first, own, other), jnp.where(first, other, own)])


def body(tokens, cotangent, w_xz, w_bcdt, rate, dt_bias, skip, gain):
    group = lax.axis_size(group_axes)
    devices = lax.axis_size(whole)
    mine = lax.axis_index(group_axes)
    chunks = lax.axis_size("yl") * lax.axis_size("core")
    seqs = group // chunks
    owners = lax.axis_size(rows_axes)
    block, model = tokens.shape[1:]
    total = cotangent.shape[2]
    inner = total // group
    heads = rate.shape[0] // group
    width = inner // heads
    states = (w_bcdt.shape[1] - rate.shape[0]) // 2

    def picked(target):
        w_dt = lax.dynamic_slice_in_dim(w_bcdt[:, 2 * states :], target * heads, heads, 1)
        return jnp.concatenate(
            [
                lax.dynamic_slice_in_dim(w_xz, target * inner, inner, 1),
                lax.dynamic_slice_in_dim(w_xz, total + target * inner, inner, 1),
                w_bcdt[:, : 2 * states],
                jnp.pad(w_dt, ((0, 0), (0, lanes - heads))),
            ],
            axis=1,
        )

    w_picked = jnp.stack([picked(lax.axis_index(("yl", "core")) * seqs + k) for k in range(seqs)])
    copies = jnp.broadcast_to(w_picked[:, None], (seqs, owners // seqs) + w_picked.shape[1:])
    copies = copies.reshape((owners,) + w_picked.shape[1:])
    weights = lax.all_to_all(copies, rows_axes, 0, 0, tiled=True).reshape(model, -1)

    core = lax.axis_index("core")
    here = lax.axis_index(("yh", "yl"))
    at = lambda a, index: lax.dynamic_index_in_dim(a, index, 0, keepdims=False)

    tok = in_order(around(lambda y: tokens[0], here), here)
    tok = by_core(tok, partner(tok), core)
    tok = tok.reshape(2, 2, 2, block, model).transpose(2, 0, 1, 3, 4).reshape(chunks, seqs, block, model)

    cut = cotangent[0].reshape(block, 2, 2, 2, inner).transpose(2, 3, 1, 0, 4)
    cut = cut.reshape(2, 4, block, inner)
    cut = by_core(at(cut, core), partner(at(cut, 1 - core)), core)
    cot = in_order(around(lambda y: lax.dynamic_index_in_dim(cut, y, 1, keepdims=False), here), here)
    cot = cot.reshape(2, 2, 2, block, inner).transpose(1, 2, 0, 3, 4).reshape(chunks, seqs, block, inner)

    own = lambda a: lax.dynamic_slice_in_dim(a, mine * heads, heads, 0)
    padded = lambda a: jnp.pad(own(a), (0, inner - heads))
    par = jnp.stack(
        [jnp.repeat(own(skip), width), lax.dynamic_slice_in_dim(gain, mine * inner, inner, 0)]
        + [padded(dt_bias), padded(rate)]
        + [jnp.zeros((inner,), f32)] * 4
    )
    xv, gate, bc, y, chunk_states, stats = forward_call(tok, weights, par, cot, width)
    stats = stats + partner(stats)
    stats = around(lambda y: stats, here)
    out, near, far, term = backward_call(
        xv, gate, bc, y, chunk_states, cot, stats, par, tok, weights, width, float(total)
    )
    shares = lax.all_to_all(term.reshape(devices, model // devices, -1), whole, 0, 0, tiled=True)

    both = at(near, core) + partner(at(far, 1 - core)).astype(f32)
    both = both.astype(bf16).transpose(1, 0, 2, 3).reshape(4, block, model)
    came = around(lambda y: at(both, y), here)
    grad_input = sum(a.astype(f32) for a in came).astype(bf16)[None]

    given = out.reshape(2, 2, 2, block, inner).transpose(2, 0, 1, 3, 4).reshape(4, 2, block, inner)
    came = in_order(around(lambda y: at(given, y), here), here)
    pick = lambda index: lax.dynamic_index_in_dim(came, index, 1, keepdims=False)
    layer_out = by_core(pick(core), partner(pick(1 - core)), core)
    layer_out = layer_out.reshape(2, 2, 2, block, inner).transpose(3, 2, 0, 1, 4).reshape(1, block, total)

    summed = shares.reshape(group, devices // group, model // devices, -1).astype(f32).sum(axis=1)
    spread = lambda a: a.transpose(1, 0, 2).reshape(model // devices, -1)
    grad_xz = jnp.concatenate([spread(summed[..., :inner]), spread(summed[..., inner : 2 * inner])], axis=1)
    grad_bcdt = jnp.concatenate(
        [
            summed[..., 2 * inner : 2 * inner + 2 * states].sum(axis=0),
            spread(summed[..., 2 * inner + 2 * states : 2 * inner + 2 * states + heads]),
        ],
        axis=1,
    )
    return (layer_out, grad_input, grad_xz, grad_bcdt)


def solution(mesh):
    split = Mesh(mesh.devices.reshape(2, 2, 2, 4, 4), whole)
    ctx, fsdp = ("yl", "core"), rows_axes
    placed = (P(fsdp, ctx, None), P(fsdp, ctx, None), P(fsdp, None), P(fsdp, None), P(), P(), P(), P())
    return jax.shard_map(
        body,
        mesh=split,
        in_specs=placed,
        out_specs=(P(fsdp, ctx, None), P(fsdp, ctx, None), P(ctx + fsdp, None), P(ctx + fsdp, None)),
        check_vma=False,
    )
```

```python
import jax
import jax.numpy as jnp
from jax import lax
from jax.experimental import pallas as pl
from jax.experimental.pallas import tpu as pltpu
from jax.sharding import Mesh, PartitionSpec as P

f32 = jnp.float32
bf16 = jnp.bfloat16
norm_eps = 1e-05
lanes = 128
NN = (((1,), (0,)), ((), ()))
NT = (((1,), (1,)), ((), ()))
TN = (((0,), (0,)), ((), ()))

whole = ("yl", "core", "yh", "x", "z")
rows_axes = ("yh", "x", "z")
group_axes = ("yl", "core", "yh")
vmem = 32 * 2**20


def dot1(a, b, dims):
    return lax.dot_general(a.astype(bf16), b.astype(bf16), dims, preferred_element_type=f32)


def halves(a):
    high = a.astype(bf16)
    return (high, (a - high.astype(f32)).astype(bf16))


def dot3(a, b, dims):
    a_high, a_low = a if isinstance(a, tuple) else halves(a)
    b_high, b_low = b if isinstance(b, tuple) else halves(b)
    dot = lambda left, right: lax.dot_general(left, right, dims, preferred_element_type=f32)
    (ca,), (cb,) = dims[0]
    both = dot(jnp.concatenate([a_high, a_low], axis=ca), jnp.concatenate([b_high, b_high], axis=cb))
    return both + dot(a_high, b_low)


def thirds(a):
    high = a.astype(bf16)
    rest = a - high.astype(f32)
    mid = rest.astype(bf16)
    return (high, mid, (rest - mid.astype(f32)).astype(bf16))


def dot_ones(pieces, ones, dims):
    first, *rest = [lax.dot_general(a, ones, dims, preferred_element_type=f32) for a in pieces]
    return first + sum(rest[1:], rest[0])


def spread_out(steps, cumul, expander):
    block = steps.shape[0]
    (s_high, s_low), (c_high, c_mid, c_low) = halves(steps), thirds(cumul)
    stacked = jnp.concatenate([s_high, s_low, c_high, c_mid, c_low], axis=0)
    wide = lax.dot_general(stacked, expander, NN, preferred_element_type=f32)
    at = lambda k: wide[k * block : (k + 1) * block]
    return at(0) + at(1), at(2) + (at(3) + at(4))


def iota(shape, axis):
    return lax.broadcasted_iota(jnp.int32, shape, axis)


def head_expander(inner, width, units):
    shape = (lanes, units * inner)
    start = iota(shape, 0) * width
    col = iota(shape, 1)
    return ((col >= start) & (col < start + width)).astype(f32).astype(bf16)


def packed(parts, heads):
    keep = iota(parts[0].shape, 1) < heads
    kept = [jnp.where(keep, a, 0.0) for a in parts]
    return sum(a if u == 0 else pltpu.roll(a, u * heads, 1) for u, a in enumerate(kept))


def unpacked(a, unit, heads):
    moved = a if unit == 0 else pltpu.roll(a, lanes - unit * heads, 1)
    return jnp.where(iota(a.shape, 1) < heads, moved, 0.0)


def beside(parts):
    return jnp.concatenate(list(parts), axis=1)


def lower_ones(block):
    shape = (block, block)
    return (iota(shape, 0) >= iota(shape, 1)).astype(f32).astype(bf16)


def ones_dot(ones, pieces):
    width = pieces[0].shape[1]
    wide = lax.dot_general(ones, jnp.concatenate(pieces, axis=1), NN, preferred_element_type=f32)
    parts = [wide[:, k * width : (k + 1) * width] for k in range(len(pieces))]
    return parts[0] + sum(parts[2:], parts[1])


def softplus(a):
    return jnp.maximum(a, 0.0) + jnp.log1p(jnp.exp(-jnp.abs(a)))


def pair_halves(a, block, width):
    left = iota(a.shape, 1) < width
    zero = jnp.zeros_like(a)
    return jnp.concatenate([jnp.where(left, a, zero), jnp.where(left, zero, a)], axis=0)


def forward_kernel(tok, weights, par, cot, xv_o, g_o, bc_o, low_o, y_o, st_o, stat_o, state, *, width, inner):
    _, seqs, block, _ = tok.shape
    units = [(j, s) for j in range(tok.shape[0]) for s in range(seqs)]
    count = len(units)
    heads = inner // width

    @pl.when(pl.program_id(0) == 0)
    def _():
        state[...] = jnp.zeros_like(state)

    proj = lax.dot_general(tok[...].reshape(count * block, -1), weights[...], NN, preferred_element_type=f32)
    cut = lambda u, first, size: proj[u * block : (u + 1) * block, first : first + size]
    part = lambda a, u: a[:, u * inner : (u + 1) * inner]
    expander = head_expander(inner, width, count)
    causal = iota((block, block), 0) >= iota((block, block), 1)
    skip, gain = beside([par[0:1, :]] * count), beside([par[1:2, :]] * count)
    bias, rate = par[2:3, :lanes], par[3:4, :lanes]

    raw = packed([cut(u, 2 * inner + 2 * lanes, lanes) for u in range(count)], heads) + bias
    steps = softplus(raw)
    cumul = ones_dot(lower_ones(block), thirds(-steps * rate))
    cumul_t = cumul.T
    low_o[0, 0], low_o[0, 1], low_o[0, 2] = raw, steps, cumul
    b_two, c_two = [], []
    for u, (j, s) in enumerate(units):
        b_in, c_out = cut(u, 2 * inner, lanes), cut(u, 2 * inner + lanes, lanes)
        bc_o[j, s] = beside([b_in, c_out])
        xv_o[j, s] = cut(u, 0, inner)
        g_o[j, s] = cut(u, inner, inner)
        b_two.append(halves(b_in))
        c_two.append(halves(c_out))
    scores = [dot3(c_two[u], b_two[u], NT) for u in range(count)]
    step_wide, cumul_wide = spread_out(steps, cumul, expander)
    last_wide = cumul_wide[block - 1 : block]
    xv = beside(cut(u, 0, inner) for u in range(count))
    gate = beside(cut(u, inner, inner) for u in range(count))
    values = xv * jax.nn.sigmoid(xv)
    scaled = values * step_wide
    tailed = scaled * jnp.exp(last_wide - cumul_wide)
    last_decay = jnp.exp(last_wide)
    updates = [dot3(b_two[u], part(tailed, u), TN) for u in range(count)]
    inners = []
    for u in range(count):
        for pair in range(heads // 2):
            both = []
            for h in (u * heads + 2 * pair, u * heads + 2 * pair + 1):
                gap = jnp.where(causal, cumul[:, h : h + 1] - cumul_t[h : h + 1, :], -1e30)
                both.append((scores[u] * jnp.exp(gap)).astype(bf16))
            first = u * inner + 2 * pair * width
            cols = scaled[:, first : first + 2 * width]
            inners.append(
                lax.dot_general(
                    beside(both), pair_halves(cols, block, width).astype(bf16), NN, preferred_element_type=f32
                )
            )
    carried = []
    for u, (j, s) in enumerate(units):
        old = state[s]
        st_o[j, s] = old
        carried.append(dot3(c_two[u], old, NN))
        state[s] = part(last_decay, u) * old + updates[u]
    y = jnp.exp(cumul_wide) * beside(carried) + beside(inners) + skip * values
    mixed = y * (gate * jax.nn.sigmoid(gate))
    weighted = beside(cot[j, s] for j, s in units).astype(f32) * gain * mixed
    squared = mixed * mixed
    row, col = iota((8, 2 * inner), 0), iota((8, 2 * inner), 1)
    chooser = ((row < 2) & ((col >= inner) == (row == 1))).astype(f32).astype(bf16)
    for u, (j, s) in enumerate(units):
        y_o[j, s] = part(y, u)
        high, low = halves(beside([part(squared, u), part(weighted, u)]))
        dot = lambda right: lax.dot_general(chooser, right, NT, preferred_element_type=f32)
        stat_o[0, :, u * block : (u + 1) * block] = dot(high) + dot(low)


def norm_kernel(y_i, g_i, cot, stat_0, stat_1, stat_2, stat_3, par, out_o, dy_o, dg_o, *, total):
    _, seqs, block, inner = y_i.shape
    gain = par[1:2, :]
    sums = (stat_0[0] + stat_1[0]) + (stat_2[0] + stat_3[0])
    scale_row = lax.rsqrt(sums[0:1] * (1.0 / total) + norm_eps)
    pull_row = scale_row * scale_row * scale_row * sums[1:2] * (1.0 / total)
    stacked = jnp.concatenate([scale_row, pull_row, jnp.zeros((6, scale_row.shape[1]), f32)], axis=0)
    row, col = iota((8, 2 * inner), 0), iota((8, 2 * inner), 1)
    chooser = ((row < 2) & ((col >= inner) == (row == 1))).astype(f32).astype(bf16)
    spread = dot_ones(halves(stacked), chooser, TN)
    for u in range(y_i.shape[0] * seqs):
        j, s = u // seqs, u % seqs
        span = slice(u * block, (u + 1) * block)
        scale, pull = spread[span, :inner], spread[span, inner:]
        gate, full = g_i[j, s], y_i[j, s]
        gate_sig = jax.nn.sigmoid(gate)
        gate_silu = gate * gate_sig
        mixed = full * gate_silu
        out_o[j, s] = (mixed * scale * gain).astype(bf16)
        d_mixed = cot[j, s].astype(f32) * gain * scale - mixed * pull
        dy_o[j, s] = d_mixed * gate_silu
        dg_o[j, s] = (d_mixed * full * (gate_sig * (1.0 + gate * (1.0 - gate_sig)))).astype(bf16)


def backward_kernel(
    core, xv_i, bc_i, low_i, y_i, st_i, dy_i, dg_i, tok, par, weights,
    near_o, far_o, term_o, give_o, grad_state, next_state, term, *, width, inner
):
    per_step, seqs, block, model = tok.shape
    units = [(j, s) for j in range(per_step) for s in range(seqs)]
    count = len(units)
    heads = inner // width
    step = pl.program_id(0)

    @pl.when(step == 0)
    def _():
        grad_state[...] = jnp.zeros_like(grad_state)
        next_state[...] = jnp.zeros_like(next_state)
        term[...] = jnp.zeros_like(term)

    part = lambda a, u: a[:, u * inner : (u + 1) * inner]
    expander = head_expander(inner, width, count)
    later = iota((block, block), 1) >= iota((block, block), 0)
    upper = (iota((block, block), 1) >= iota((block, block), 0)).astype(f32).astype(bf16)
    skip, rate = beside([par[0:1, :]] * count), par[3:4, :lanes]
    raw, steps, cumul = low_i[0, 0], low_i[0, 1], low_i[0, 2]
    cumul_t = cumul.T
    step_wide, cumul_wide = spread_out(steps, cumul, expander)
    last_wide = cumul_wide[block - 1 : block]
    tail, last_decay = jnp.exp(last_wide - cumul_wide), jnp.exp(last_wide)
    b_two = [halves(bc_i[j, s, :, :lanes]) for j, s in units]
    c_two = [halves(bc_i[j, s, :, lanes:]) for j, s in units]
    scores_t = [dot3(b_two[u], c_two[u], NT) for u in range(count)]
    xv = beside(xv_i[j, s] for j, s in units)
    d_y = beside(dy_i[j, s] for j, s in units)
    sig = jax.nn.sigmoid(xv)
    values = xv * sig
    y = beside(y_i[j, s] for j, s in units) - skip * values
    scaled = values * step_wide
    tailed = scaled * tail
    lifted = halves(d_y * jnp.exp(cumul_wide))
    lifted = [(part(lifted[0], u), part(lifted[1], u)) for u in range(count)]
    updates = [dot3(c_two[u], lifted[u], TN) for u in range(count)]

    back, through, from_state = [None] * count, [None] * count, [None] * count
    for u in reversed(range(count)):
        j, s = units[u]
        grad = grad_state[s]
        grad_two = halves(grad)
        back[u] = dot3(b_two[u], grad_two, NN)
        from_state[u] = dot3(part(tailed, u), grad_two, NT)
        through[u] = jnp.sum(next_state[s] * grad, axis=0, keepdims=True)
        grad_state[s] = part(last_decay, u) * grad + updates[u]
        next_state[s] = st_i[j, s]

    inners, d_scores = [], []
    for u in range(count):
        d_scores_t = jnp.zeros((block, block), f32)
        for pair in range(heads // 2):
            first = u * inner + 2 * pair * width
            cols = slice(first, first + 2 * width)
            products = lax.dot_general(
                pair_halves(scaled[:, cols], block, width).astype(bf16),
                d_y[:, cols].astype(bf16),
                NT,
                preferred_element_type=f32,
            )
            both = []
            for k in range(2):
                h = u * heads + 2 * pair + k
                gap = jnp.where(later, cumul_t[h : h + 1, :] - cumul[:, h : h + 1], -1e30)
                decay = jnp.exp(gap)
                both.append((scores_t[u] * decay).astype(bf16))
                d_scores_t += products[k * block : (k + 1) * block] * decay
            inners.append(
                lax.dot_general(
                    beside(both), pair_halves(d_y[:, cols], block, width).astype(bf16), NN, preferred_element_type=f32
                )
            )
        d_scores.append(halves(d_scores_t))
    d_c = [
        dot3(d_scores[u], b_two[u], TN) + dot3(lifted[u], st_i[j, s], NT) for u, (j, s) in enumerate(units)
    ]
    d_b = [dot3(d_scores[u], c_two[u], NN) + from_state[u] for u in range(count)]
    back = tail * beside(back) + beside(inners)
    last_row = iota((block, count * inner), 0) == block - 1
    products = jnp.concatenate([values * back, d_y * y + jnp.where(last_row, beside(through), 0.0)], axis=0)
    reduced = dot_ones(halves(products), expander, NT)
    d_steps = reduced[:block]
    d_log = ones_dot(upper, halves(reduced[block:] - steps * d_steps))
    d_raw = (d_steps - d_log * rate) * jax.nn.sigmoid(raw)
    d_values = back * step_wide + skip * d_y
    d_xv = (d_values * (sig * (1.0 + xv * (1.0 - sig)))).astype(bf16)
    here = jnp.concatenate(
        [
            beside([part(d_xv, u), dg_i[j, s], d_b[u].astype(bf16), d_c[u].astype(bf16)]
                   + [unpacked(d_raw, u, heads).astype(bf16)])
            for u, (j, s) in enumerate(units)
        ],
        axis=0,
    )
    term[...] += lax.dot_general(tok[...].reshape(count * block, model), here, TN, preferred_element_type=f32)
    partial = lax.dot_general(here, weights[...], NT, preferred_element_type=f32)
    partial = partial.reshape(per_step, seqs, block, model)
    first = core[0] == 0

    @pl.when(first)
    def _():
        near_o[0] = partial[0]
        far_o[0] = partial[1].astype(bf16)

    @pl.when(jnp.logical_not(first))
    def _():
        near_o[0] = partial[1]
        far_o[0] = partial[0].astype(bf16)

    @pl.when(step == pl.num_programs(0) - 1)
    def _():
        wide = 2 * inner
        term_o[:, :wide] = term[:, :wide].astype(bf16)
        term_o[:, wide + lanes :] = term[:, wide + 2 * lanes :].astype(bf16)
        b_part, c_part = term[:, wide : wide + lanes], term[:, wide + lanes : wide + 2 * lanes]
        term_o[:, wide : wide + lanes] = jnp.where(first, b_part, c_part).astype(bf16)
        give_o[...] = jnp.where(first, c_part, b_part).astype(bf16)


def join_kernel(_, near, far, term, got, out_0, out_1, out_2, out_3, term_o):
    step = pl.program_id(0)
    both = (near[0, 0] + far[0, 0].astype(f32)).astype(bf16)
    for k, out in enumerate((out_0, out_1, out_2, out_3)):

        @pl.when(step == k)
        def _(out=out):
            out[...] = both

    @pl.when(step == 0)
    def _():
        term_o[...] = (term[...].astype(f32) + got[...].astype(f32)).astype(bf16)


def total_kernel(shares, xz_o, bcdt_o, *, inner, heads, group):
    step = pl.program_id(0)
    half = group * inner

    @pl.when(step == 0)
    def _():
        bcdt_o[...] = jnp.zeros_like(bcdt_o)

    summed = jnp.sum(shares[0].astype(f32), axis=0)
    at = pl.multiple_of(step * inner, inner)
    xz_o[:, pl.ds(at, inner)] = summed[:, :inner]
    xz_o[:, pl.ds(pl.multiple_of(half + at, inner), inner)] = summed[:, inner : 2 * inner]
    core = lax.rem(lax.div(step, 2), 2)
    bc = summed[:, 2 * inner : 2 * inner + lanes]
    bcdt_o[:, :lanes] += jnp.where(core == 0, bc, 0.0)
    bcdt_o[:, lanes : 2 * lanes] += jnp.where(core == 0, 0.0, bc)
    steps = summed[:, 2 * inner + lanes :]
    lane = iota(steps.shape, 1)
    moved = pltpu.roll(jnp.where(lane < heads, steps, 0.0), step * heads, 1)
    bcdt_o[:, 2 * lanes :] += moved[:, : group * heads]


def cost(micros):
    return pl.CostEstimate(flops=int(micros * 1.1e9), bytes_accessed=int(micros * 3.5e6), transcendentals=0)


def chunk_spec(shape, count=None, per_step=1):
    blank = (0,) * (len(shape) - 1)
    if count is None:
        return pl.BlockSpec((per_step,) + shape[1:], lambda i: (i,) + blank)
    return pl.BlockSpec((per_step,) + shape[1:], lambda i: (count - 1 - i,) + blank)


def fixed_spec(shape):
    return pl.BlockSpec(shape, lambda i: (0,) * len(shape))


chunks_per_step = 2


def forward_call(tok, weights, par, cot, width):
    chunks, seqs, block, model = tok.shape
    inner = cot.shape[3]
    steps = chunks // chunks_per_step
    wide = (chunks, seqs, block, inner)
    by_chunk = lambda a: chunk_spec(a, per_step=chunks_per_step)
    outs = [
        (wide, by_chunk),
        (wide, by_chunk),
        ((chunks, seqs, block, 2 * lanes), by_chunk),
        ((steps, 3, block, lanes), chunk_spec),
        (wide, by_chunk),
        ((chunks, seqs, lanes, inner), by_chunk),
        ((steps, 8, chunks_per_step * seqs * block), chunk_spec),
    ]

    def kernel(*refs):
        forward_kernel(*refs, width=width, inner=inner)

    return pl.pallas_call(
        kernel,
        grid=(steps,),
        in_specs=[by_chunk(tok.shape), fixed_spec(weights.shape), fixed_spec(par.shape), by_chunk(cot.shape)],
        out_specs=[spec(a) for a, spec in outs],
        out_shape=[jax.ShapeDtypeStruct(a, f32) for a, _ in outs],
        scratch_shapes=[pltpu.VMEM((seqs, lanes, inner), f32)],
        compiler_params=pltpu.CompilerParams(vmem_limit_bytes=vmem),
        cost_estimate=cost(12),
        name="forward_scan",
    )(tok, weights, par, cot)


def norm_call(y, gate, cot, stats, par, total):
    chunks = y.shape[0]
    by_chunk = lambda a: chunk_spec(a.shape, per_step=chunks_per_step)

    def kernel(*refs):
        norm_kernel(*refs, total=total)

    return pl.pallas_call(
        kernel,
        grid=(chunks // chunks_per_step,),
        in_specs=[by_chunk(a) for a in (y, gate, cot)] + [chunk_spec(a.shape) for a in stats] + [fixed_spec(par.shape)],
        out_specs=[by_chunk(y)] * 3,
        out_shape=[jax.ShapeDtypeStruct(y.shape, kind) for kind in (bf16, f32, bf16)],
        compiler_params=pltpu.CompilerParams(vmem_limit_bytes=vmem),
        cost_estimate=cost(5),
        name="gated_norm",
    )(y, gate, cot, *stats, par)


def backward_call(core, xv, bc, low, y, states, d_y, d_gate, tok, par, weights, width):
    chunks, seqs, block, inner = xv.shape
    model, columns = weights.shape
    steps = chunks // chunks_per_step
    half = (steps, seqs, block, model)
    half_spec = chunk_spec(half, steps)
    by_chunk = lambda a: chunk_spec(a.shape, steps, chunks_per_step)

    def kernel(*refs):
        backward_kernel(*refs, width=width, inner=inner)

    return pl.pallas_call(
        kernel,
        grid=(steps,),
        in_specs=[pl.BlockSpec(memory_space=pltpu.SMEM), by_chunk(xv), by_chunk(bc), chunk_spec(low.shape, steps)]
        + [by_chunk(a) for a in (y, states, d_y, d_gate, tok)]
        + [fixed_spec(par.shape), fixed_spec(weights.shape)],
        out_specs=[half_spec, half_spec, fixed_spec((model, columns - lanes)), fixed_spec((model, lanes))],
        out_shape=[
            jax.ShapeDtypeStruct(half, f32),
            jax.ShapeDtypeStruct(half, bf16),
            jax.ShapeDtypeStruct((model, columns - lanes), bf16),
            jax.ShapeDtypeStruct((model, lanes), bf16),
        ],
        scratch_shapes=[
            pltpu.VMEM((seqs, lanes, inner), f32),
            pltpu.VMEM((seqs, lanes, inner), f32),
            pltpu.VMEM((model, columns), f32),
        ],
        compiler_params=pltpu.CompilerParams(vmem_limit_bytes=vmem),
        cost_estimate=cost(20),
        name="backward_scan",
    )(core, xv, bc, low, y, states, d_y, d_gate, tok, par, weights)


def join_call(here, near, far, term, got, inner):
    halves_of, seqs, block, model = near.shape
    count = halves_of * seqs
    bc_spec = pl.BlockSpec((term.shape[0], lanes), lambda k, here: (0, 2 * inner // lanes))

    def place(k, here):
        y = lax.rem(here[0] + k, count)
        return (lax.rem(y, 2), lax.div(y, 2), 0, 0)

    spec = pl.BlockSpec((1, 1, block, model), place)
    return pl.pallas_call(
        join_kernel,
        grid_spec=pltpu.PrefetchScalarGridSpec(
            num_scalar_prefetch=1,
            grid=(count,),
            in_specs=[spec, spec, bc_spec, pl.BlockSpec(got.shape, lambda k, here: (0, 0))],
            out_specs=[pl.BlockSpec((block, model), lambda k, here: (0, 0))] * count + [bc_spec],
        ),
        out_shape=[jax.ShapeDtypeStruct((block, model), bf16)] * count + [jax.ShapeDtypeStruct(term.shape, bf16)],
        input_output_aliases={3: count},
        compiler_params=pltpu.CompilerParams(vmem_limit_bytes=vmem),
        cost_estimate=cost(3),
        name="join_halves",
    )(here, near, far, term, got)


def total_call(shares, inner, heads):
    group, _, rows, columns = shares.shape
    shapes = [(rows, 2 * group * inner), (rows, 2 * lanes + group * heads)]

    def kernel(*refs):
        total_kernel(*refs, inner=inner, heads=heads, group=group)

    return pl.pallas_call(
        kernel,
        grid=(group,),
        in_specs=[chunk_spec(shares.shape)],
        out_specs=[fixed_spec(a) for a in shapes],
        out_shape=[jax.ShapeDtypeStruct(a, f32) for a in shapes],
        compiler_params=pltpu.CompilerParams(vmem_limit_bytes=vmem),
        cost_estimate=cost(2),
        name="total_shares",
    )(shares)


def partner(a):
    return lax.ppermute(a, "core", [(0, 1), (1, 0)])


def around(give, mine):
    came = [give(0 if mine is None else mine)]
    spot = lambda y: (y % 2) * 2 + y // 2
    for shift in (1, 3, 2):
        pairs = [(spot(y), spot((y + shift) % 4)) for y in range(4)]
        came.append(lax.ppermute(give(shift if mine is None else (mine + shift) % 4), ("yl", "yh"), pairs))
    return [came[0], came[1], came[3], came[2]]


def in_order(came, mine):
    turned = [came[0], came[3], came[2], came[1]]
    return lax.dynamic_slice_in_dim(jnp.stack(turned + turned), 4 - mine, 4, 0)


def by_core(own, other, core):
    first = core == 0
    return jnp.stack([jnp.where(first, own, other), jnp.where(first, other, own)])


def body(tokens, cotangent, w_xz, w_bcdt, rate, dt_bias, skip, gain):
    group = lax.axis_size(group_axes)
    devices = lax.axis_size(whole)
    mine = lax.axis_index(group_axes)
    chunks = lax.axis_size("yl") * lax.axis_size("core")
    seqs = group // chunks
    owners = lax.axis_size(rows_axes)
    block, model = tokens.shape[1:]
    total = cotangent.shape[2]
    inner = total // group
    heads = rate.shape[0] // group
    width = inner // heads
    states = (w_bcdt.shape[1] - rate.shape[0]) // 2

    def picked(target):
        w_dt = lax.dynamic_slice_in_dim(w_bcdt[:, 2 * states :], target * heads, heads, 1)
        return jnp.concatenate(
            [
                lax.dynamic_slice_in_dim(w_xz, target * inner, inner, 1),
                lax.dynamic_slice_in_dim(w_xz, total + target * inner, inner, 1),
                w_bcdt[:, : 2 * states],
                jnp.pad(w_dt, ((0, 0), (0, lanes - heads))),
            ],
            axis=1,
        )

    yl, yh, core = lax.axis_index("yl"), lax.axis_index("yh"), lax.axis_index("core")
    w_picked = jnp.stack([picked((((yl + yh + k) % 2) * 2 + core) * seqs + k) for k in range(seqs)])
    copies = jnp.broadcast_to(w_picked[:, None], (seqs, owners // seqs) + w_picked.shape[1:])
    copies = copies.reshape((owners,) + w_picked.shape[1:])
    rest = owners // seqs
    traders = [
        [(((start + k) % 2) * seqs + k) * rest + i for k in range(seqs) for i in range(rest)] for start in range(2)
    ]
    weights = lax.all_to_all(copies, ("yl",) + rows_axes, 0, 0, axis_index_groups=traders, tiled=True)
    weights = weights.reshape(model, -1)

    here = lax.axis_index(("yh", "yl"))
    at = lambda a, index: lax.dynamic_index_in_dim(a, index, 0, keepdims=False)

    tok = in_order(around(lambda y: tokens[0], here), here)
    tok = by_core(tok, partner(tok), core)
    tok = tok.reshape(2, 2, 2, block, model).transpose(2, 0, 1, 3, 4).reshape(chunks, seqs, block, model)

    cut = cotangent[0].reshape(block, 2, 2, 2, inner).transpose(2, 3, 1, 0, 4)
    cut = cut.reshape(2, 4, block, inner)
    cut = by_core(at(cut, core), partner(at(cut, 1 - core)), core)
    cot = in_order(around(lambda y: lax.dynamic_index_in_dim(cut, y, 1, keepdims=False), here), here)
    cot = cot.reshape(2, 2, 2, block, inner).transpose(1, 2, 0, 3, 4).reshape(chunks, seqs, block, inner)

    own = lambda a: lax.dynamic_slice_in_dim(a, mine * heads, heads, 0)
    padded = lambda a: jnp.pad(jnp.tile(own(a), lanes // heads), (0, inner - lanes))
    par = jnp.stack(
        [jnp.repeat(own(skip), width), lax.dynamic_slice_in_dim(gain, mine * inner, inner, 0)]
        + [padded(dt_bias), padded(rate)]
        + [jnp.zeros((inner,), f32)] * 4
    )
    xv, gate, bc, low, y, chunk_states, stats = forward_call(tok, weights, par, cot, width)
    stats = stats + partner(stats)
    stats = around(lambda y: stats, here)
    out, d_y, d_gate = norm_call(y, gate, cot, stats, par, float(total))
    layer_out = lax.all_to_all(out.reshape(group, block, inner), group_axes, 0, 0, tiled=True)
    layer_out = layer_out.transpose(1, 0, 2).reshape(1, block, total)
    scalar = lambda a: jnp.full((1,), a, jnp.int32)
    near, far, term, give = backward_call(
        scalar(core), xv, bc, low, y, chunk_states, d_y, d_gate, tok, par, weights, width
    )
    *sums, term = join_call(scalar(here), near, partner(far), term, partner(give), inner)
    shares = lax.all_to_all(term.reshape(devices, model // devices, -1), whole, 0, 0, tiled=True)
    came = around(lambda shift: sums[shift], None)
    grad_input = sum(a.astype(f32) for a in came).astype(bf16)[None]
    grad_xz, grad_bcdt = total_call(
        shares.reshape(group, devices // group, model // devices, -1), inner, heads
    )
    return (layer_out, grad_input, grad_xz, grad_bcdt)


def solution(mesh):
    split = Mesh(mesh.devices.reshape(2, 2, 2, 4, 4), whole)
    ctx, fsdp = ("yl", "core"), rows_axes
    placed = (P(fsdp, ctx, None), P(fsdp, ctx, None), P(fsdp, None), P(fsdp, None), P(), P(), P(), P())
    return jax.shard_map(
        body,
        mesh=split,
        in_specs=placed,
        out_specs=(P(fsdp, ctx, None), P(fsdp, ctx, None), P(ctx + fsdp, None), P(ctx + fsdp, None)),
        check_vma=False,
    )
```

```python
import jax
import jax.numpy as jnp
from jax import lax
from jax.experimental import pallas as pl
from jax.experimental.pallas import tpu as pltpu
from jax.sharding import Mesh, PartitionSpec as P

f32 = jnp.float32
bf16 = jnp.bfloat16
norm_eps = 1e-05
lanes = 128
NN = (((1,), (0,)), ((), ()))
NT = (((1,), (1,)), ((), ()))
TN = (((0,), (0,)), ((), ()))

whole = ("yl", "core", "yh", "xh", "xl", "z")
rows_axes = ("yh", "xh", "xl", "z")
group_axes = ("yl", "core", "xl")
vmem = 32 * 2**20
wide_vmem = 60 * 2**20
stack_cost, sum_cost = 12, 24


def dot1(a, b, dims):
    return lax.dot_general(a.astype(bf16), b.astype(bf16), dims, preferred_element_type=f32)


def halves(a):
    high = a.astype(bf16)
    return (high, (a - high.astype(f32)).astype(bf16))


def dot3(a, b, dims):
    a_high, a_low = a if isinstance(a, tuple) else halves(a)
    b_high, b_low = b if isinstance(b, tuple) else halves(b)
    dot = lambda left, right: lax.dot_general(left, right, dims, preferred_element_type=f32)
    (ca,), (cb,) = dims[0]
    both = dot(jnp.concatenate([a_high, a_low], axis=ca), jnp.concatenate([b_high, b_high], axis=cb))
    return both + dot(a_high, b_low)


def thirds(a):
    high = a.astype(bf16)
    rest = a - high.astype(f32)
    mid = rest.astype(bf16)
    return (high, mid, (rest - mid.astype(f32)).astype(bf16))


def dot_ones(pieces, ones, dims):
    first, *rest = [lax.dot_general(a, ones, dims, preferred_element_type=f32) for a in pieces]
    return first + sum(rest[1:], rest[0])


def spread_out(steps, cumul, expander):
    block = steps.shape[0]
    (s_high, s_low), (c_high, c_mid, c_low) = halves(steps), thirds(cumul)
    stacked = jnp.concatenate([s_high, s_low, c_high, c_mid, c_low], axis=0)
    wide = lax.dot_general(stacked, expander, NN, preferred_element_type=f32)
    at = lambda k: wide[k * block : (k + 1) * block]
    return at(0) + at(1), at(2) + (at(3) + at(4))


def iota(shape, axis):
    return lax.broadcasted_iota(jnp.int32, shape, axis)


def head_expander(inner, width, units):
    shape = (lanes, units * inner)
    start = iota(shape, 0) * width
    col = iota(shape, 1)
    return ((col >= start) & (col < start + width)).astype(f32).astype(bf16)


def packed(parts, heads):
    keep = iota(parts[0].shape, 1) < heads
    kept = [jnp.where(keep, a, 0.0) for a in parts]
    return sum(a if u == 0 else pltpu.roll(a, u * heads, 1) for u, a in enumerate(kept))


def unpacked(a, unit, heads):
    moved = a if unit == 0 else pltpu.roll(a, lanes - unit * heads, 1)
    return jnp.where(iota(a.shape, 1) < heads, moved, 0.0)


def beside(parts):
    return jnp.concatenate(list(parts), axis=1)


def lower_ones(block):
    shape = (block, block)
    return (iota(shape, 0) >= iota(shape, 1)).astype(f32).astype(bf16)


def ones_dot(ones, pieces):
    width = pieces[0].shape[1]
    wide = lax.dot_general(ones, jnp.concatenate(pieces, axis=1), NN, preferred_element_type=f32)
    parts = [wide[:, k * width : (k + 1) * width] for k in range(len(pieces))]
    return parts[0] + sum(parts[2:], parts[1])


def softplus(a):
    return jnp.maximum(a, 0.0) + jnp.log1p(jnp.exp(-jnp.abs(a)))


def pair_halves(a, block, width):
    left = iota(a.shape, 1) < width
    zero = jnp.zeros_like(a)
    return jnp.concatenate([jnp.where(left, a, zero), jnp.where(left, zero, a)], axis=0)


def pack_kernel(place, tokens, cot, w_xz, w_bcdt, out_0, out_1, out_2, out_3, copies, *, inner, heads, states):
    cols = lambda block, count=1: pl.ds(pl.multiple_of(block * inner, inner), count * inner)
    mine = tokens[...]
    for k, out in enumerate((out_0, out_1, out_2, out_3)):
        chip = lax.bitwise_xor(place[0], k)
        first = lax.rem(chip, 2) * 4 + lax.div(chip, 2)
        out[...] = jnp.concatenate([mine, cot[:, cols(first)], cot[:, cols(first + 2)]], axis=1)

    low = w_bcdt[...].astype(f32)
    rows = low.shape[0]
    filled = jnp.zeros((rows, 2 * lanes - (low.shape[1] - 2 * states)), f32)
    all_steps = jnp.concatenate([low[:, 2 * states :], filled], axis=1)
    half = jnp.where(place[1] == 0, low[:, :states], low[:, states : 2 * states]).astype(bf16)
    group = w_xz.shape[1] // (2 * inner)
    yh, xh, xl, z = copies.shape[:4]
    for side in range(yh):
        for s in range(xl):
            target = (lax.rem(place[2] + side, 2) * 2 + place[1]) * 2 + s
            steps = pltpu.roll(all_steps, 2 * lanes - target * heads, 1)[:, :lanes]
            steps = jnp.where(iota(steps.shape, 1) < heads, steps, 0.0).astype(bf16)
            row = jnp.concatenate([w_xz[:, cols(target)], w_xz[:, cols(group + target)], half, steps], axis=1)
            for upper in range(xh):
                copies[side, upper, s] = jnp.broadcast_to(row[None], (z,) + row.shape)


def whole_weights(main, other, first, inner):
    half, got = main[:, 2 * inner : 2 * inner + lanes], other[...]
    b_part, c_part = jnp.where(first, half, got), jnp.where(first, got, half)
    return jnp.concatenate([main[:, : 2 * inner], b_part, c_part, main[:, 2 * inner + lanes :]], axis=1)


def forward_kernel(place, own, far, w_main, w_other, par, *rest, width, inner):
    *outs, state = rest
    first = place[1] == 0
    weights = whole_weights(w_main, w_other, first, inner)
    state[...] = jnp.zeros_like(state)
    steps = outs[0].shape[0] // chunks_per_step
    for i in range(steps):
        came = [
            [a[lax.bitwise_xor(place[0], 2 * s + i)] for a in (own, far)] for s in range(outs[0].shape[1])
        ]
        views = [a.at[pl.ds(i * (a.shape[0] // steps), a.shape[0] // steps)] for a in outs]
        forward_step(first, came, weights, par, *views, state, width=width, inner=inner)


def forward_step(
    first, came, weights, par, tok, cot, xv_o, g_o, bc_o, low_o, y_o, st_o, stat_o, state, *, width, inner
):
    per_step, seqs, block, model = tok.shape
    units = [(j, s) for j in range(per_step) for s in range(seqs)]
    for s, (own, far) in enumerate(came):
        one, two = jnp.where(first, own, far), jnp.where(first, far, own)
        tok[0, s], tok[1, s] = one[:, :model], two[:, :model]
        cot[0, s], cot[1, s] = one[:, model:], two[:, model:]
    count = len(units)
    heads = inner // width

    proj = lax.dot_general(tok[...].reshape(count * block, -1), weights, NN, preferred_element_type=f32)
    cut = lambda u, first, size: proj[u * block : (u + 1) * block, first : first + size]
    part = lambda a, u: a[:, u * inner : (u + 1) * inner]
    expander = head_expander(inner, width, count)
    causal = iota((block, block), 0) >= iota((block, block), 1)
    skip, gain = beside([par[0:1, :]] * count), beside([par[1:2, :]] * count)
    bias, rate = par[2:3, :lanes], par[3:4, :lanes]

    raw = packed([cut(u, 2 * inner + 2 * lanes, lanes) for u in range(count)], heads) + bias
    steps = softplus(raw)
    cumul = ones_dot(lower_ones(block), thirds(-steps * rate))
    cumul_t = cumul.T
    low_o[0, 0], low_o[0, 1], low_o[0, 2] = raw, steps, cumul
    b_two, c_two = [], []
    for u, (j, s) in enumerate(units):
        b_in, c_out = cut(u, 2 * inner, lanes), cut(u, 2 * inner + lanes, lanes)
        bc_o[j, s] = beside([b_in, c_out])
        xv_o[j, s] = cut(u, 0, inner)
        g_o[j, s] = cut(u, inner, inner)
        b_two.append(halves(b_in))
        c_two.append(halves(c_out))
    scores = [dot3(c_two[u], b_two[u], NT) for u in range(count)]
    step_wide, cumul_wide = spread_out(steps, cumul, expander)
    last_wide = cumul_wide[block - 1 : block]
    xv = beside(cut(u, 0, inner) for u in range(count))
    gate = beside(cut(u, inner, inner) for u in range(count))
    values = xv * jax.nn.sigmoid(xv)
    scaled = values * step_wide
    tailed = scaled * jnp.exp(last_wide - cumul_wide)
    last_decay = jnp.exp(last_wide)
    updates = [dot3(b_two[u], part(tailed, u), TN) for u in range(count)]
    inners = []
    for u in range(count):
        for pair in range(heads // 2):
            both = []
            for h in (u * heads + 2 * pair, u * heads + 2 * pair + 1):
                gap = jnp.where(causal, cumul[:, h : h + 1] - cumul_t[h : h + 1, :], -1e30)
                both.append((scores[u] * jnp.exp(gap)).astype(bf16))
            first = u * inner + 2 * pair * width
            cols = scaled[:, first : first + 2 * width]
            inners.append(
                lax.dot_general(
                    beside(both), pair_halves(cols, block, width).astype(bf16), NN, preferred_element_type=f32
                )
            )
    carried = []
    for u, (j, s) in enumerate(units):
        old = state[s]
        st_o[j, s] = old
        carried.append(dot3(c_two[u], old, NN))
        state[s] = part(last_decay, u) * old + updates[u]
    y = jnp.exp(cumul_wide) * beside(carried) + beside(inners) + skip * values
    mixed = y * (gate * jax.nn.sigmoid(gate))
    weighted = beside(cot[j, s] for j, s in units).astype(f32) * gain * mixed
    squared = mixed * mixed
    sums = []
    for u, (j, s) in enumerate(units):
        y_o[j, s] = part(y, u)
        high, low = halves(beside([part(squared, u), part(weighted, u)]))
        dot = lambda right: lax.dot_general(stat_rows(u, inner), right, NT, preferred_element_type=f32)
        sums.append(dot(high) + dot(low))
    stat_o[0] = (sums[0] + sums[1]) + (sums[2] + sums[3])


def stat_rows(unit, inner):
    row, col = iota((8, 2 * inner), 0), iota((8, 2 * inner), 1)
    return (((row == 2 * unit) & (col < inner)) | ((row == 2 * unit + 1) & (col >= inner))).astype(f32).astype(bf16)


def norm_kernel(y, g, cot, stat_0, stat_1, stat_2, stat_3, par, out, dy, dg, *, total):
    for i in range(y.shape[0] // chunks_per_step):
        cut = lambda a: a.at[pl.ds(i * chunks_per_step, chunks_per_step)]
        sums = (stat_0[i] + stat_1[i]) + (stat_2[i] + stat_3[i])
        norm_step(cut(y), cut(g), cut(cot), sums, par, cut(out), cut(dy), cut(dg), total=total)


def norm_step(y_i, g_i, cot, sums, par, out_o, dy_o, dg_o, *, total):
    _, seqs, block, inner = y_i.shape
    gain = par[1:2, :]
    mean = sums * (1.0 / total)
    even = lax.rem(iota(mean.shape, 0), 2) == 0
    scales = lax.rsqrt(jnp.where(even, mean, 1.0) + norm_eps)
    before = pltpu.roll(scales, 1, 0)
    stacked = halves(jnp.where(even, scales, before * before * before * mean))
    for u in range(y_i.shape[0] * seqs):
        j, s = u // seqs, u % seqs
        spread = dot_ones(stacked, stat_rows(u, inner), TN)
        scale, pull = spread[:, :inner], spread[:, inner:]
        gate, full = g_i[j, s], y_i[j, s]
        gate_sig = jax.nn.sigmoid(gate)
        gate_silu = gate * gate_sig
        mixed = full * gate_silu
        out_o[j, s] = (mixed * scale * gain).astype(bf16)
        d_mixed = cot[j, s].astype(f32) * gain * scale - mixed * pull
        dy_o[j, s] = d_mixed * gate_silu
        dg_o[j, s] = (d_mixed * full * (gate_sig * (1.0 + gate * (1.0 - gate_sig)))).astype(bf16)


def backward_kernel(core, *refs, width, inner):
    ins, (par, w_main, w_other) = refs[:8], refs[8:11]
    near, far, term_o, give_o, grad_state, next_state, term = refs[11:]
    grad_state[...] = jnp.zeros_like(grad_state)
    next_state[...] = jnp.zeros_like(next_state)
    first = core[0] == 0
    weights = whole_weights(w_main, w_other, first, inner)
    steps = near.shape[0]
    for i in reversed(range(steps)):
        views = [a.at[pl.ds(i * (a.shape[0] // steps), a.shape[0] // steps)] for a in ins + (near, far)]
        added = backward_step(first, *views, par, weights, grad_state, next_state, width=width, inner=inner)
        if i == steps - 1:
            term[...] = added
        else:
            term[...] += added

    wide = 2 * inner
    term_o[:, :wide] = term[:, :wide].astype(bf16)
    term_o[:, wide + lanes :] = term[:, wide + 2 * lanes :].astype(bf16)
    b_part, c_part = term[:, wide : wide + lanes], term[:, wide + lanes : wide + 2 * lanes]
    term_o[:, wide : wide + lanes] = jnp.where(first, b_part, c_part).astype(bf16)
    give_o[...] = jnp.where(first, c_part, b_part).astype(bf16)


def backward_step(
    first_core, xv_i, bc_i, low_i, y_i, st_i, dy_i, dg_i, tok, near_o, far_o, par, weights, grad_state, next_state,
    *, width, inner
):
    per_step, seqs, block, model = tok.shape
    units = [(j, s) for j in range(per_step) for s in range(seqs)]
    count = len(units)
    heads = inner // width
    part = lambda a, u: a[:, u * inner : (u + 1) * inner]
    expander = head_expander(inner, width, count)
    later = iota((block, block), 1) >= iota((block, block), 0)
    upper = (iota((block, block), 1) >= iota((block, block), 0)).astype(f32).astype(bf16)
    skip, rate = beside([par[0:1, :]] * count), par[3:4, :lanes]
    raw, steps, cumul = low_i[0, 0], low_i[0, 1], low_i[0, 2]
    cumul_t = cumul.T
    step_wide, cumul_wide = spread_out(steps, cumul, expander)
    last_wide = cumul_wide[block - 1 : block]
    tail, last_decay = jnp.exp(last_wide - cumul_wide), jnp.exp(last_wide)
    b_two = [halves(bc_i[j, s, :, :lanes]) for j, s in units]
    c_two = [halves(bc_i[j, s, :, lanes:]) for j, s in units]
    scores_t = [dot3(b_two[u], c_two[u], NT) for u in range(count)]
    xv = beside(xv_i[j, s] for j, s in units)
    d_y = beside(dy_i[j, s] for j, s in units)
    sig = jax.nn.sigmoid(xv)
    values = xv * sig
    y = beside(y_i[j, s] for j, s in units) - skip * values
    scaled = values * step_wide
    tailed = scaled * tail
    lifted = halves(d_y * jnp.exp(cumul_wide))
    lifted = [(part(lifted[0], u), part(lifted[1], u)) for u in range(count)]
    updates = [dot3(c_two[u], lifted[u], TN) for u in range(count)]

    back, through, from_state = [None] * count, [None] * count, [None] * count
    for u in reversed(range(count)):
        j, s = units[u]
        grad = grad_state[s]
        grad_two = halves(grad)
        back[u] = dot3(b_two[u], grad_two, NN)
        from_state[u] = dot3(part(tailed, u), grad_two, NT)
        through[u] = jnp.sum(next_state[s] * grad, axis=0, keepdims=True)
        grad_state[s] = part(last_decay, u) * grad + updates[u]
        next_state[s] = st_i[j, s]

    inners, d_scores = [], []
    for u in range(count):
        d_scores_t = jnp.zeros((block, block), f32)
        for pair in range(heads // 2):
            first = u * inner + 2 * pair * width
            cols = slice(first, first + 2 * width)
            products = lax.dot_general(
                pair_halves(scaled[:, cols], block, width).astype(bf16),
                d_y[:, cols].astype(bf16),
                NT,
                preferred_element_type=f32,
            )
            both = []
            for k in range(2):
                h = u * heads + 2 * pair + k
                gap = jnp.where(later, cumul_t[h : h + 1, :] - cumul[:, h : h + 1], -1e30)
                decay = jnp.exp(gap)
                both.append((scores_t[u] * decay).astype(bf16))
                d_scores_t += products[k * block : (k + 1) * block] * decay
            inners.append(
                lax.dot_general(
                    beside(both), pair_halves(d_y[:, cols], block, width).astype(bf16), NN, preferred_element_type=f32
                )
            )
        d_scores.append(halves(d_scores_t))
    d_c = [
        dot3(d_scores[u], b_two[u], TN) + dot3(lifted[u], st_i[j, s], NT) for u, (j, s) in enumerate(units)
    ]
    d_b = [dot3(d_scores[u], c_two[u], NN) + from_state[u] for u in range(count)]
    back = tail * beside(back) + beside(inners)
    last_row = iota((block, count * inner), 0) == block - 1
    products = jnp.concatenate([values * back, d_y * y + jnp.where(last_row, beside(through), 0.0)], axis=0)
    reduced = dot_ones(halves(products), expander, NT)
    d_steps = reduced[:block]
    d_log = ones_dot(upper, halves(reduced[block:] - steps * d_steps))
    d_raw = (d_steps - d_log * rate) * jax.nn.sigmoid(raw)
    d_values = back * step_wide + skip * d_y
    d_xv = (d_values * (sig * (1.0 + xv * (1.0 - sig)))).astype(bf16)
    here = jnp.concatenate(
        [
            beside([part(d_xv, u), dg_i[j, s], d_b[u].astype(bf16), d_c[u].astype(bf16)]
                   + [unpacked(d_raw, u, heads).astype(bf16)])
            for u, (j, s) in enumerate(units)
        ],
        axis=0,
    )
    added = lax.dot_general(tok[...].reshape(count * block, model), here, TN, preferred_element_type=f32)
    partial = lax.dot_general(here, weights, NT, preferred_element_type=f32)
    partial = partial.reshape(per_step, seqs, block, model)
    near_o[0] = jnp.where(first_core, partial[0], partial[1])
    far_o[0] = jnp.where(first_core, partial[1], partial[0]).astype(bf16)
    return added


def join_kernel(_, near, far, term, got, out_0, out_1, out_2, out_3, term_o):
    step = pl.program_id(0)
    both = (near[0, 0] + far[0, 0].astype(f32)).astype(bf16)
    for k, out in enumerate((out_0, out_1, out_2, out_3)):

        @pl.when(step == k)
        def _(out=out):
            out[...] = both

    @pl.when(step == 0)
    def _():
        term_o[...] = (term[...].astype(f32) + got[...].astype(f32)).astype(bf16)


def total_kernel(shares, xz_o, bcdt_o, *, inner, heads, group):
    step = pl.program_id(0)
    half = group * inner

    @pl.when(step == 0)
    def _():
        bcdt_o[...] = jnp.zeros_like(bcdt_o)

    summed = jnp.sum(shares[0, :, 0].astype(f32), axis=(0, 1))
    at = pl.multiple_of(step * inner, inner)
    xz_o[:, pl.ds(at, inner)] = summed[:, :inner]
    xz_o[:, pl.ds(pl.multiple_of(half + at, inner), inner)] = summed[:, inner : 2 * inner]
    core = lax.rem(lax.div(step, 2), 2)
    bc = summed[:, 2 * inner : 2 * inner + lanes]
    bcdt_o[:, :lanes] += jnp.where(core == 0, bc, 0.0)
    bcdt_o[:, lanes : 2 * lanes] += jnp.where(core == 0, 0.0, bc)
    steps = summed[:, 2 * inner + lanes :]
    lane = iota(steps.shape, 1)
    moved = pltpu.roll(jnp.where(lane < heads, steps, 0.0), step * heads, 1)
    bcdt_o[:, 2 * lanes :] += moved[:, : group * heads]


def cost(micros):
    return pl.CostEstimate(flops=int(micros * 1.1e9), bytes_accessed=int(micros * 3.5e6), transcendentals=0)


def chunk_spec(shape, count=None, per_step=1):
    blank = (0,) * (len(shape) - 1)
    if count is None:
        return pl.BlockSpec((per_step,) + shape[1:], lambda i: (i,) + blank)
    return pl.BlockSpec((per_step,) + shape[1:], lambda i: (count - 1 - i,) + blank)


def fixed_spec(shape):
    return pl.BlockSpec(shape, lambda i: (0,) * len(shape))


chunks_per_step = 2
smem_spec = pl.BlockSpec(memory_space=pltpu.SMEM)
vmem_spec = pl.BlockSpec(memory_space=pltpu.VMEM)
HBM = pltpu.HBM


def pack_call(place, tokens, cot, w_xz, w_bcdt, sides, group, heads):
    block, total = cot.shape
    inner = total // group
    states = (w_bcdt.shape[1] - heads * group) // 2
    copies = sides + (w_xz.shape[0], 2 * inner + states + lanes)
    piece = (block, tokens.shape[1] + 2 * inner)

    def kernel(*refs):
        pack_kernel(*refs, inner=inner, heads=heads, states=states)

    return pl.pallas_call(
        kernel,
        in_specs=[pl.BlockSpec(memory_space=pltpu.SMEM)] + [pl.BlockSpec(memory_space=pltpu.VMEM)] * 4,
        out_specs=[pl.BlockSpec(memory_space=pltpu.VMEM)] * 5,
        out_shape=[HBM(piece, bf16)] * 4 + [HBM(copies, bf16)],
        compiler_params=pltpu.CompilerParams(vmem_limit_bytes=wide_vmem),
        cost_estimate=cost(2),
        name="pack_pieces",
    )(place, tokens, cot, w_xz, w_bcdt)


def forward_call(place, own, far, weights, w_other, par, width):
    _, block, columns = own.shape
    model = weights.shape[0]
    inner = columns - model
    chunks, seqs = 4, 2
    steps = chunks // chunks_per_step
    wide = (chunks, seqs, block, inner)

    outs = [
        ((chunks, seqs, block, model), bf16),
        (wide, bf16),
        (wide, f32),
        (wide, f32),
        ((chunks, seqs, block, 2 * lanes), f32),
        ((steps, 3, block, lanes), f32),
        (wide, f32),
        ((chunks, seqs, lanes, inner), f32),
        ((steps, 8, block), f32),
    ]

    def kernel(*refs):
        forward_kernel(*refs, width=width, inner=inner)

    return pl.pallas_call(
        kernel,
        in_specs=[smem_spec] + [vmem_spec] * 5,
        out_specs=[vmem_spec] * len(outs),
        out_shape=[jax.ShapeDtypeStruct(a, kind) for a, kind in outs],
        scratch_shapes=[pltpu.VMEM((seqs, lanes, inner), f32)],
        compiler_params=pltpu.CompilerParams(vmem_limit_bytes=vmem),
        cost_estimate=cost(12),
        name="forward_scan",
    )(place, own, far, weights, w_other, par)


def norm_call(y, gate, cot, stats, par, total):
    def kernel(*refs):
        norm_kernel(*refs, total=total)

    return pl.pallas_call(
        kernel,
        in_specs=[vmem_spec] * 8,
        out_specs=[vmem_spec] * 3,
        out_shape=[HBM(y.shape, bf16), jax.ShapeDtypeStruct(y.shape, f32), jax.ShapeDtypeStruct(y.shape, bf16)],
        compiler_params=pltpu.CompilerParams(vmem_limit_bytes=vmem),
        cost_estimate=cost(5),
        name="gated_norm",
    )(y, gate, cot, *stats, par)


def backward_call(core, xv, bc, low, y, states, d_y, d_gate, tok, par, weights, w_other, width):
    chunks, seqs, block, inner = xv.shape
    model, columns = weights.shape
    columns = columns + lanes
    steps = chunks // chunks_per_step
    half = (steps, seqs, block, model)

    def kernel(*refs):
        backward_kernel(*refs, width=width, inner=inner)

    return pl.pallas_call(
        kernel,
        in_specs=[smem_spec] + [vmem_spec] * 11,
        out_specs=[vmem_spec] * 4,
        out_shape=[
            HBM(half, f32),
            HBM(half, bf16),
            HBM((model, columns - lanes), bf16),
            HBM((model, lanes), bf16),
        ],
        scratch_shapes=[
            pltpu.VMEM((seqs, lanes, inner), f32),
            pltpu.VMEM((seqs, lanes, inner), f32),
            pltpu.VMEM((model, columns), f32),
        ],
        compiler_params=pltpu.CompilerParams(vmem_limit_bytes=vmem),
        cost_estimate=cost(20),
        name="backward_scan",
    )(core, xv, bc, low, y, states, d_y, d_gate, tok, par, weights, w_other)


def join_call(here, near, far, term, got, inner):
    halves_of, seqs, block, model = near.shape
    count = halves_of * seqs
    bc_spec = pl.BlockSpec((term.shape[0], lanes), lambda k, here: (0, 2 * inner // lanes))

    def place(k, here):
        y = lax.bitwise_xor(here[0], k)
        return (lax.rem(y, 2), lax.div(y, 2), 0, 0)

    spec = pl.BlockSpec((1, 1, block, model), place)
    return pl.pallas_call(
        join_kernel,
        grid_spec=pltpu.PrefetchScalarGridSpec(
            num_scalar_prefetch=1,
            grid=(count,),
            in_specs=[spec, spec, bc_spec, pl.BlockSpec(got.shape, lambda k, here: (0, 0))],
            out_specs=[pl.BlockSpec((block, model), lambda k, here: (0, 0))] * count + [bc_spec],
        ),
        out_shape=[HBM((block, model), bf16)] * count + [HBM(term.shape, bf16)],
        input_output_aliases={3: count},
        compiler_params=pltpu.CompilerParams(vmem_limit_bytes=wide_vmem),
        cost_estimate=cost(3),
        name="join_halves",
    )(here, near, far, term, got)


def total_call(shares, inner, heads):
    times, far, seqs, near, rows, columns = shares.shape
    group = times * seqs
    shapes = [(rows, 2 * group * inner), (rows, 2 * lanes + group * heads)]

    def kernel(*refs):
        total_kernel(*refs, inner=inner, heads=heads, group=group)

    return pl.pallas_call(
        kernel,
        grid=(group,),
        in_specs=[pl.BlockSpec((1, far, 1, near, rows, columns), lambda i: (i // seqs, 0, i % seqs, 0, 0, 0))],
        out_specs=[fixed_spec(a) for a in shapes],
        out_shape=[jax.ShapeDtypeStruct(a, f32) for a in shapes],
        compiler_params=pltpu.CompilerParams(vmem_limit_bytes=vmem),
        cost_estimate=cost(2),
        name="total_shares",
    )(shares)


def partner(a):
    return lax.ppermute(a, "core", [(0, 1), (1, 0)])


def around(give):
    came = [give(0)]
    spot = lambda chip: (chip % 2) * 2 + chip // 2
    for k in (1, 2, 3):
        came.append(lax.ppermute(give(k), ("yl", "xl"), [(spot(chip), spot(chip ^ k)) for chip in range(4)]))
    return came


def stack_kernel(place, a, b, c, d, own_o, give_o):
    inner = own_o.shape[2] // 5
    model = 4 * inner
    for k, came in enumerate((a, b, c, d)):
        tokens = came[:, :model]
        one, two = came[:, model : model + inner], came[:, model + inner :]
        first = place[1] == 0
        own_o[k] = jnp.concatenate([tokens, jnp.where(first, one, two)], axis=1)
        give_o[k] = jnp.concatenate([tokens, jnp.where(first, two, one)], axis=1)


def stack_call(place, came):
    block, columns = came[0].shape
    stacked = (4, block, columns // 6 * 5)
    return pl.pallas_call(
        stack_kernel,
        in_specs=[pl.BlockSpec(memory_space=pltpu.SMEM)] + [pl.BlockSpec(memory_space=pltpu.VMEM)] * 4,
        out_specs=[pl.BlockSpec(memory_space=pltpu.VMEM)] * 2,
        out_shape=[HBM(stacked, bf16), HBM(stacked, bf16)],
        compiler_params=pltpu.CompilerParams(vmem_limit_bytes=wide_vmem),
        cost_estimate=cost(stack_cost),
        name="stack_pieces",
    )(place, *came)


def sum_kernel(a, b, c, d, heads, out, layer_o):
    out[...] = ((a[...].astype(f32) + b[...].astype(f32)) + (c[...].astype(f32) + d[...].astype(f32))).astype(bf16)
    inner = heads.shape[2]
    for k in range(heads.shape[0]):
        layer_o[:, k * inner : (k + 1) * inner] = heads[k]


def sum_call(arrays, heads):
    group, block, inner = heads.shape
    return pl.pallas_call(
        sum_kernel,
        out_shape=[
            jax.ShapeDtypeStruct(arrays[0].shape, bf16),
            jax.ShapeDtypeStruct((block, group * inner), bf16),
        ],
        compiler_params=pltpu.CompilerParams(vmem_limit_bytes=wide_vmem),
        cost_estimate=cost(sum_cost),
        name="sum_pieces",
    )(*arrays, heads)


def body(tokens, cotangent, w_xz, w_bcdt, rate, dt_bias, skip, gain):
    group = lax.axis_size(group_axes)
    devices = lax.axis_size(whole)
    mine = lax.axis_index(group_axes)
    chunks = lax.axis_size("yl") * lax.axis_size("core")
    seqs = group // chunks
    owners = lax.axis_size(rows_axes)
    block, model = tokens.shape[1:]
    total = cotangent.shape[2]
    inner = total // group
    heads = rate.shape[0] // group
    width = inner // heads
    states = (w_bcdt.shape[1] - rate.shape[0]) // 2

    core = lax.axis_index("core")
    here = lax.axis_index(("xl", "yl"))
    place = jnp.stack([here, core, lax.axis_index("yl") + lax.axis_index("yh")]).astype(jnp.int32)
    sides = tuple(lax.axis_size(name) for name in rows_axes)
    *pieces, copies = pack_call(place, tokens[0], cotangent[0], w_xz, w_bcdt, sides, group, heads)
    copies = copies.reshape((owners,) + copies.shape[4:])

    own_came, give_came = stack_call(place, around(lambda shift: pieces[shift]))
    far_came = partner(give_came)

    rest = owners // sides[0]
    traders = [
        [(((start + k) % 2) * sides[0] + k) * rest + i for k in range(sides[0]) for i in range(rest)]
        for start in range(2)
    ]
    weights = lax.all_to_all(copies, ("yl",) + rows_axes, 0, 0, axis_index_groups=traders, tiled=True)
    weights = weights.reshape(model, -1)
    w_other = partner(weights[:, 2 * inner : 2 * inner + lanes])

    own = lambda a: lax.dynamic_slice_in_dim(a, mine * heads, heads, 0)
    padded = lambda a: jnp.pad(jnp.tile(own(a), lanes // heads), (0, inner - lanes))
    par = jnp.stack(
        [jnp.repeat(own(skip), width), lax.dynamic_slice_in_dim(gain, mine * inner, inner, 0)]
        + [padded(dt_bias), padded(rate)]
        + [jnp.zeros((inner,), f32)] * 4
    )
    tok, cot, xv, gate, bc, low, y, chunk_states, stats = forward_call(
        place, own_came, far_came, weights, w_other, par, width
    )
    stats = stats + partner(stats)
    stats = around(lambda shift: stats)
    out, d_y, d_gate = norm_call(y, gate, cot, stats, par, float(total))
    layer_out = lax.all_to_all(out.reshape(group, block, inner), group_axes, 0, 0, tiled=True)
    scalar = lambda a: jnp.full((1,), a, jnp.int32)
    near, far, term, give = backward_call(
        scalar(core), xv, bc, low, y, chunk_states, d_y, d_gate, tok, par, weights, w_other, width
    )
    *sums, term = join_call(scalar(here), near, partner(far), term, partner(give), inner)
    shares = lax.all_to_all(term.reshape(devices, model // devices, -1), whole, 0, 0, tiled=True)
    came = around(lambda shift: sums[shift])
    grad_input, layer_out = sum_call(came, layer_out)
    grad_xz, grad_bcdt = total_call(
        shares.reshape(chunks, -1, seqs, lax.axis_size("z"), model // devices, shares.shape[-1]), inner, heads
    )
    return (layer_out[None], grad_input[None], grad_xz, grad_bcdt)


def solution(mesh):
    split = Mesh(mesh.devices.reshape(2, 2, 2, 2, 2, 4), whole)
    ctx, fsdp = ("yl", "core"), rows_axes
    placed = (P(fsdp, ctx, None), P(fsdp, ctx, None), P(fsdp, None), P(fsdp, None), P(), P(), P(), P())
    return jax.shard_map(
        body,
        mesh=split,
        in_specs=placed,
        out_specs=(P(fsdp, ctx, None), P(fsdp, ctx, None), P(ctx + fsdp, None), P(ctx + fsdp)),
        check_vma=False,
    )
```

```python
import jax
import jax.numpy as jnp
from jax import lax
from jax.experimental import pallas as pl
from jax.experimental.pallas import tpu as pltpu
from jax.sharding import Mesh, PartitionSpec as P

f32 = jnp.float32
bf16 = jnp.bfloat16
norm_eps = 1e-05
lanes = 128
NN = (((1,), (0,)), ((), ()))
NT = (((1,), (1,)), ((), ()))
TN = (((0,), (0,)), ((), ()))

whole = ("yl", "core", "yh", "xh", "xl", "z")
rows_axes = ("yh", "xh", "xl", "z")
group_axes = ("yl", "core", "xl")
vmem = 32 * 2**20
wide_vmem = 60 * 2**20
stack_cost, sum_cost = 12, 24


def dot1(a, b, dims):
    return lax.dot_general(a.astype(bf16), b.astype(bf16), dims, preferred_element_type=f32)


def halves(a):
    high = a.astype(bf16)
    return (high, (a - high.astype(f32)).astype(bf16))


def dot3(a, b, dims):
    a_high, a_low = a if isinstance(a, tuple) else halves(a)
    b_high, b_low = b if isinstance(b, tuple) else halves(b)
    dot = lambda left, right: lax.dot_general(left, right, dims, preferred_element_type=f32)
    (ca,), (cb,) = dims[0]
    both = dot(jnp.concatenate([a_high, a_low], axis=ca), jnp.concatenate([b_high, b_high], axis=cb))
    return both + dot(a_high, b_low)


def thirds(a):
    high = a.astype(bf16)
    rest = a - high.astype(f32)
    mid = rest.astype(bf16)
    return (high, mid, (rest - mid.astype(f32)).astype(bf16))


def dot_ones(pieces, ones, dims):
    first, *rest = [lax.dot_general(a, ones, dims, preferred_element_type=f32) for a in pieces]
    return first + sum(rest[1:], rest[0])


def spread_out(steps, cumul, expander):
    block = steps.shape[0]
    (s_high, s_low), (c_high, c_mid, c_low) = halves(steps), thirds(cumul)
    stacked = jnp.concatenate([s_high, s_low, c_high, c_mid, c_low], axis=0)
    wide = lax.dot_general(stacked, expander, NN, preferred_element_type=f32)
    at = lambda k: wide[k * block : (k + 1) * block]
    return at(0) + at(1), at(2) + (at(3) + at(4))


def iota(shape, axis):
    return lax.broadcasted_iota(jnp.int32, shape, axis)


def head_expander(inner, width, units):
    shape = (lanes, units * inner)
    start = iota(shape, 0) * width
    col = iota(shape, 1)
    return ((col >= start) & (col < start + width)).astype(f32).astype(bf16)


def packed(parts, heads):
    keep = iota(parts[0].shape, 1) < heads
    kept = [jnp.where(keep, a, 0.0) for a in parts]
    return sum(a if u == 0 else pltpu.roll(a, u * heads, 1) for u, a in enumerate(kept))


def unpacked(a, unit, heads):
    moved = a if unit == 0 else pltpu.roll(a, lanes - unit * heads, 1)
    return jnp.where(iota(a.shape, 1) < heads, moved, 0.0)


def beside(parts):
    return jnp.concatenate(list(parts), axis=1)


def lower_ones(block):
    shape = (block, block)
    return (iota(shape, 0) >= iota(shape, 1)).astype(f32).astype(bf16)


def ones_dot(ones, pieces):
    width = pieces[0].shape[1]
    wide = lax.dot_general(ones, jnp.concatenate(pieces, axis=1), NN, preferred_element_type=f32)
    parts = [wide[:, k * width : (k + 1) * width] for k in range(len(pieces))]
    return parts[0] + sum(parts[2:], parts[1])


def softplus(a):
    return jnp.maximum(a, 0.0) + jnp.log1p(jnp.exp(-jnp.abs(a)))


def pair_halves(a, block, width):
    left = iota(a.shape, 1) < width
    zero = jnp.zeros_like(a)
    return jnp.concatenate([jnp.where(left, a, zero), jnp.where(left, zero, a)], axis=0)


def pack_kernel(tokens, cot, w_xz, w_bcdt, out_0, out_1, out_2, out_3, copies, *, inner, heads, states):
    yl = lax.axis_index("yl")
    place = (lax.axis_index("xl") * 2 + yl, lax.axis_index("core"), yl + lax.axis_index("yh"))
    cols = lambda block, count=1: pl.ds(pl.multiple_of(block * inner, inner), count * inner)
    mine = tokens[...]
    for k, out in enumerate((out_0, out_1, out_2, out_3)):
        chip = lax.bitwise_xor(place[0], k)
        first = lax.rem(chip, 2) * 4 + lax.div(chip, 2)
        out[...] = jnp.concatenate([mine, cot[:, cols(first)], cot[:, cols(first + 2)]], axis=1)

    low = w_bcdt[...].astype(f32)
    rows = low.shape[0]
    filled = jnp.zeros((rows, 2 * lanes - (low.shape[1] - 2 * states)), f32)
    all_steps = jnp.concatenate([low[:, 2 * states :], filled], axis=1)
    half = jnp.where(place[1] == 0, low[:, :states], low[:, states : 2 * states]).astype(bf16)
    group = w_xz.shape[1] // (2 * inner)
    yh, xh, xl, z = copies.shape[:4]
    for side in range(yh):
        for s in range(xl):
            target = (lax.rem(place[2] + side, 2) * 2 + place[1]) * 2 + s
            steps = pltpu.roll(all_steps, 2 * lanes - target * heads, 1)[:, :lanes]
            steps = jnp.where(iota(steps.shape, 1) < heads, steps, 0.0).astype(bf16)
            row = jnp.concatenate([w_xz[:, cols(target)], w_xz[:, cols(group + target)], half, steps], axis=1)
            for upper in range(xh):
                copies[side, upper, s] = jnp.broadcast_to(row[None], (z,) + row.shape)


def whole_weights(main, other, first, inner):
    half, got = main[:, 2 * inner : 2 * inner + lanes], other[...]
    b_part, c_part = jnp.where(first, half, got), jnp.where(first, got, half)
    return jnp.concatenate([main[:, : 2 * inner], b_part, c_part, main[:, 2 * inner + lanes :]], axis=1)


def forward_kernel(place, own, far, w_main, w_other, par, *rest, width, inner):
    *outs, state = rest
    first = place[1] == 0
    weights = whole_weights(w_main, w_other, first, inner)
    state[...] = jnp.zeros_like(state)
    steps = outs[0].shape[0] // chunks_per_step
    for i in range(steps):
        came = [
            [a[lax.bitwise_xor(place[0], 2 * s + i)] for a in (own, far)] for s in range(outs[0].shape[1])
        ]
        views = [a.at[pl.ds(i * (a.shape[0] // steps), a.shape[0] // steps)] for a in outs]
        forward_step(first, came, weights, par, *views, state, width=width, inner=inner)


def forward_step(
    first, came, weights, par, tok, cot, xv_o, g_o, bc_o, low_o, y_o, st_o, stat_o, state, *, width, inner
):
    per_step, seqs, block, model = tok.shape
    units = [(j, s) for j in range(per_step) for s in range(seqs)]
    for s, (own, far) in enumerate(came):
        one, two = jnp.where(first, own, far), jnp.where(first, far, own)
        tok[0, s], tok[1, s] = one[:, :model], two[:, :model]
        cot[0, s], cot[1, s] = one[:, model:], two[:, model:]
    count = len(units)
    heads = inner // width

    proj = lax.dot_general(tok[...].reshape(count * block, -1), weights, NN, preferred_element_type=f32)
    cut = lambda u, first, size: proj[u * block : (u + 1) * block, first : first + size]
    part = lambda a, u: a[:, u * inner : (u + 1) * inner]
    expander = head_expander(inner, width, count)
    causal = iota((block, block), 0) >= iota((block, block), 1)
    skip, gain = beside([par[0:1, :]] * count), beside([par[1:2, :]] * count)
    bias, rate = par[2:3, :lanes], par[3:4, :lanes]

    raw = packed([cut(u, 2 * inner + 2 * lanes, lanes) for u in range(count)], heads) + bias
    steps = softplus(raw)
    cumul = ones_dot(lower_ones(block), thirds(-steps * rate))
    cumul_t = cumul.T
    low_o[0, 0], low_o[0, 1], low_o[0, 2] = raw, steps, cumul
    b_two, c_two = [], []
    for u, (j, s) in enumerate(units):
        b_in, c_out = cut(u, 2 * inner, lanes), cut(u, 2 * inner + lanes, lanes)
        bc_o[j, s] = beside([b_in, c_out])
        xv_o[j, s] = cut(u, 0, inner)
        g_o[j, s] = cut(u, inner, inner)
        b_two.append(halves(b_in))
        c_two.append(halves(c_out))
    scores = [dot3(c_two[u], b_two[u], NT) for u in range(count)]
    step_wide, cumul_wide = spread_out(steps, cumul, expander)
    last_wide = cumul_wide[block - 1 : block]
    xv = beside(cut(u, 0, inner) for u in range(count))
    gate = beside(cut(u, inner, inner) for u in range(count))
    values = xv * jax.nn.sigmoid(xv)
    scaled = values * step_wide
    tailed = scaled * jnp.exp(last_wide - cumul_wide)
    last_decay = jnp.exp(last_wide)
    updates = [dot3(b_two[u], part(tailed, u), TN) for u in range(count)]
    inners = []
    for u in range(count):
        for pair in range(heads // 2):
            both = []
            for h in (u * heads + 2 * pair, u * heads + 2 * pair + 1):
                gap = jnp.where(causal, cumul[:, h : h + 1] - cumul_t[h : h + 1, :], -1e30)
                both.append((scores[u] * jnp.exp(gap)).astype(bf16))
            first = u * inner + 2 * pair * width
            cols = scaled[:, first : first + 2 * width]
            inners.append(
                lax.dot_general(
                    beside(both), pair_halves(cols, block, width).astype(bf16), NN, preferred_element_type=f32
                )
            )
    carried = []
    for u, (j, s) in enumerate(units):
        old = state[s]
        st_o[j, s] = old
        carried.append(dot3(c_two[u], old, NN))
        state[s] = part(last_decay, u) * old + updates[u]
    y = jnp.exp(cumul_wide) * beside(carried) + beside(inners) + skip * values
    mixed = y * (gate * jax.nn.sigmoid(gate))
    weighted = beside(cot[j, s] for j, s in units).astype(f32) * gain * mixed
    squared = mixed * mixed
    sums = []
    for u, (j, s) in enumerate(units):
        y_o[j, s] = part(y, u)
        high, low = halves(beside([part(squared, u), part(weighted, u)]))
        dot = lambda right: lax.dot_general(stat_rows(u, inner), right, NT, preferred_element_type=f32)
        sums.append(dot(high) + dot(low))
    stat_o[0] = (sums[0] + sums[1]) + (sums[2] + sums[3])


def stat_rows(unit, inner):
    row, col = iota((8, 2 * inner), 0), iota((8, 2 * inner), 1)
    return (((row == 2 * unit) & (col < inner)) | ((row == 2 * unit + 1) & (col >= inner))).astype(f32).astype(bf16)


def norm_step(y_i, g_i, cot, sums, par, out_o, *, total):
    _, seqs, block, inner = y_i.shape
    gain = par[1:2, :]
    mean = sums * (1.0 / total)
    even = lax.rem(iota(mean.shape, 0), 2) == 0
    scales = lax.rsqrt(jnp.where(even, mean, 1.0) + norm_eps)
    before = pltpu.roll(scales, 1, 0)
    stacked = halves(jnp.where(even, scales, before * before * before * mean))
    d_y, d_gate = [], []
    for u in range(y_i.shape[0] * seqs):
        j, s = u // seqs, u % seqs
        spread = dot_ones(stacked, stat_rows(u, inner), TN)
        scale, pull = spread[:, :inner], spread[:, inner:]
        gate, full = g_i[j, s], y_i[j, s]
        gate_sig = jax.nn.sigmoid(gate)
        gate_silu = gate * gate_sig
        mixed = full * gate_silu
        out_o[j, s] = (mixed * scale * gain).astype(bf16)
        d_mixed = cot[j, s].astype(f32) * gain * scale - mixed * pull
        d_y.append(d_mixed * gate_silu)
        d_gate.append((d_mixed * full * (gate_sig * (1.0 + gate * (1.0 - gate_sig)))).astype(bf16))
    return beside(d_y), d_gate


def backward_kernel(core, *refs, width, inner, total):
    ins, stats, (par, w_main, w_other) = refs[:8], refs[8:12], refs[12:15]
    out, near, far, term_o, give_o, grad_state, next_state, here_all = refs[15:]
    grad_state[...] = jnp.zeros_like(grad_state)
    next_state[...] = jnp.zeros_like(next_state)
    first = core[0] == 0
    weights = whole_weights(w_main, w_other, first, inner)
    steps = near.shape[0]
    for i in reversed(range(steps)):
        views = [a.at[pl.ds(i * (a.shape[0] // steps), a.shape[0] // steps)] for a in ins + (out, near, far)]
        sums = (stats[0][i] + stats[1][i]) + (stats[2][i] + stats[3][i])
        added = backward_step(
            first, *views, sums, par, weights, grad_state, next_state, width=width, inner=inner, total=total
        )
        rows = added.shape[0]
        here_all[i * rows : (i + 1) * rows, :] = added
    tok = ins[7]
    term = lax.dot_general(tok[...].reshape(steps * rows, -1), here_all[...], TN, preferred_element_type=f32)

    wide = 2 * inner
    term_o[:, :wide] = term[:, :wide].astype(bf16)
    term_o[:, wide + lanes :] = term[:, wide + 2 * lanes :].astype(bf16)
    b_part, c_part = term[:, wide : wide + lanes], term[:, wide + lanes : wide + 2 * lanes]
    term_o[:, wide : wide + lanes] = jnp.where(first, b_part, c_part).astype(bf16)
    give_o[...] = jnp.where(first, c_part, b_part).astype(bf16)


def backward_step(
    first_core, xv_i, g_i, bc_i, low_i, y_i, st_i, cot, tok, out_o, near_o, far_o, sums, par, weights,
    grad_state, next_state, *, width, inner, total
):
    per_step, seqs, block, model = tok.shape
    units = [(j, s) for j in range(per_step) for s in range(seqs)]
    count = len(units)
    heads = inner // width
    part = lambda a, u: a[:, u * inner : (u + 1) * inner]
    expander = head_expander(inner, width, count)
    later = iota((block, block), 1) >= iota((block, block), 0)
    upper = (iota((block, block), 1) >= iota((block, block), 0)).astype(f32).astype(bf16)
    skip, rate = beside([par[0:1, :]] * count), par[3:4, :lanes]
    raw, steps, cumul = low_i[0, 0], low_i[0, 1], low_i[0, 2]
    cumul_t = cumul.T
    step_wide, cumul_wide = spread_out(steps, cumul, expander)
    last_wide = cumul_wide[block - 1 : block]
    tail, last_decay = jnp.exp(last_wide - cumul_wide), jnp.exp(last_wide)
    b_two = [halves(bc_i[j, s, :, :lanes]) for j, s in units]
    c_two = [halves(bc_i[j, s, :, lanes:]) for j, s in units]
    scores_t = [dot3(b_two[u], c_two[u], NT) for u in range(count)]
    xv = beside(xv_i[j, s] for j, s in units)
    d_y, d_gate = norm_step(y_i, g_i, cot, sums, par, out_o, total=total)
    sig = jax.nn.sigmoid(xv)
    values = xv * sig
    y = beside(y_i[j, s] for j, s in units) - skip * values
    scaled = values * step_wide
    tailed = scaled * tail
    lifted = halves(d_y * jnp.exp(cumul_wide))
    lifted = [(part(lifted[0], u), part(lifted[1], u)) for u in range(count)]
    updates = [dot3(c_two[u], lifted[u], TN) for u in range(count)]

    back, through, from_state = [None] * count, [None] * count, [None] * count
    for u in reversed(range(count)):
        j, s = units[u]
        grad = grad_state[s]
        grad_two = halves(grad)
        back[u] = dot3(b_two[u], grad_two, NN)
        from_state[u] = dot3(part(tailed, u), grad_two, NT)
        through[u] = jnp.sum(next_state[s] * grad, axis=0, keepdims=True)
        grad_state[s] = part(last_decay, u) * grad + updates[u]
        next_state[s] = st_i[j, s]

    inners, d_scores = [], []
    for u in range(count):
        d_scores_t = jnp.zeros((block, block), f32)
        for pair in range(heads // 2):
            first = u * inner + 2 * pair * width
            cols = slice(first, first + 2 * width)
            products = lax.dot_general(
                pair_halves(scaled[:, cols], block, width).astype(bf16),
                d_y[:, cols].astype(bf16),
                NT,
                preferred_element_type=f32,
            )
            both = []
            for k in range(2):
                h = u * heads + 2 * pair + k
                gap = jnp.where(later, cumul_t[h : h + 1, :] - cumul[:, h : h + 1], -1e30)
                decay = jnp.exp(gap)
                both.append((scores_t[u] * decay).astype(bf16))
                d_scores_t += products[k * block : (k + 1) * block] * decay
            inners.append(
                lax.dot_general(
                    beside(both), pair_halves(d_y[:, cols], block, width).astype(bf16), NN, preferred_element_type=f32
                )
            )
        d_scores.append(halves(d_scores_t))
    d_c = [
        dot3(d_scores[u], b_two[u], TN) + dot3(lifted[u], st_i[j, s], NT) for u, (j, s) in enumerate(units)
    ]
    d_b = [dot3(d_scores[u], c_two[u], NN) + from_state[u] for u in range(count)]
    back = tail * beside(back) + beside(inners)
    last_row = iota((block, count * inner), 0) == block - 1
    products = jnp.concatenate([values * back, d_y * y + jnp.where(last_row, beside(through), 0.0)], axis=0)
    reduced = dot_ones(halves(products), expander, NT)
    d_steps = reduced[:block]
    d_log = ones_dot(upper, halves(reduced[block:] - steps * d_steps))
    d_raw = (d_steps - d_log * rate) * jax.nn.sigmoid(raw)
    d_values = back * step_wide + skip * d_y
    d_xv = (d_values * (sig * (1.0 + xv * (1.0 - sig)))).astype(bf16)
    here = jnp.concatenate(
        [
            beside([part(d_xv, u), d_gate[u], d_b[u].astype(bf16), d_c[u].astype(bf16)]
                   + [unpacked(d_raw, u, heads).astype(bf16)])
            for u, (j, s) in enumerate(units)
        ],
        axis=0,
    )
    partial = lax.dot_general(here, weights, NT, preferred_element_type=f32)
    partial = partial.reshape(per_step, seqs, block, model)
    near_o[0] = jnp.where(first_core, partial[0], partial[1])
    far_o[0] = jnp.where(first_core, partial[1], partial[0]).astype(bf16)
    return here


def join_kernel(place, near, far, term, got, out_0, out_1, out_2, out_3, term_o):
    for k, out in enumerate((out_0, out_1, out_2, out_3)):
        chip = lax.bitwise_xor(place[0], k)
        yl, xl = lax.rem(chip, 2), lax.div(chip, 2)
        out[...] = (near[yl, xl] + far[yl, xl].astype(f32)).astype(bf16)
    term_o[...] = (term[...].astype(f32) + got[...].astype(f32)).astype(bf16)


def total_kernel(shares, xz_o, bcdt_o, *, inner, heads, group):
    step = pl.program_id(0)
    half = group * inner

    @pl.when(step == 0)
    def _():
        bcdt_o[...] = jnp.zeros_like(bcdt_o)

    summed = jnp.sum(shares[0, :, 0].astype(f32), axis=(0, 1))
    at = pl.multiple_of(step * inner, inner)
    xz_o[:, pl.ds(at, inner)] = summed[:, :inner]
    xz_o[:, pl.ds(pl.multiple_of(half + at, inner), inner)] = summed[:, inner : 2 * inner]
    core = lax.rem(lax.div(step, 2), 2)
    bc = summed[:, 2 * inner : 2 * inner + lanes]
    bcdt_o[:, :lanes] += jnp.where(core == 0, bc, 0.0)
    bcdt_o[:, lanes : 2 * lanes] += jnp.where(core == 0, 0.0, bc)
    steps = summed[:, 2 * inner + lanes :]
    lane = iota(steps.shape, 1)
    moved = pltpu.roll(jnp.where(lane < heads, steps, 0.0), step * heads, 1)
    bcdt_o[:, 2 * lanes :] += moved[:, : group * heads]


def cost(micros):
    return pl.CostEstimate(flops=int(micros * 1.1e9), bytes_accessed=int(micros * 3.5e6), transcendentals=0)


def chunk_spec(shape, count=None, per_step=1):
    blank = (0,) * (len(shape) - 1)
    if count is None:
        return pl.BlockSpec((per_step,) + shape[1:], lambda i: (i,) + blank)
    return pl.BlockSpec((per_step,) + shape[1:], lambda i: (count - 1 - i,) + blank)


def fixed_spec(shape):
    return pl.BlockSpec(shape, lambda i: (0,) * len(shape))


chunks_per_step = 2
smem_spec = pl.BlockSpec(memory_space=pltpu.SMEM)
vmem_spec = pl.BlockSpec(memory_space=pltpu.VMEM)
HBM = pltpu.HBM


def pack_call(tokens, cot, w_xz, w_bcdt, sides, group, heads):
    block, total = cot.shape
    inner = total // group
    states = (w_bcdt.shape[1] - heads * group) // 2
    copies = sides + (w_xz.shape[0], 2 * inner + states + lanes)
    piece = (block, tokens.shape[1] + 2 * inner)

    def kernel(*refs):
        pack_kernel(*refs, inner=inner, heads=heads, states=states)

    return pl.pallas_call(
        kernel,
        in_specs=[vmem_spec] * 4,
        out_specs=[vmem_spec] * 5,
        out_shape=[HBM(piece, bf16)] * 4 + [HBM(copies, bf16)],
        compiler_params=pltpu.CompilerParams(vmem_limit_bytes=wide_vmem),
        cost_estimate=cost(2),
        name="pack_pieces",
    )(tokens, cot, w_xz, w_bcdt)


def forward_call(place, own, far, weights, w_other, par, width):
    _, block, columns = own.shape
    model = weights.shape[0]
    inner = columns - model
    chunks, seqs = 4, 2
    steps = chunks // chunks_per_step
    wide = (chunks, seqs, block, inner)

    outs = [
        ((chunks, seqs, block, model), bf16),
        (wide, bf16),
        (wide, f32),
        (wide, f32),
        ((chunks, seqs, block, 2 * lanes), f32),
        ((steps, 3, block, lanes), f32),
        (wide, f32),
        ((chunks, seqs, lanes, inner), f32),
        ((steps, 8, block), f32),
    ]

    def kernel(*refs):
        forward_kernel(*refs, width=width, inner=inner)

    return pl.pallas_call(
        kernel,
        in_specs=[smem_spec] + [vmem_spec] * 5,
        out_specs=[vmem_spec] * len(outs),
        out_shape=[jax.ShapeDtypeStruct(a, kind) for a, kind in outs],
        scratch_shapes=[pltpu.VMEM((seqs, lanes, inner), f32)],
        compiler_params=pltpu.CompilerParams(vmem_limit_bytes=vmem),
        cost_estimate=cost(12),
        name="forward_scan",
    )(place, own, far, weights, w_other, par)


def backward_call(core, scanned, stats, par, weights, w_other, width, total):
    xv = scanned[0]
    chunks, seqs, block, inner = xv.shape
    model, columns = weights.shape
    columns = columns + lanes
    half = (chunks // chunks_per_step, seqs, block, model)

    def kernel(*refs):
        backward_kernel(*refs, width=width, inner=inner, total=total)

    return pl.pallas_call(
        kernel,
        in_specs=[smem_spec] + [vmem_spec] * 15,
        out_specs=[vmem_spec] * 5,
        out_shape=[
            HBM(xv.shape, bf16),
            HBM(half, f32),
            HBM(half, bf16),
            HBM((model, columns - lanes), bf16),
            HBM((model, lanes), bf16),
        ],
        scratch_shapes=[
            pltpu.VMEM((seqs, lanes, inner), f32),
            pltpu.VMEM((seqs, lanes, inner), f32),
            pltpu.VMEM((chunks * seqs * block, columns), bf16),
        ],
        compiler_params=pltpu.CompilerParams(vmem_limit_bytes=vmem),
        cost_estimate=cost(20),
        name="backward_scan",
    )(core, *scanned, *stats, par, weights, w_other)


def join_call(here, near, far, term, got, inner):
    _, _, block, model = near.shape
    fixed = lambda shape: pl.BlockSpec(shape, lambda i: (0,) * len(shape))
    bc_spec = pl.BlockSpec((term.shape[0], lanes), lambda i: (0, 2 * inner // lanes))
    return pl.pallas_call(
        join_kernel,
        grid=(1,),
        in_specs=[smem_spec, fixed(near.shape), fixed(far.shape), bc_spec, fixed(got.shape)],
        out_specs=[fixed((block, model))] * 4 + [bc_spec],
        out_shape=[HBM((block, model), bf16)] * 4 + [HBM(term.shape, bf16)],
        input_output_aliases={3: 4},
        compiler_params=pltpu.CompilerParams(vmem_limit_bytes=wide_vmem),
        cost_estimate=cost(3),
        name="join_halves",
    )(here, near, far, term, got)


def total_call(shares, inner, heads):
    times, far, seqs, near, rows, columns = shares.shape
    group = times * seqs
    shapes = [(rows, 2 * group * inner), (rows, 2 * lanes + group * heads)]

    def kernel(*refs):
        total_kernel(*refs, inner=inner, heads=heads, group=group)

    return pl.pallas_call(
        kernel,
        grid=(group,),
        in_specs=[pl.BlockSpec((1, far, 1, near, rows, columns), lambda i: (i // seqs, 0, i % seqs, 0, 0, 0))],
        out_specs=[fixed_spec(a) for a in shapes],
        out_shape=[jax.ShapeDtypeStruct(a, f32) for a in shapes],
        compiler_params=pltpu.CompilerParams(vmem_limit_bytes=vmem),
        cost_estimate=cost(2),
        name="total_shares",
    )(shares)


def partner(a):
    return lax.ppermute(a, "core", [(0, 1), (1, 0)])


def around(give):
    came = [give(0)]
    spot = lambda chip: (chip % 2) * 2 + chip // 2
    for k in (1, 2, 3):
        came.append(lax.ppermute(give(k), ("yl", "xl"), [(spot(chip), spot(chip ^ k)) for chip in range(4)]))
    return came


def stack_kernel(place, a, b, c, d, _, own_o, give_o):
    inner = own_o.shape[2] // 5
    model = 4 * inner
    for k, came in enumerate((a, b, c, d)):
        tokens = came[:, :model]
        one, two = came[:, model : model + inner], came[:, model + inner :]
        first = place[1] == 0
        own_o[k] = jnp.concatenate([tokens, jnp.where(first, one, two)], axis=1)
        give_o[k] = jnp.concatenate([tokens, jnp.where(first, two, one)], axis=1)


def stack_call(place, came, early):
    block, columns = came[0].shape
    stacked = (4, block, columns // 6 * 5)
    return pl.pallas_call(
        stack_kernel,
        in_specs=[pl.BlockSpec(memory_space=pltpu.SMEM)] + [vmem_spec] * 4 + [pl.BlockSpec(memory_space=pl.ANY)],
        out_specs=[vmem_spec] * 2,
        out_shape=[HBM(stacked, bf16), HBM(stacked, bf16)],
        compiler_params=pltpu.CompilerParams(vmem_limit_bytes=wide_vmem),
        cost_estimate=cost(stack_cost),
        name="stack_pieces",
    )(place, *came, early)


def sum_kernel(a, b, c, d, heads, out, layer_o):
    out[...] = ((a[...].astype(f32) + b[...].astype(f32)) + (c[...].astype(f32) + d[...].astype(f32))).astype(bf16)
    inner = heads.shape[2]
    for k in range(heads.shape[0]):
        layer_o[:, k * inner : (k + 1) * inner] = heads[k]


def sum_call(arrays, heads):
    group, block, inner = heads.shape
    return pl.pallas_call(
        sum_kernel,
        out_shape=[
            jax.ShapeDtypeStruct(arrays[0].shape, bf16),
            jax.ShapeDtypeStruct((block, group * inner), bf16),
        ],
        compiler_params=pltpu.CompilerParams(vmem_limit_bytes=wide_vmem),
        cost_estimate=cost(sum_cost),
        name="sum_pieces",
    )(*arrays, heads)


def body(tokens, cotangent, w_xz, w_bcdt, rate, dt_bias, skip, gain):
    group = lax.axis_size(group_axes)
    devices = lax.axis_size(whole)
    mine = lax.axis_index(group_axes)
    chunks = lax.axis_size("yl") * lax.axis_size("core")
    seqs = group // chunks
    owners = lax.axis_size(rows_axes)
    block, model = tokens.shape[1:]
    total = cotangent.shape[2]
    inner = total // group
    heads = rate.shape[0] // group
    width = inner // heads
    states = (w_bcdt.shape[1] - rate.shape[0]) // 2

    core = lax.axis_index("core")
    here = lax.axis_index(("xl", "yl"))
    place = jnp.stack([here, core]).astype(jnp.int32)
    sides = tuple(lax.axis_size(name) for name in rows_axes)
    *pieces, copies = pack_call(tokens[0], cotangent[0], w_xz, w_bcdt, sides, group, heads)
    copies = copies.reshape((owners,) + copies.shape[4:])

    own = lambda a: lax.dynamic_slice_in_dim(a, mine * heads, heads, 0)
    padded = lambda a: jnp.pad(jnp.tile(own(a), lanes // heads), (0, inner - lanes))
    par = jnp.stack(
        [jnp.repeat(own(skip), width), lax.dynamic_slice_in_dim(gain, mine * inner, inner, 0)]
        + [padded(dt_bias), padded(rate)]
        + [jnp.zeros((inner,), f32)] * 4
    )
    own_came, give_came = stack_call(place, around(lambda shift: pieces[shift]), par)
    far_came = partner(give_came)

    rest = owners // sides[0]
    traders = [
        [(((start + k) % 2) * sides[0] + k) * rest + i for k in range(sides[0]) for i in range(rest)]
        for start in range(2)
    ]
    weights = lax.all_to_all(copies, ("yl",) + rows_axes, 0, 0, axis_index_groups=traders, tiled=True)
    weights = weights.reshape(model, -1)
    w_other = partner(weights[:, 2 * inner : 2 * inner + lanes])

    tok, cot, xv, gate, bc, low, y, chunk_states, stats = forward_call(
        place, own_came, far_came, weights, w_other, par, width
    )
    stats = stats + partner(stats)
    stats = around(lambda shift: stats)
    scalar = lambda a: jnp.full((1,), a, jnp.int32)
    scanned = (xv, gate, bc, low, y, chunk_states, cot, tok)
    out, near, far, term, give = backward_call(
        scalar(core), scanned, stats, par, weights, w_other, width, float(total)
    )
    layer_out = lax.all_to_all(out.reshape(group, block, inner), group_axes, 0, 0, tiled=True)
    *sums, term = join_call(scalar(here), near, partner(far), term, partner(give), inner)
    shares = lax.all_to_all(term.reshape(devices, model // devices, -1), whole, 0, 0, tiled=True)
    came = around(lambda shift: sums[shift])
    grad_input, layer_out = sum_call(came, layer_out)
    grad_xz, grad_bcdt = total_call(
        shares.reshape(chunks, -1, seqs, lax.axis_size("z"), model // devices, shares.shape[-1]), inner, heads
    )
    return (layer_out[None], grad_input[None], grad_xz, grad_bcdt)


def solution(mesh):
    split = Mesh(mesh.devices.reshape(2, 2, 2, 2, 2, 4), whole)
    ctx, fsdp = ("yl", "core"), rows_axes
    placed = (P(fsdp, ctx, None), P(fsdp, ctx, None), P(fsdp, None), P(fsdp, None), P(), P(), P(), P())
    return jax.shard_map(
        body,
        mesh=split,
        in_specs=placed,
        out_specs=(P(fsdp, ctx, None), P(fsdp, ctx, None), P(ctx + fsdp, None), P(ctx + fsdp)),
        check_vma=False,
    )
```

```python
import jax
import jax.numpy as jnp
from jax import lax
from jax.experimental import pallas as pl
from jax.experimental.pallas import tpu as pltpu
from jax.sharding import Mesh, PartitionSpec as P

f32 = jnp.float32
bf16 = jnp.bfloat16
norm_eps = 1e-05
lanes = 128
NN = (((1,), (0,)), ((), ()))
NT = (((1,), (1,)), ((), ()))
TN = (((0,), (0,)), ((), ()))

whole = ("yl", "core", "yh", "xh", "xl", "z")
rows_axes = ("yh", "xh", "xl", "z")
group_axes = ("yl", "core", "xl")
vmem = 32 * 2**20
wide_vmem = 60 * 2**20
stack_cost, sum_cost = 12, 24


def dot1(a, b, dims):
    return lax.dot_general(a.astype(bf16), b.astype(bf16), dims, preferred_element_type=f32)


def halves(a):
    high = a.astype(bf16)
    return (high, (a - high.astype(f32)).astype(bf16))


def dot3(a, b, dims):
    a_high, a_low = a if isinstance(a, tuple) else halves(a)
    b_high, b_low = b if isinstance(b, tuple) else halves(b)
    dot = lambda left, right: lax.dot_general(left, right, dims, preferred_element_type=f32)
    (ca,), (cb,) = dims[0]
    both = dot(jnp.concatenate([a_high, a_low], axis=ca), jnp.concatenate([b_high, b_high], axis=cb))
    return both + dot(a_high, b_low)


def thirds(a):
    high = a.astype(bf16)
    rest = a - high.astype(f32)
    mid = rest.astype(bf16)
    return (high, mid, (rest - mid.astype(f32)).astype(bf16))


def dot_ones(pieces, ones, dims):
    first, *rest = [lax.dot_general(a, ones, dims, preferred_element_type=f32) for a in pieces]
    return first + sum(rest[1:], rest[0])


def spread_out(steps, cumul, expander):
    block = steps.shape[0]
    (s_high, s_low), (c_high, c_mid, c_low) = halves(steps), thirds(cumul)
    stacked = jnp.concatenate([s_high, s_low, c_high, c_mid, c_low], axis=0)
    wide = lax.dot_general(stacked, expander, NN, preferred_element_type=f32)
    at = lambda k: wide[k * block : (k + 1) * block]
    return at(0) + at(1), at(2) + (at(3) + at(4))


def iota(shape, axis):
    return lax.broadcasted_iota(jnp.int32, shape, axis)


def head_expander(inner, width, units):
    shape = (lanes, units * inner)
    start = iota(shape, 0) * width
    col = iota(shape, 1)
    return ((col >= start) & (col < start + width)).astype(f32).astype(bf16)


def packed(parts, heads):
    keep = iota(parts[0].shape, 1) < heads
    kept = [jnp.where(keep, a, 0.0) for a in parts]
    return sum(a if u == 0 else pltpu.roll(a, u * heads, 1) for u, a in enumerate(kept))


def unpacked(a, unit, heads):
    moved = a if unit == 0 else pltpu.roll(a, lanes - unit * heads, 1)
    return jnp.where(iota(a.shape, 1) < heads, moved, 0.0)


def beside(parts):
    return jnp.concatenate(list(parts), axis=1)


def lower_ones(block):
    shape = (block, block)
    return (iota(shape, 0) >= iota(shape, 1)).astype(f32).astype(bf16)


def ones_dot(ones, pieces):
    width = pieces[0].shape[1]
    wide = lax.dot_general(ones, jnp.concatenate(pieces, axis=1), NN, preferred_element_type=f32)
    parts = [wide[:, k * width : (k + 1) * width] for k in range(len(pieces))]
    return parts[0] + sum(parts[2:], parts[1])


def softplus(a):
    return jnp.maximum(a, 0.0) + jnp.log1p(jnp.exp(-jnp.abs(a)))


def pair_halves(a, block, width):
    left = iota(a.shape, 1) < width
    zero = jnp.zeros_like(a)
    return jnp.concatenate([jnp.where(left, a, zero), jnp.where(left, zero, a)], axis=0)


def pack_kernel(tokens, cot, w_xz, w_bcdt, out_0, out_1, out_2, out_3, copies, *, inner, heads, states):
    yl = lax.axis_index("yl")
    place = (lax.axis_index("xl") * 2 + yl, lax.axis_index("core"), yl + lax.axis_index("yh"))
    cols = lambda block, count=1: pl.ds(pl.multiple_of(block * inner, inner), count * inner)
    mine = tokens[...]
    for k, out in enumerate((out_0, out_1, out_2, out_3)):
        chip = lax.bitwise_xor(place[0], k)
        first = lax.rem(chip, 2) * 4 + lax.div(chip, 2)
        out[...] = jnp.concatenate([mine, cot[:, cols(first)], cot[:, cols(first + 2)]], axis=1)

    low = w_bcdt[...].astype(f32)
    rows = low.shape[0]
    filled = jnp.zeros((rows, 2 * lanes - (low.shape[1] - 2 * states)), f32)
    all_steps = jnp.concatenate([low[:, 2 * states :], filled], axis=1)
    half = jnp.where(place[1] == 0, low[:, :states], low[:, states : 2 * states]).astype(bf16)
    group = w_xz.shape[1] // (2 * inner)
    yh, xh, xl, z = copies.shape[:4]
    for side in range(yh):
        for s in range(xl):
            target = (lax.rem(place[2] + side, 2) * 2 + place[1]) * 2 + s
            steps = pltpu.roll(all_steps, 2 * lanes - target * heads, 1)[:, :lanes]
            steps = jnp.where(iota(steps.shape, 1) < heads, steps, 0.0).astype(bf16)
            row = jnp.concatenate([w_xz[:, cols(target)], w_xz[:, cols(group + target)], half, steps], axis=1)
            for upper in range(xh):
                copies[side, upper, s] = jnp.broadcast_to(row[None], (z,) + row.shape)


def whole_weights(main, other, first, inner):
    half, got = main[:, 2 * inner : 2 * inner + lanes], other[...]
    b_part, c_part = jnp.where(first, half, got), jnp.where(first, got, half)
    return jnp.concatenate([main[:, : 2 * inner], b_part, c_part, main[:, 2 * inner + lanes :]], axis=1)


def forward_kernel(place, own, far, w_main, w_other, par, *rest, width, inner):
    *outs, state = rest
    first = place[1] == 0
    weights = whole_weights(w_main, w_other, first, inner)
    state[...] = jnp.zeros_like(state)
    steps = outs[0].shape[0] // chunks_per_step
    for i in range(steps):
        came = [
            [a[lax.bitwise_xor(place[0], 2 * s + i)] for a in (own, far)] for s in range(outs[0].shape[1])
        ]
        views = [a.at[pl.ds(i * (a.shape[0] // steps), a.shape[0] // steps)] for a in outs]
        forward_step(first, came, weights, par, *views, state, width=width, inner=inner)


def forward_step(
    first, came, weights, par, tok, cot, xv_o, g_o, bc_o, low_o, y_o, st_o, stat_o, state, *, width, inner
):
    per_step, seqs, block, model = tok.shape
    units = [(j, s) for j in range(per_step) for s in range(seqs)]
    for s, (own, far) in enumerate(came):
        one, two = jnp.where(first, own, far), jnp.where(first, far, own)
        tok[0, s], tok[1, s] = one[:, :model], two[:, :model]
        cot[0, s], cot[1, s] = one[:, model:], two[:, model:]
    count = len(units)
    heads = inner // width

    proj = lax.dot_general(tok[...].reshape(count * block, -1), weights, NN, preferred_element_type=f32)
    cut = lambda u, first, size: proj[u * block : (u + 1) * block, first : first + size]
    part = lambda a, u: a[:, u * inner : (u + 1) * inner]
    expander = head_expander(inner, width, count)
    causal = iota((block, block), 0) >= iota((block, block), 1)
    skip, gain = beside([par[0:1, :]] * count), beside([par[1:2, :]] * count)
    bias, rate = par[2:3, :lanes], par[3:4, :lanes]

    raw = packed([cut(u, 2 * inner + 2 * lanes, lanes) for u in range(count)], heads) + bias
    steps = softplus(raw)
    cumul = ones_dot(lower_ones(block), thirds(-steps * rate))
    cumul_t = cumul.T
    low_o[0, 0], low_o[0, 1], low_o[0, 2] = raw, steps, cumul
    b_two, c_two = [], []
    for u, (j, s) in enumerate(units):
        b_in, c_out = cut(u, 2 * inner, lanes), cut(u, 2 * inner + lanes, lanes)
        bc_o[j, s] = beside([b_in, c_out])
        xv_o[j, s] = cut(u, 0, inner)
        g_o[j, s] = cut(u, inner, inner)
        b_two.append(halves(b_in))
        c_two.append(halves(c_out))
    scores = [dot3(c_two[u], b_two[u], NT) for u in range(count)]
    step_wide, cumul_wide = spread_out(steps, cumul, expander)
    last_wide = cumul_wide[block - 1 : block]
    xv = beside(cut(u, 0, inner) for u in range(count))
    gate = beside(cut(u, inner, inner) for u in range(count))
    values = xv * jax.nn.sigmoid(xv)
    scaled = values * step_wide
    tailed = scaled * jnp.exp(last_wide - cumul_wide)
    last_decay = jnp.exp(last_wide)
    updates = [dot3(b_two[u], part(tailed, u), TN) for u in range(count)]
    inners = []
    for u in range(count):
        for pair in range(heads // 2):
            both = []
            for h in (u * heads + 2 * pair, u * heads + 2 * pair + 1):
                gap = jnp.where(causal, cumul[:, h : h + 1] - cumul_t[h : h + 1, :], -1e30)
                both.append((scores[u] * jnp.exp(gap)).astype(bf16))
            first = u * inner + 2 * pair * width
            cols = scaled[:, first : first + 2 * width]
            inners.append(
                lax.dot_general(
                    beside(both), pair_halves(cols, block, width).astype(bf16), NN, preferred_element_type=f32
                )
            )
    carried = []
    for u, (j, s) in enumerate(units):
        old = state[s]
        st_o[j, s] = old
        carried.append(dot3(c_two[u], old, NN))
        state[s] = part(last_decay, u) * old + updates[u]
    y = jnp.exp(cumul_wide) * beside(carried) + beside(inners) + skip * values
    mixed = y * (gate * jax.nn.sigmoid(gate))
    weighted = beside(cot[j, s] for j, s in units).astype(f32) * gain * mixed
    squared = mixed * mixed
    sums = []
    for u, (j, s) in enumerate(units):
        y_o[j, s] = part(y, u)
        high, low = halves(beside([part(squared, u), part(weighted, u)]))
        dot = lambda right: lax.dot_general(stat_rows(u, inner), right, NT, preferred_element_type=f32)
        sums.append(dot(high) + dot(low))
    stat_o[0] = (sums[0] + sums[1]) + (sums[2] + sums[3])


def stat_rows(unit, inner):
    row, col = iota((8, 2 * inner), 0), iota((8, 2 * inner), 1)
    return (((row == 2 * unit) & (col < inner)) | ((row == 2 * unit + 1) & (col >= inner))).astype(f32).astype(bf16)


def norm_step(y_i, g_i, cot, sums, par, out_o, *, total):
    _, seqs, block, inner = y_i.shape
    gain = par[1:2, :]
    mean = sums * (1.0 / total)
    even = lax.rem(iota(mean.shape, 0), 2) == 0
    scales = lax.rsqrt(jnp.where(even, mean, 1.0) + norm_eps)
    before = pltpu.roll(scales, 1, 0)
    stacked = halves(jnp.where(even, scales, before * before * before * mean))
    d_y, d_gate = [], []
    for u in range(y_i.shape[0] * seqs):
        j, s = u // seqs, u % seqs
        spread = dot_ones(stacked, stat_rows(u, inner), TN)
        scale, pull = spread[:, :inner], spread[:, inner:]
        gate, full = g_i[j, s], y_i[j, s]
        gate_sig = jax.nn.sigmoid(gate)
        gate_silu = gate * gate_sig
        mixed = full * gate_silu
        out_o[j, s] = (mixed * scale * gain).astype(bf16)
        d_mixed = cot[j, s].astype(f32) * gain * scale - mixed * pull
        d_y.append(d_mixed * gate_silu)
        d_gate.append((d_mixed * full * (gate_sig * (1.0 + gate * (1.0 - gate_sig)))).astype(bf16))
    return beside(d_y), d_gate


def backward_kernel(core, *refs, width, inner, total):
    ins, stats, (par, w_main, w_other) = refs[:8], refs[8:12], refs[12:15]
    far_outs, (out, near, far, term, give), (grad_state, next_state, here_all, sems) = refs[15:20], refs[20:25], refs[25:]
    copies = []

    def send(index, first_row, rows):
        here, there = (out, near, far, term, give)[index], far_outs[index]
        span = pl.ds(first_row, rows)
        copies.append(pltpu.make_async_copy(here.at[span], there.at[span], sems.at[len(copies)]))
        copies[-1].start()

    grad_state[...] = jnp.zeros_like(grad_state)
    next_state[...] = jnp.zeros_like(next_state)
    first = core[0] == 0
    weights = whole_weights(w_main, w_other, first, inner)
    steps = near.shape[0]
    rows = here_all.shape[0] // steps
    for i in reversed(range(steps)):
        views = [a.at[pl.ds(i * (a.shape[0] // steps), a.shape[0] // steps)] for a in ins + (out, near, far)]
        sums = (stats[0][i] + stats[1][i]) + (stats[2][i] + stats[3][i])
        here_all[i * rows : (i + 1) * rows, :] = backward_step(
            first, *views, sums, par, weights, grad_state, next_state, width=width, inner=inner, total=total
        )
        for index in (2, 1, 0):
            size = (out, near, far)[index].shape[0] // steps
            send(index, i * size, size)

    tok = ins[7]
    wide = 2 * inner
    slab = term.shape[0] // slabs
    for q in range(slabs):
        span = slice(q * slab, (q + 1) * slab)
        left = tok[:, :, :, span].reshape(steps * rows, slab)
        part = lax.dot_general(left, here_all[...], TN, preferred_element_type=f32).astype(bf16)
        b_part, c_part = part[:, wide : wide + lanes], part[:, wide + lanes : wide + 2 * lanes]
        give[span, :] = jnp.where(first, c_part, b_part)
        term[span, :] = jnp.concatenate(
            [part[:, :wide], jnp.where(first, b_part, c_part), part[:, wide + 2 * lanes :]], axis=1
        )
        send(4, q * slab, slab)
        send(3, q * slab, slab)
    for copy in copies:
        copy.wait()


def backward_step(
    first_core, xv_i, g_i, bc_i, low_i, y_i, st_i, cot, tok, out_o, near_o, far_o, sums, par, weights,
    grad_state, next_state, *, width, inner, total
):
    per_step, seqs, block, model = tok.shape
    units = [(j, s) for j in range(per_step) for s in range(seqs)]
    count = len(units)
    heads = inner // width
    part = lambda a, u: a[:, u * inner : (u + 1) * inner]
    expander = head_expander(inner, width, count)
    later = iota((block, block), 1) >= iota((block, block), 0)
    upper = (iota((block, block), 1) >= iota((block, block), 0)).astype(f32).astype(bf16)
    skip, rate = beside([par[0:1, :]] * count), par[3:4, :lanes]
    raw, steps, cumul = low_i[0, 0], low_i[0, 1], low_i[0, 2]
    cumul_t = cumul.T
    step_wide, cumul_wide = spread_out(steps, cumul, expander)
    last_wide = cumul_wide[block - 1 : block]
    tail, last_decay = jnp.exp(last_wide - cumul_wide), jnp.exp(last_wide)
    b_two = [halves(bc_i[j, s, :, :lanes]) for j, s in units]
    c_two = [halves(bc_i[j, s, :, lanes:]) for j, s in units]
    scores_t = [dot3(b_two[u], c_two[u], NT) for u in range(count)]
    xv = beside(xv_i[j, s] for j, s in units)
    d_y, d_gate = norm_step(y_i, g_i, cot, sums, par, out_o, total=total)
    sig = jax.nn.sigmoid(xv)
    values = xv * sig
    y = beside(y_i[j, s] for j, s in units) - skip * values
    scaled = values * step_wide
    tailed = scaled * tail
    lifted = halves(d_y * jnp.exp(cumul_wide))
    lifted = [(part(lifted[0], u), part(lifted[1], u)) for u in range(count)]
    updates = [dot3(c_two[u], lifted[u], TN) for u in range(count)]

    back, through, from_state = [None] * count, [None] * count, [None] * count
    for u in reversed(range(count)):
        j, s = units[u]
        grad = grad_state[s]
        grad_two = halves(grad)
        back[u] = dot3(b_two[u], grad_two, NN)
        from_state[u] = dot3(part(tailed, u), grad_two, NT)
        through[u] = jnp.sum(next_state[s] * grad, axis=0, keepdims=True)
        grad_state[s] = part(last_decay, u) * grad + updates[u]
        next_state[s] = st_i[j, s]

    inners, d_scores = [], []
    for u in range(count):
        d_scores_t = jnp.zeros((block, block), f32)
        for pair in range(heads // 2):
            first = u * inner + 2 * pair * width
            cols = slice(first, first + 2 * width)
            products = lax.dot_general(
                pair_halves(scaled[:, cols], block, width).astype(bf16),
                d_y[:, cols].astype(bf16),
                NT,
                preferred_element_type=f32,
            )
            both = []
            for k in range(2):
                h = u * heads + 2 * pair + k
                gap = jnp.where(later, cumul_t[h : h + 1, :] - cumul[:, h : h + 1], -1e30)
                decay = jnp.exp(gap)
                both.append((scores_t[u] * decay).astype(bf16))
                d_scores_t += products[k * block : (k + 1) * block] * decay
            inners.append(
                lax.dot_general(
                    beside(both), pair_halves(d_y[:, cols], block, width).astype(bf16), NN, preferred_element_type=f32
                )
            )
        d_scores.append(halves(d_scores_t))
    d_c = [
        dot3(d_scores[u], b_two[u], TN) + dot3(lifted[u], st_i[j, s], NT) for u, (j, s) in enumerate(units)
    ]
    d_b = [dot3(d_scores[u], c_two[u], NN) + from_state[u] for u in range(count)]
    back = tail * beside(back) + beside(inners)
    last_row = iota((block, count * inner), 0) == block - 1
    products = jnp.concatenate([values * back, d_y * y + jnp.where(last_row, beside(through), 0.0)], axis=0)
    reduced = dot_ones(halves(products), expander, NT)
    d_steps = reduced[:block]
    d_log = ones_dot(upper, halves(reduced[block:] - steps * d_steps))
    d_raw = (d_steps - d_log * rate) * jax.nn.sigmoid(raw)
    d_values = back * step_wide + skip * d_y
    d_xv = (d_values * (sig * (1.0 + xv * (1.0 - sig)))).astype(bf16)
    here = jnp.concatenate(
        [
            beside([part(d_xv, u), d_gate[u], d_b[u].astype(bf16), d_c[u].astype(bf16)]
                   + [unpacked(d_raw, u, heads).astype(bf16)])
            for u, (j, s) in enumerate(units)
        ],
        axis=0,
    )
    partial = lax.dot_general(here, weights, NT, preferred_element_type=f32)
    partial = partial.reshape(per_step, seqs, block, model)
    near_o[0] = jnp.where(first_core, partial[0], partial[1])
    far_o[0] = jnp.where(first_core, partial[1], partial[0]).astype(bf16)
    return here


def join_kernel(place, near, far, term, got, out_0, out_1, out_2, out_3, term_o):
    for k, out in enumerate((out_0, out_1, out_2, out_3)):
        chip = lax.bitwise_xor(place[0], k)
        yl, xl = lax.rem(chip, 2), lax.div(chip, 2)
        out[...] = (near[yl, xl] + far[yl, xl].astype(f32)).astype(bf16)
    term_o[...] = (term[...].astype(f32) + got[...].astype(f32)).astype(bf16)


def total_kernel(shares, xz_o, bcdt_o, *, inner, heads, group):
    step = pl.program_id(0)
    half = group * inner

    @pl.when(step == 0)
    def _():
        bcdt_o[...] = jnp.zeros_like(bcdt_o)

    summed = jnp.sum(shares[0, :, 0].astype(f32), axis=(0, 1))
    at = pl.multiple_of(step * inner, inner)
    xz_o[:, pl.ds(at, inner)] = summed[:, :inner]
    xz_o[:, pl.ds(pl.multiple_of(half + at, inner), inner)] = summed[:, inner : 2 * inner]
    core = lax.rem(lax.div(step, 2), 2)
    bc = summed[:, 2 * inner : 2 * inner + lanes]
    bcdt_o[:, :lanes] += jnp.where(core == 0, bc, 0.0)
    bcdt_o[:, lanes : 2 * lanes] += jnp.where(core == 0, 0.0, bc)
    steps = summed[:, 2 * inner + lanes :]
    lane = iota(steps.shape, 1)
    moved = pltpu.roll(jnp.where(lane < heads, steps, 0.0), step * heads, 1)
    bcdt_o[:, 2 * lanes :] += moved[:, : group * heads]


def cost(micros):
    return pl.CostEstimate(flops=int(micros * 1.1e9), bytes_accessed=int(micros * 3.5e6), transcendentals=0)


def chunk_spec(shape, count=None, per_step=1):
    blank = (0,) * (len(shape) - 1)
    if count is None:
        return pl.BlockSpec((per_step,) + shape[1:], lambda i: (i,) + blank)
    return pl.BlockSpec((per_step,) + shape[1:], lambda i: (count - 1 - i,) + blank)


def fixed_spec(shape):
    return pl.BlockSpec(shape, lambda i: (0,) * len(shape))


chunks_per_step = 2
slabs = 2
smem_spec = pl.BlockSpec(memory_space=pltpu.SMEM)
vmem_spec = pl.BlockSpec(memory_space=pltpu.VMEM)
HBM = pltpu.HBM


def pack_call(tokens, cot, w_xz, w_bcdt, sides, group, heads):
    block, total = cot.shape
    inner = total // group
    states = (w_bcdt.shape[1] - heads * group) // 2
    copies = sides + (w_xz.shape[0], 2 * inner + states + lanes)
    piece = (block, tokens.shape[1] + 2 * inner)

    def kernel(*refs):
        pack_kernel(*refs, inner=inner, heads=heads, states=states)

    return pl.pallas_call(
        kernel,
        in_specs=[vmem_spec] * 4,
        out_specs=[vmem_spec] * 5,
        out_shape=[HBM(piece, bf16)] * 4 + [HBM(copies, bf16)],
        compiler_params=pltpu.CompilerParams(vmem_limit_bytes=wide_vmem),
        cost_estimate=cost(2),
        name="pack_pieces",
    )(tokens, cot, w_xz, w_bcdt)


def forward_call(place, own, far, weights, w_other, par, width):
    _, block, columns = own.shape
    model = weights.shape[0]
    inner = columns - model
    chunks, seqs = 4, 2
    steps = chunks // chunks_per_step
    wide = (chunks, seqs, block, inner)

    outs = [
        ((chunks, seqs, block, model), bf16),
        (wide, bf16),
        (wide, f32),
        (wide, f32),
        ((chunks, seqs, block, 2 * lanes), f32),
        ((steps, 3, block, lanes), f32),
        (wide, f32),
        ((chunks, seqs, lanes, inner), f32),
        ((steps, 8, block), f32),
    ]

    def kernel(*refs):
        forward_kernel(*refs, width=width, inner=inner)

    return pl.pallas_call(
        kernel,
        in_specs=[smem_spec] + [vmem_spec] * 5,
        out_specs=[vmem_spec] * len(outs),
        out_shape=[jax.ShapeDtypeStruct(a, kind) for a, kind in outs],
        scratch_shapes=[pltpu.VMEM((seqs, lanes, inner), f32)],
        compiler_params=pltpu.CompilerParams(vmem_limit_bytes=vmem),
        cost_estimate=cost(12),
        name="forward_scan",
    )(place, own, far, weights, w_other, par)


def backward_call(core, scanned, stats, par, weights, w_other, width, total):
    xv = scanned[0]
    chunks, seqs, block, inner = xv.shape
    model, columns = weights.shape
    columns = columns + lanes
    half = (chunks // chunks_per_step, seqs, block, model)
    outs = [
        (xv.shape, bf16),
        (half, f32),
        (half, bf16),
        ((model, columns - lanes), bf16),
        ((model, lanes), bf16),
    ]

    def kernel(*refs):
        backward_kernel(*refs, width=width, inner=inner, total=total)

    return pl.pallas_call(
        kernel,
        in_specs=[smem_spec] + [vmem_spec] * 15,
        out_specs=[pl.BlockSpec(memory_space=pltpu.HBM)] * 5,
        out_shape=[HBM(shape, kind) for shape, kind in outs],
        scratch_shapes=[pltpu.VMEM(shape, kind) for shape, kind in outs]
        + [
            pltpu.VMEM((seqs, lanes, inner), f32),
            pltpu.VMEM((seqs, lanes, inner), f32),
            pltpu.VMEM((chunks * seqs * block, columns), bf16),
            pltpu.SemaphoreType.DMA((3 * half[0] + 2 * slabs,)),
        ],
        compiler_params=pltpu.CompilerParams(vmem_limit_bytes=vmem),
        cost_estimate=cost(20),
        name="backward_scan",
    )(core, *scanned, *stats, par, weights, w_other)


def join_call(here, near, far, term, got, inner):
    _, _, block, model = near.shape
    fixed = lambda shape: pl.BlockSpec(shape, lambda i: (0,) * len(shape))
    bc_spec = pl.BlockSpec((term.shape[0], lanes), lambda i: (0, 2 * inner // lanes))
    return pl.pallas_call(
        join_kernel,
        grid=(1,),
        in_specs=[smem_spec, fixed(near.shape), fixed(far.shape), bc_spec, fixed(got.shape)],
        out_specs=[fixed((block, model))] * 4 + [bc_spec],
        out_shape=[HBM((block, model), bf16)] * 4 + [HBM(term.shape, bf16)],
        input_output_aliases={3: 4},
        compiler_params=pltpu.CompilerParams(vmem_limit_bytes=wide_vmem),
        cost_estimate=cost(3),
        name="join_halves",
    )(here, near, far, term, got)


def total_call(shares, inner, heads):
    times, far, seqs, near, rows, columns = shares.shape
    group = times * seqs
    shapes = [(rows, 2 * group * inner), (rows, 2 * lanes + group * heads)]

    def kernel(*refs):
        total_kernel(*refs, inner=inner, heads=heads, group=group)

    return pl.pallas_call(
        kernel,
        grid=(group,),
        in_specs=[pl.BlockSpec((1, far, 1, near, rows, columns), lambda i: (i // seqs, 0, i % seqs, 0, 0, 0))],
        out_specs=[fixed_spec(a) for a in shapes],
        out_shape=[jax.ShapeDtypeStruct(a, f32) for a in shapes],
        compiler_params=pltpu.CompilerParams(vmem_limit_bytes=vmem),
        cost_estimate=cost(2),
        name="total_shares",
    )(shares)


def partner(a):
    return lax.ppermute(a, "core", [(0, 1), (1, 0)])


def around(give):
    came = [give(0)]
    spot = lambda chip: (chip % 2) * 2 + chip // 2
    for k in (1, 2, 3):
        came.append(lax.ppermute(give(k), ("yl", "xl"), [(spot(chip), spot(chip ^ k)) for chip in range(4)]))
    return came


def stack_kernel(place, a, b, c, d, _, own_o, give_o):
    inner = own_o.shape[2] // 5
    model = 4 * inner
    for k, came in enumerate((a, b, c, d)):
        tokens = came[:, :model]
        one, two = came[:, model : model + inner], came[:, model + inner :]
        first = place[1] == 0
        own_o[k] = jnp.concatenate([tokens, jnp.where(first, one, two)], axis=1)
        give_o[k] = jnp.concatenate([tokens, jnp.where(first, two, one)], axis=1)


def stack_call(place, came, early):
    block, columns = came[0].shape
    stacked = (4, block, columns // 6 * 5)
    return pl.pallas_call(
        stack_kernel,
        in_specs=[pl.BlockSpec(memory_space=pltpu.SMEM)] + [vmem_spec] * 4 + [pl.BlockSpec(memory_space=pl.ANY)],
        out_specs=[vmem_spec] * 2,
        out_shape=[HBM(stacked, bf16), HBM(stacked, bf16)],
        compiler_params=pltpu.CompilerParams(vmem_limit_bytes=wide_vmem),
        cost_estimate=cost(stack_cost),
        name="stack_pieces",
    )(place, *came, early)


def sum_kernel(a, b, c, d, heads, out, layer_o):
    out[...] = ((a[...].astype(f32) + b[...].astype(f32)) + (c[...].astype(f32) + d[...].astype(f32))).astype(bf16)
    inner = heads.shape[2]
    for k in range(heads.shape[0]):
        layer_o[:, k * inner : (k + 1) * inner] = heads[k]


def sum_call(arrays, heads):
    group, block, inner = heads.shape
    return pl.pallas_call(
        sum_kernel,
        out_shape=[
            jax.ShapeDtypeStruct(arrays[0].shape, bf16),
            jax.ShapeDtypeStruct((block, group * inner), bf16),
        ],
        compiler_params=pltpu.CompilerParams(vmem_limit_bytes=wide_vmem),
        cost_estimate=cost(sum_cost),
        name="sum_pieces",
    )(*arrays, heads)


def body(tokens, cotangent, w_xz, w_bcdt, rate, dt_bias, skip, gain):
    group = lax.axis_size(group_axes)
    devices = lax.axis_size(whole)
    mine = lax.axis_index(group_axes)
    chunks = lax.axis_size("yl") * lax.axis_size("core")
    seqs = group // chunks
    owners = lax.axis_size(rows_axes)
    block, model = tokens.shape[1:]
    total = cotangent.shape[2]
    inner = total // group
    heads = rate.shape[0] // group
    width = inner // heads
    states = (w_bcdt.shape[1] - rate.shape[0]) // 2

    core = lax.axis_index("core")
    here = lax.axis_index(("xl", "yl"))
    place = jnp.stack([here, core]).astype(jnp.int32)
    sides = tuple(lax.axis_size(name) for name in rows_axes)
    *pieces, copies = pack_call(tokens[0], cotangent[0], w_xz, w_bcdt, sides, group, heads)
    copies = copies.reshape((owners,) + copies.shape[4:])

    own = lambda a: lax.dynamic_slice_in_dim(a, mine * heads, heads, 0)
    padded = lambda a: jnp.pad(jnp.tile(own(a), lanes // heads), (0, inner - lanes))
    par = jnp.stack(
        [jnp.repeat(own(skip), width), lax.dynamic_slice_in_dim(gain, mine * inner, inner, 0)]
        + [padded(dt_bias), padded(rate)]
        + [jnp.zeros((inner,), f32)] * 4
    )
    own_came, give_came = stack_call(place, around(lambda shift: pieces[shift]), par)
    far_came = partner(give_came)

    rest = owners // sides[0]
    traders = [
        [(((start + k) % 2) * sides[0] + k) * rest + i for k in range(sides[0]) for i in range(rest)]
        for start in range(2)
    ]
    weights = lax.all_to_all(copies, ("yl",) + rows_axes, 0, 0, axis_index_groups=traders, tiled=True)
    weights = weights.reshape(model, -1)
    w_other = partner(weights[:, 2 * inner : 2 * inner + lanes])

    tok, cot, xv, gate, bc, low, y, chunk_states, stats = forward_call(
        place, own_came, far_came, weights, w_other, par, width
    )
    stats = stats + partner(stats)
    stats = around(lambda shift: stats)
    scalar = lambda a: jnp.full((1,), a, jnp.int32)
    scanned = (xv, gate, bc, low, y, chunk_states, cot, tok)
    out, near, far, term, give = backward_call(
        scalar(core), scanned, stats, par, weights, w_other, width, float(total)
    )
    layer_out = lax.all_to_all(out.reshape(group, block, inner), group_axes, 0, 0, tiled=True)
    *sums, term = join_call(scalar(here), near, partner(far), term, partner(give), inner)
    shares = lax.all_to_all(term.reshape(devices, model // devices, -1), whole, 0, 0, tiled=True)
    came = around(lambda shift: sums[shift])
    grad_input, layer_out = sum_call(came, layer_out)
    grad_xz, grad_bcdt = total_call(
        shares.reshape(chunks, -1, seqs, lax.axis_size("z"), model // devices, shares.shape[-1]), inner, heads
    )
    return (layer_out[None], grad_input[None], grad_xz, grad_bcdt)


def solution(mesh):
    split = Mesh(mesh.devices.reshape(2, 2, 2, 2, 2, 4), whole)
    ctx, fsdp = ("yl", "core"), rows_axes
    placed = (P(fsdp, ctx, None), P(fsdp, ctx, None), P(fsdp, None), P(fsdp, None), P(), P(), P(), P())
    return jax.shard_map(
        body,
        mesh=split,
        in_specs=placed,
        out_specs=(P(fsdp, ctx, None), P(fsdp, ctx, None), P(ctx + fsdp, None), P(ctx + fsdp)),
        check_vma=False,
    )
```

```python
import jax
import jax.numpy as jnp
from jax import lax
from jax.experimental import pallas as pl
from jax.experimental.pallas import tpu as pltpu
from jax.sharding import Mesh, PartitionSpec as P

f32 = jnp.float32
bf16 = jnp.bfloat16
norm_eps = 1e-05
lanes = 128
NN = (((1,), (0,)), ((), ()))
NT = (((1,), (1,)), ((), ()))
TN = (((0,), (0,)), ((), ()))

whole = ("yl", "core", "yh", "xh", "xl", "z")
rows_axes = ("yh", "xh", "xl", "z")
group_axes = ("yl", "core", "xl")
vmem = 32 * 2**20
wide_vmem = 60 * 2**20
stack_cost, sum_cost = 12, 24


def dot1(a, b, dims):
    return lax.dot_general(a.astype(bf16), b.astype(bf16), dims, preferred_element_type=f32)


def halves(a):
    high = a.astype(bf16)
    return (high, (a - high.astype(f32)).astype(bf16))


def dot3(a, b, dims):
    a_high, a_low = a if isinstance(a, tuple) else halves(a)
    b_high, b_low = b if isinstance(b, tuple) else halves(b)
    dot = lambda left, right: lax.dot_general(left, right, dims, preferred_element_type=f32)
    (ca,), (cb,) = dims[0]
    both = dot(jnp.concatenate([a_high, a_low], axis=ca), jnp.concatenate([b_high, b_high], axis=cb))
    return both + dot(a_high, b_low)


def thirds(a):
    high = a.astype(bf16)
    rest = a - high.astype(f32)
    mid = rest.astype(bf16)
    return (high, mid, (rest - mid.astype(f32)).astype(bf16))


def dot_ones(pieces, ones, dims):
    first, *rest = [lax.dot_general(a, ones, dims, preferred_element_type=f32) for a in pieces]
    return first + sum(rest[1:], rest[0])


def spread_out(steps, cumul, expander):
    block = steps.shape[0]
    (s_high, s_low), (c_high, c_mid, c_low) = halves(steps), thirds(cumul)
    stacked = jnp.concatenate([s_high, s_low, c_high, c_mid, c_low], axis=0)
    wide = lax.dot_general(stacked, expander, NN, preferred_element_type=f32)
    at = lambda k: wide[k * block : (k + 1) * block]
    return at(0) + at(1), at(2) + (at(3) + at(4))


def iota(shape, axis):
    return lax.broadcasted_iota(jnp.int32, shape, axis)


def head_expander(inner, width, units):
    shape = (lanes, units * inner)
    start = iota(shape, 0) * width
    col = iota(shape, 1)
    return ((col >= start) & (col < start + width)).astype(f32).astype(bf16)


def packed(parts, heads):
    keep = iota(parts[0].shape, 1) < heads
    kept = [jnp.where(keep, a, 0.0) for a in parts]
    return sum(a if u == 0 else pltpu.roll(a, u * heads, 1) for u, a in enumerate(kept))


def unpacked(a, unit, heads):
    moved = a if unit == 0 else pltpu.roll(a, lanes - unit * heads, 1)
    return jnp.where(iota(a.shape, 1) < heads, moved, 0.0)


def beside(parts):
    return jnp.concatenate(list(parts), axis=1)


def lower_ones(block):
    shape = (block, block)
    return (iota(shape, 0) >= iota(shape, 1)).astype(f32).astype(bf16)


def ones_dot(ones, pieces):
    width = pieces[0].shape[1]
    wide = lax.dot_general(ones, jnp.concatenate(pieces, axis=1), NN, preferred_element_type=f32)
    parts = [wide[:, k * width : (k + 1) * width] for k in range(len(pieces))]
    return parts[0] + sum(parts[2:], parts[1])


def softplus(a):
    return jnp.maximum(a, 0.0) + jnp.log1p(jnp.exp(-jnp.abs(a)))


def pair_halves(a, block, width):
    left = iota(a.shape, 1) < width
    zero = jnp.zeros_like(a)
    return jnp.concatenate([jnp.where(left, a, zero), jnp.where(left, zero, a)], axis=0)


def pack_kernel(tokens, cot, w_xz, w_bcdt, out_0, out_1, out_2, out_3, copies, *, inner, heads, states):
    yl = lax.axis_index("yl")
    place = (lax.axis_index("xl") * 2 + yl, lax.axis_index("core"), yl + lax.axis_index("yh"))
    cols = lambda block, count=1: pl.ds(pl.multiple_of(block * inner, inner), count * inner)
    mine = tokens[...]
    for k, out in enumerate((out_0, out_1, out_2, out_3)):
        chip = lax.bitwise_xor(place[0], k)
        first = lax.rem(chip, 2) * 4 + lax.div(chip, 2)
        out[...] = jnp.concatenate([mine, cot[:, cols(first)], cot[:, cols(first + 2)]], axis=1)

    low = w_bcdt[...].astype(f32)
    rows = low.shape[0]
    filled = jnp.zeros((rows, 2 * lanes - (low.shape[1] - 2 * states)), f32)
    all_steps = jnp.concatenate([low[:, 2 * states :], filled], axis=1)
    half = jnp.where(place[1] == 0, low[:, :states], low[:, states : 2 * states]).astype(bf16)
    group = w_xz.shape[1] // (2 * inner)
    yh, xh, xl, z = copies.shape[:4]
    for side in range(yh):
        for s in range(xl):
            target = (lax.rem(place[2] + side, 2) * 2 + place[1]) * 2 + s
            steps = pltpu.roll(all_steps, 2 * lanes - target * heads, 1)[:, :lanes]
            steps = jnp.where(iota(steps.shape, 1) < heads, steps, 0.0).astype(bf16)
            row = jnp.concatenate([w_xz[:, cols(target)], w_xz[:, cols(group + target)], half, steps], axis=1)
            for upper in range(xh):
                copies[side, upper, s] = jnp.broadcast_to(row[None], (z,) + row.shape)


def whole_weights(main, other, first, inner):
    half, got = main[:, 2 * inner : 2 * inner + lanes], other[...]
    b_part, c_part = jnp.where(first, half, got), jnp.where(first, got, half)
    return jnp.concatenate([main[:, : 2 * inner], b_part, c_part, main[:, 2 * inner + lanes :]], axis=1)


def forward_kernel(place, own, far, w_main, w_other, par, *rest, width, inner):
    *outs, state = rest
    first = place[1] == 0
    weights = whole_weights(w_main, w_other, first, inner)
    state[...] = jnp.zeros_like(state)
    steps = outs[0].shape[0] // chunks_per_step
    for i in range(steps):
        came = [
            [a[lax.bitwise_xor(place[0], 2 * s + i)] for a in (own, far)] for s in range(outs[0].shape[1])
        ]
        views = [a.at[pl.ds(i * (a.shape[0] // steps), a.shape[0] // steps)] for a in outs]
        forward_step(first, came, weights, par, *views, state, width=width, inner=inner)


def forward_step(
    first, came, weights, par, tok, cot, xv_o, g_o, bc_o, low_o, y_o, st_o, stat_o, state, *, width, inner
):
    per_step, seqs, block, model = tok.shape
    units = [(j, s) for j in range(per_step) for s in range(seqs)]
    for s, (own, far) in enumerate(came):
        one, two = jnp.where(first, own, far), jnp.where(first, far, own)
        tok[0, s], tok[1, s] = one[:, :model], two[:, :model]
        cot[0, s], cot[1, s] = one[:, model:], two[:, model:]
    count = len(units)
    heads = inner // width

    proj = lax.dot_general(tok[...].reshape(count * block, -1), weights, NN, preferred_element_type=f32)
    cut = lambda u, first, size: proj[u * block : (u + 1) * block, first : first + size]
    part = lambda a, u: a[:, u * inner : (u + 1) * inner]
    expander = head_expander(inner, width, count)
    causal = iota((block, block), 0) >= iota((block, block), 1)
    skip, gain = beside([par[0:1, :]] * count), beside([par[1:2, :]] * count)
    bias, rate = par[2:3, :lanes], par[3:4, :lanes]

    raw = packed([cut(u, 2 * inner + 2 * lanes, lanes) for u in range(count)], heads) + bias
    steps = softplus(raw)
    cumul = ones_dot(lower_ones(block), thirds(-steps * rate))
    cumul_t = cumul.T
    low_o[0, 0], low_o[0, 1], low_o[0, 2] = raw, steps, cumul
    b_two, c_two = [], []
    for u, (j, s) in enumerate(units):
        b_in, c_out = cut(u, 2 * inner, lanes), cut(u, 2 * inner + lanes, lanes)
        bc_o[j, s] = beside([b_in, c_out])
        xv_o[j, s] = cut(u, 0, inner)
        g_o[j, s] = cut(u, inner, inner)
        b_two.append(halves(b_in))
        c_two.append(halves(c_out))
    scores = [dot3(c_two[u], b_two[u], NT) for u in range(count)]
    step_wide, cumul_wide = spread_out(steps, cumul, expander)
    last_wide = cumul_wide[block - 1 : block]
    xv = beside(cut(u, 0, inner) for u in range(count))
    gate = beside(cut(u, inner, inner) for u in range(count))
    values = xv * jax.nn.sigmoid(xv)
    scaled = values * step_wide
    tailed = scaled * jnp.exp(last_wide - cumul_wide)
    last_decay = jnp.exp(last_wide)
    updates = [dot3(b_two[u], part(tailed, u), TN) for u in range(count)]
    inners = []
    for u in range(count):
        for pair in range(heads // 2):
            both = []
            for h in (u * heads + 2 * pair, u * heads + 2 * pair + 1):
                gap = jnp.where(causal, cumul[:, h : h + 1] - cumul_t[h : h + 1, :], -1e30)
                both.append((scores[u] * jnp.exp(gap)).astype(bf16))
            first = u * inner + 2 * pair * width
            cols = scaled[:, first : first + 2 * width]
            inners.append(
                lax.dot_general(
                    beside(both), pair_halves(cols, block, width).astype(bf16), NN, preferred_element_type=f32
                )
            )
    carried = []
    for u, (j, s) in enumerate(units):
        old = state[s]
        st_o[j, s] = old
        carried.append(dot3(c_two[u], old, NN))
        state[s] = part(last_decay, u) * old + updates[u]
    y = jnp.exp(cumul_wide) * beside(carried) + beside(inners) + skip * values
    mixed = y * (gate * jax.nn.sigmoid(gate))
    weighted = beside(cot[j, s] for j, s in units).astype(f32) * gain * mixed
    squared = mixed * mixed
    sums = []
    for u, (j, s) in enumerate(units):
        y_o[j, s] = part(y, u)
        high, low = halves(beside([part(squared, u), part(weighted, u)]))
        dot = lambda right: lax.dot_general(stat_rows(u, inner), right, NT, preferred_element_type=f32)
        sums.append(dot(high) + dot(low))
    stat_o[0] = (sums[0] + sums[1]) + (sums[2] + sums[3])


def stat_rows(unit, inner):
    row, col = iota((8, 2 * inner), 0), iota((8, 2 * inner), 1)
    return (((row == 2 * unit) & (col < inner)) | ((row == 2 * unit + 1) & (col >= inner))).astype(f32).astype(bf16)


def norm_step(y_i, g_i, cot, sums, par, out_o, *, total):
    _, seqs, block, inner = y_i.shape
    gain = par[1:2, :]
    mean = sums * (1.0 / total)
    even = lax.rem(iota(mean.shape, 0), 2) == 0
    scales = lax.rsqrt(jnp.where(even, mean, 1.0) + norm_eps)
    before = pltpu.roll(scales, 1, 0)
    stacked = halves(jnp.where(even, scales, before * before * before * mean))
    d_y, d_gate = [], []
    for u in range(y_i.shape[0] * seqs):
        j, s = u // seqs, u % seqs
        spread = dot_ones(stacked, stat_rows(u, inner), TN)
        scale, pull = spread[:, :inner], spread[:, inner:]
        gate, full = g_i[j, s], y_i[j, s]
        gate_sig = jax.nn.sigmoid(gate)
        gate_silu = gate * gate_sig
        mixed = full * gate_silu
        out_o[j, s] = (mixed * scale * gain).astype(bf16)
        d_mixed = cot[j, s].astype(f32) * gain * scale - mixed * pull
        d_y.append(d_mixed * gate_silu)
        d_gate.append((d_mixed * full * (gate_sig * (1.0 + gate * (1.0 - gate_sig)))).astype(bf16))
    return beside(d_y), d_gate


def backward_kernel(core, *refs, width, inner, total):
    ins, stats, (par, w_main, w_other) = refs[:8], refs[8:12], refs[12:15]
    far_outs, (out, near, far, term, give), (grad_state, next_state, here_all, sems) = refs[15:20], refs[20:25], refs[25:]
    copies = []

    def send(index, first_row, rows):
        here, there = (out, near, far, term, give)[index], far_outs[index]
        span = pl.ds(first_row, rows)
        copies.append(pltpu.make_async_copy(here.at[span], there.at[span], sems.at[len(copies)]))
        copies[-1].start()

    grad_state[...] = jnp.zeros_like(grad_state)
    next_state[...] = jnp.zeros_like(next_state)
    first = core[0] == 0
    weights = whole_weights(w_main, w_other, first, inner)
    steps = near.shape[0]
    rows = here_all.shape[0] // steps
    for i in reversed(range(steps)):
        views = [a.at[pl.ds(i * (a.shape[0] // steps), a.shape[0] // steps)] for a in ins + (out, near, far)]
        sums = (stats[0][i] + stats[1][i]) + (stats[2][i] + stats[3][i])
        here_all[i * rows : (i + 1) * rows, :] = backward_step(
            first, *views, sums, par, weights, grad_state, next_state, width=width, inner=inner, total=total
        )
        for index in (2, 1, 0):
            size = (out, near, far)[index].shape[0] // steps
            send(index, i * size, size)

    tok = ins[7]
    wide = 2 * inner
    slab = term.shape[0] // slabs
    for q in range(slabs):
        span = slice(q * slab, (q + 1) * slab)
        left = tok[:, :, :, span].reshape(steps * rows, slab)
        part = lax.dot_general(left, here_all[...], TN, preferred_element_type=f32).astype(bf16)
        b_part, c_part = part[:, wide : wide + lanes], part[:, wide + lanes : wide + 2 * lanes]
        give[span, :] = jnp.where(first, c_part, b_part)
        term[span, :] = jnp.concatenate(
            [part[:, :wide], jnp.where(first, b_part, c_part), part[:, wide + 2 * lanes :]], axis=1
        )
        send(4, q * slab, slab)
        send(3, q * slab, slab)
    for copy in copies:
        copy.wait()


def backward_step(
    first_core, xv_i, g_i, bc_i, low_i, y_i, st_i, cot, tok, out_o, near_o, far_o, sums, par, weights,
    grad_state, next_state, *, width, inner, total
):
    per_step, seqs, block, model = tok.shape
    units = [(j, s) for j in range(per_step) for s in range(seqs)]
    count = len(units)
    heads = inner // width
    part = lambda a, u: a[:, u * inner : (u + 1) * inner]
    expander = head_expander(inner, width, count)
    later = iota((block, block), 1) >= iota((block, block), 0)
    upper = (iota((block, block), 1) >= iota((block, block), 0)).astype(f32).astype(bf16)
    skip, rate = beside([par[0:1, :]] * count), par[3:4, :lanes]
    raw, steps, cumul = low_i[0, 0], low_i[0, 1], low_i[0, 2]
    cumul_t = cumul.T
    step_wide, cumul_wide = spread_out(steps, cumul, expander)
    last_wide = cumul_wide[block - 1 : block]
    tail, last_decay = jnp.exp(last_wide - cumul_wide), jnp.exp(last_wide)
    b_two = [halves(bc_i[j, s, :, :lanes]) for j, s in units]
    c_two = [halves(bc_i[j, s, :, lanes:]) for j, s in units]
    scores_t = [dot3(b_two[u], c_two[u], NT) for u in range(count)]
    xv = beside(xv_i[j, s] for j, s in units)
    d_y, d_gate = norm_step(y_i, g_i, cot, sums, par, out_o, total=total)
    sig = jax.nn.sigmoid(xv)
    values = xv * sig
    y = beside(y_i[j, s] for j, s in units) - skip * values
    scaled = values * step_wide
    tailed = scaled * tail
    lifted = halves(d_y * jnp.exp(cumul_wide))
    lifted = [(part(lifted[0], u), part(lifted[1], u)) for u in range(count)]
    updates = [dot3(c_two[u], lifted[u], TN) for u in range(count)]

    back, through, from_state = [None] * count, [None] * count, [None] * count
    for u in reversed(range(count)):
        j, s = units[u]
        grad = grad_state[s]
        grad_two = halves(grad)
        back[u] = dot3(b_two[u], grad_two, NN)
        from_state[u] = dot3(part(tailed, u), grad_two, NT)
        through[u] = jnp.sum(next_state[s] * grad, axis=0, keepdims=True)
        grad_state[s] = part(last_decay, u) * grad + updates[u]
        next_state[s] = st_i[j, s]

    inners, d_scores = [], []
    for u in range(count):
        d_scores_t = jnp.zeros((block, block), f32)
        for pair in range(heads // 2):
            first = u * inner + 2 * pair * width
            cols = slice(first, first + 2 * width)
            products = lax.dot_general(
                pair_halves(scaled[:, cols], block, width).astype(bf16),
                d_y[:, cols].astype(bf16),
                NT,
                preferred_element_type=f32,
            )
            both = []
            for k in range(2):
                h = u * heads + 2 * pair + k
                gap = jnp.where(later, cumul_t[h : h + 1, :] - cumul[:, h : h + 1], -1e30)
                decay = jnp.exp(gap)
                both.append((scores_t[u] * decay).astype(bf16))
                d_scores_t += products[k * block : (k + 1) * block] * decay
            inners.append(
                lax.dot_general(
                    beside(both), pair_halves(d_y[:, cols], block, width).astype(bf16), NN, preferred_element_type=f32
                )
            )
        d_scores.append(halves(d_scores_t))
    d_c = [
        dot3(d_scores[u], b_two[u], TN) + dot3(lifted[u], st_i[j, s], NT) for u, (j, s) in enumerate(units)
    ]
    d_b = [dot3(d_scores[u], c_two[u], NN) + from_state[u] for u in range(count)]
    back = tail * beside(back) + beside(inners)
    last_row = iota((block, count * inner), 0) == block - 1
    products = jnp.concatenate([values * back, d_y * y + jnp.where(last_row, beside(through), 0.0)], axis=0)
    reduced = dot_ones(halves(products), expander, NT)
    d_steps = reduced[:block]
    d_log = ones_dot(upper, halves(reduced[block:] - steps * d_steps))
    d_raw = (d_steps - d_log * rate) * jax.nn.sigmoid(raw)
    d_values = back * step_wide + skip * d_y
    d_xv = (d_values * (sig * (1.0 + xv * (1.0 - sig)))).astype(bf16)
    here = jnp.concatenate(
        [
            beside([part(d_xv, u), d_gate[u], d_b[u].astype(bf16), d_c[u].astype(bf16)]
                   + [unpacked(d_raw, u, heads).astype(bf16)])
            for u, (j, s) in enumerate(units)
        ],
        axis=0,
    )
    partial = lax.dot_general(here, weights, NT, preferred_element_type=f32)
    partial = partial.reshape(per_step, seqs, block, model)
    near_o[0] = jnp.where(first_core, partial[0], partial[1])
    far_o[0] = jnp.where(first_core, partial[1], partial[0]).astype(bf16)
    return here


def join_kernel(place, near, far, term, got, out_0, out_1, out_2, out_3, term_o):
    for k, out in enumerate((out_0, out_1, out_2, out_3)):
        chip = lax.bitwise_xor(place[0], k)
        yl, xl = lax.rem(chip, 2), lax.div(chip, 2)
        out[...] = (near[yl, xl] + far[yl, xl].astype(f32)).astype(bf16)
    term_o[...] = (term[...].astype(f32) + got[...].astype(f32)).astype(bf16)


def total_kernel(shares, xz_o, bcdt_o, *, inner, heads, group):
    step = pl.program_id(0)
    half = group * inner

    @pl.when(step == 0)
    def _():
        bcdt_o[...] = jnp.zeros_like(bcdt_o)

    summed = jnp.sum(shares[0, :, 0].astype(f32), axis=(0, 1))
    at = pl.multiple_of(step * inner, inner)
    xz_o[:, pl.ds(at, inner)] = summed[:, :inner]
    xz_o[:, pl.ds(pl.multiple_of(half + at, inner), inner)] = summed[:, inner : 2 * inner]
    core = lax.rem(lax.div(step, 2), 2)
    bc = summed[:, 2 * inner : 2 * inner + lanes]
    bcdt_o[:, :lanes] += jnp.where(core == 0, bc, 0.0)
    bcdt_o[:, lanes : 2 * lanes] += jnp.where(core == 0, 0.0, bc)
    steps = summed[:, 2 * inner + lanes :]
    lane = iota(steps.shape, 1)
    moved = pltpu.roll(jnp.where(lane < heads, steps, 0.0), step * heads, 1)
    bcdt_o[:, 2 * lanes :] += moved[:, : group * heads]


def cost(micros):
    return pl.CostEstimate(flops=int(micros * 1.1e9), bytes_accessed=int(micros * 3.5e6), transcendentals=0)


def chunk_spec(shape, count=None, per_step=1):
    blank = (0,) * (len(shape) - 1)
    if count is None:
        return pl.BlockSpec((per_step,) + shape[1:], lambda i: (i,) + blank)
    return pl.BlockSpec((per_step,) + shape[1:], lambda i: (count - 1 - i,) + blank)


def fixed_spec(shape):
    return pl.BlockSpec(shape, lambda i: (0,) * len(shape))


chunks_per_step = 2
slabs = 2
smem_spec = pl.BlockSpec(memory_space=pltpu.SMEM)
vmem_spec = pl.BlockSpec(memory_space=pltpu.VMEM)
HBM = pltpu.HBM


def pack_call(tokens, cot, w_xz, w_bcdt, sides, group, heads):
    block, total = cot.shape
    inner = total // group
    states = (w_bcdt.shape[1] - heads * group) // 2
    copies = sides + (w_xz.shape[0], 2 * inner + states + lanes)
    piece = (block, tokens.shape[1] + 2 * inner)

    def kernel(*refs):
        pack_kernel(*refs, inner=inner, heads=heads, states=states)

    return pl.pallas_call(
        kernel,
        in_specs=[vmem_spec] * 4,
        out_specs=[vmem_spec] * 5,
        out_shape=[HBM(piece, bf16)] * 4 + [HBM(copies, bf16)],
        compiler_params=pltpu.CompilerParams(vmem_limit_bytes=wide_vmem),
        cost_estimate=cost(2),
        name="pack_pieces",
    )(tokens, cot, w_xz, w_bcdt)


def forward_call(place, own, far, weights, w_other, par, width):
    _, block, columns = own.shape
    model = weights.shape[0]
    inner = columns - model
    chunks, seqs = 4, 2
    steps = chunks // chunks_per_step
    wide = (chunks, seqs, block, inner)

    outs = [
        ((chunks, seqs, block, model), bf16),
        (wide, bf16),
        (wide, f32),
        (wide, f32),
        ((chunks, seqs, block, 2 * lanes), f32),
        ((steps, 3, block, lanes), f32),
        (wide, f32),
        ((chunks, seqs, lanes, inner), f32),
        ((steps, 8, block), f32),
    ]

    def kernel(*refs):
        forward_kernel(*refs, width=width, inner=inner)

    return pl.pallas_call(
        kernel,
        in_specs=[smem_spec] + [vmem_spec] * 5,
        out_specs=[vmem_spec] * len(outs),
        out_shape=[jax.ShapeDtypeStruct(a, kind) for a, kind in outs],
        scratch_shapes=[pltpu.VMEM((seqs, lanes, inner), f32)],
        compiler_params=pltpu.CompilerParams(vmem_limit_bytes=vmem),
        cost_estimate=cost(12),
        name="forward_scan",
    )(place, own, far, weights, w_other, par)


def backward_call(core, scanned, stats, par, weights, w_other, width, total):
    xv = scanned[0]
    chunks, seqs, block, inner = xv.shape
    model, columns = weights.shape
    columns = columns + lanes
    half = (chunks // chunks_per_step, seqs, block, model)
    outs = [
        (xv.shape, bf16),
        (half, f32),
        (half, bf16),
        ((model, columns - lanes), bf16),
        ((model, lanes), bf16),
    ]

    def kernel(*refs):
        backward_kernel(*refs, width=width, inner=inner, total=total)

    return pl.pallas_call(
        kernel,
        in_specs=[smem_spec] + [vmem_spec] * 15,
        out_specs=[pl.BlockSpec(memory_space=pltpu.HBM)] * 5,
        out_shape=[HBM(shape, kind) for shape, kind in outs],
        scratch_shapes=[pltpu.VMEM(shape, kind) for shape, kind in outs]
        + [
            pltpu.VMEM((seqs, lanes, inner), f32),
            pltpu.VMEM((seqs, lanes, inner), f32),
            pltpu.VMEM((chunks * seqs * block, columns), bf16),
            pltpu.SemaphoreType.DMA((3 * half[0] + 2 * slabs,)),
        ],
        compiler_params=pltpu.CompilerParams(vmem_limit_bytes=vmem),
        cost_estimate=cost(20),
        name="backward_scan",
    )(core, *scanned, *stats, par, weights, w_other)


def join_call(here, near, far, term, got, inner):
    _, _, block, model = near.shape
    fixed = lambda shape: pl.BlockSpec(shape, lambda i: (0,) * len(shape))
    bc_spec = pl.BlockSpec((term.shape[0], lanes), lambda i: (0, 2 * inner // lanes))
    return pl.pallas_call(
        join_kernel,
        grid=(1,),
        in_specs=[smem_spec, fixed(near.shape), fixed(far.shape), bc_spec, fixed(got.shape)],
        out_specs=[fixed((block, model))] * 4 + [bc_spec],
        out_shape=[HBM((block, model), bf16)] * 4 + [HBM(term.shape, bf16)],
        input_output_aliases={3: 4},
        compiler_params=pltpu.CompilerParams(vmem_limit_bytes=wide_vmem),
        cost_estimate=cost(3),
        name="join_halves",
    )(here, near, far, term, got)


def total_call(shares, inner, heads):
    times, far, seqs, near, rows, columns = shares.shape
    group = times * seqs
    shapes = [(rows, 2 * group * inner), (rows, 2 * lanes + group * heads)]

    def kernel(*refs):
        total_kernel(*refs, inner=inner, heads=heads, group=group)

    return pl.pallas_call(
        kernel,
        grid=(group,),
        in_specs=[pl.BlockSpec((1, far, 1, near, rows, columns), lambda i: (i // seqs, 0, i % seqs, 0, 0, 0))],
        out_specs=[fixed_spec(a) for a in shapes],
        out_shape=[jax.ShapeDtypeStruct(a, f32) for a in shapes],
        compiler_params=pltpu.CompilerParams(vmem_limit_bytes=vmem),
        cost_estimate=cost(2),
        name="total_shares",
    )(shares)


def partner(a):
    return lax.ppermute(a, "core", [(0, 1), (1, 0)])


def around(give):
    came = {0: give(0)}
    spot = lambda chip: (chip % 2) * 2 + chip // 2
    for k in (3, 1, 2):
        came[k] = lax.ppermute(give(k), ("yl", "xl"), [(spot(chip), spot(chip ^ k)) for chip in range(4)])
    return [came[k] for k in range(4)]


def stack_kernel(place, a, b, c, d, _, own_o, give_o):
    inner = own_o.shape[2] // 5
    model = 4 * inner
    for k, came in enumerate((a, b, c, d)):
        tokens = came[:, :model]
        one, two = came[:, model : model + inner], came[:, model + inner :]
        first = place[1] == 0
        own_o[k] = jnp.concatenate([tokens, jnp.where(first, one, two)], axis=1)
        give_o[k] = jnp.concatenate([tokens, jnp.where(first, two, one)], axis=1)


def stack_call(place, came, early):
    block, columns = came[0].shape
    stacked = (4, block, columns // 6 * 5)
    return pl.pallas_call(
        stack_kernel,
        in_specs=[pl.BlockSpec(memory_space=pltpu.SMEM)] + [vmem_spec] * 4 + [pl.BlockSpec(memory_space=pl.ANY)],
        out_specs=[vmem_spec] * 2,
        out_shape=[HBM(stacked, bf16), HBM(stacked, bf16)],
        compiler_params=pltpu.CompilerParams(vmem_limit_bytes=wide_vmem),
        cost_estimate=cost(stack_cost),
        name="stack_pieces",
    )(place, *came, early)


def sum_kernel(a, b, c, d, heads, out, layer_o):
    out[...] = ((a[...].astype(f32) + b[...].astype(f32)) + (c[...].astype(f32) + d[...].astype(f32))).astype(bf16)
    inner = heads.shape[2]
    for k in range(heads.shape[0]):
        layer_o[:, k * inner : (k + 1) * inner] = heads[k]


def sum_call(arrays, heads):
    group, block, inner = heads.shape
    return pl.pallas_call(
        sum_kernel,
        out_shape=[
            jax.ShapeDtypeStruct(arrays[0].shape, bf16),
            jax.ShapeDtypeStruct((block, group * inner), bf16),
        ],
        compiler_params=pltpu.CompilerParams(vmem_limit_bytes=wide_vmem),
        cost_estimate=cost(sum_cost),
        name="sum_pieces",
    )(*arrays, heads)


def body(tokens, cotangent, w_xz, w_bcdt, rate, dt_bias, skip, gain):
    group = lax.axis_size(group_axes)
    devices = lax.axis_size(whole)
    mine = lax.axis_index(group_axes)
    chunks = lax.axis_size("yl") * lax.axis_size("core")
    seqs = group // chunks
    owners = lax.axis_size(rows_axes)
    block, model = tokens.shape[1:]
    total = cotangent.shape[2]
    inner = total // group
    heads = rate.shape[0] // group
    width = inner // heads
    states = (w_bcdt.shape[1] - rate.shape[0]) // 2

    core = lax.axis_index("core")
    here = lax.axis_index(("xl", "yl"))
    place = jnp.stack([here, core]).astype(jnp.int32)
    sides = tuple(lax.axis_size(name) for name in rows_axes)
    *pieces, copies = pack_call(tokens[0], cotangent[0], w_xz, w_bcdt, sides, group, heads)
    copies = copies.reshape((owners,) + copies.shape[4:])

    own = lambda a: lax.dynamic_slice_in_dim(a, mine * heads, heads, 0)
    padded = lambda a: jnp.pad(jnp.tile(own(a), lanes // heads), (0, inner - lanes))
    par = jnp.stack(
        [jnp.repeat(own(skip), width), lax.dynamic_slice_in_dim(gain, mine * inner, inner, 0)]
        + [padded(dt_bias), padded(rate)]
        + [jnp.zeros((inner,), f32)] * 4
    )
    own_came, give_came = stack_call(place, around(lambda shift: pieces[shift]), par)
    far_came = partner(give_came)

    rest = owners // sides[0]
    traders = [
        [(((start + k) % 2) * sides[0] + k) * rest + i for k in range(sides[0]) for i in range(rest)]
        for start in range(2)
    ]
    weights = lax.all_to_all(copies, ("yl",) + rows_axes, 0, 0, axis_index_groups=traders, tiled=True)
    weights = weights.reshape(model, -1)
    w_other = partner(weights[:, 2 * inner : 2 * inner + lanes])

    tok, cot, xv, gate, bc, low, y, chunk_states, stats = forward_call(
        place, own_came, far_came, weights, w_other, par, width
    )
    stats = stats + partner(stats)
    stats = around(lambda shift: stats)
    scalar = lambda a: jnp.full((1,), a, jnp.int32)
    scanned = (xv, gate, bc, low, y, chunk_states, cot, tok)
    out, near, far, term, give = backward_call(
        scalar(core), scanned, stats, par, weights, w_other, width, float(total)
    )
    layer_out = lax.all_to_all(out.reshape(group, block, inner), group_axes, 0, 0, tiled=True)
    *sums, term = join_call(scalar(here), near, partner(far), term, partner(give), inner)
    shares = lax.all_to_all(term.reshape(devices, model // devices, -1), whole, 0, 0, tiled=True)
    came = around(lambda shift: sums[shift])
    grad_input, layer_out = sum_call(came, layer_out)
    grad_xz, grad_bcdt = total_call(
        shares.reshape(chunks, -1, seqs, lax.axis_size("z"), model // devices, shares.shape[-1]), inner, heads
    )
    return (layer_out[None], grad_input[None], grad_xz, grad_bcdt)


def solution(mesh):
    split = Mesh(mesh.devices.reshape(2, 2, 2, 2, 2, 4), whole)
    ctx, fsdp = ("yl", "core"), rows_axes
    placed = (P(fsdp, ctx, None), P(fsdp, ctx, None), P(fsdp, None), P(fsdp, None), P(), P(), P(), P())
    return jax.shard_map(
        body,
        mesh=split,
        in_specs=placed,
        out_specs=(P(fsdp, ctx, None), P(fsdp, ctx, None), P(ctx + fsdp, None), P(ctx + fsdp)),
        check_vma=False,
    )
```
